32 devices in a mesh: batch: 8 (over z, x), seq: 4 (over y, core).
Axes of the slice: x: 2, y: 2, z: 4, core: 2. Of those that a mesh axis runs over, the one named last changes fastest.
Arguments:
- inputs: bfloat16 [16, 1024, 1024], P('batch', 'seq'), may hold values from -6 to 6
- ends: int32 [16], P('batch'), may hold values from 256 to 1024, as said below
- ln_gain: bfloat16 [1024], P(('batch', 'seq')), may hold values from 0.5 to 1.5
- ln_bias: bfloat16 [1024], P(('batch', 'seq')), may hold values from -1.5 to 1.5
- w_qkv: bfloat16 [1024, 3072], P(('batch', 'seq')), may hold values from -0.1875 to 0.1875
- w_attn: bfloat16 [1024, 1024], P(('batch', 'seq')), may hold values from -2 to 2
- w_in: bfloat16 [1024, 4096], P(('batch', 'seq')), may hold values from -0.1875 to 0.1875
- b_in: bfloat16 [4096], P(('batch', 'seq')), may hold values from -2.5 to 2.5
- w_out: bfloat16 [4096, 1024], P(('batch', 'seq')), may hold values from -0.09375 to 0.09375
- b_out: bfloat16 [1024], P(('batch', 'seq')), may hold values from -2.5 to 2.5
- cotangent: bfloat16 [16, 1024, 1024], P('batch', 'seq'), may hold values from -6 to 6
Outputs:
- output: bfloat16 [16, 1024, 1024], P('batch', 'seq')
- grad_inputs: float32 [16, 1024, 1024], P('batch', 'seq')
- grad_ln_gain: float32 [1024], P(('batch', 'seq'))
- grad_ln_bias: float32 [1024], P(('batch', 'seq'))
- grad_w_qkv: float32 [1024, 3072], P(('batch', 'seq'))
- grad_w_attn: float32 [1024, 1024], P(('batch', 'seq'))
- grad_w_in: float32 [1024, 4096], P(('batch', 'seq'))
- grad_b_in: float32 [4096], P(('batch', 'seq'))
- grad_w_out: float32 [4096, 1024], P(('batch', 'seq'))
- grad_b_out: float32 [1024], P(('batch', 'seq'))
The draws below stay inside these ranges and needn't reach their ends.
Inputs may be any that keep to these rules, and one draw needn't show every extreme that they name: A window holds the end of one protein at position ends - 1 when ends < 1024; the next protein starts there. In each aligned block of 2 windows, one drawn from the seed has ends = 1024 and the next one in the block, cyclically, has ends = 256.
All inputs are finite; a program needn't handle non-finite values.
Results may differ from the reference program's by a relative error of at most 0.0086.
Values may be sent and summed in bfloat16 or wider, within the bound.
A program may use at most 256 MiB of HBM per device.

```python
import math
import jax
import jax.numpy as jnp
from jax import lax

D = 1024
FF = 4096
HEADS = 16
HD = 64
ROTARY = 32
SEQ_LEN = 1024
WPB = 2
WINDOWS = 16


def draw_ends(key, part):
    key = jax.random.fold_in(key, 11)
    key_bounds, key_choice = jax.random.split(key)
    groups = WINDOWS // WPB
    boundary = jax.random.randint(key_bounds, (groups, WPB), SEQ_LEN // 4, SEQ_LEN + 1)
    chosen = jax.random.randint(key_choice, (groups, 1), 0, WPB)
    within = jnp.arange(WPB, dtype=jnp.int32)[None, :]
    boundary = jnp.where(within == chosen, SEQ_LEN, boundary)
    boundary = jnp.where(within == (chosen + 1) % WPB, SEQ_LEN // 4, boundary)
    return boundary.reshape(WINDOWS).astype(jnp.int32)


def level_of(key, extent, cuts, smallest, largest):
    gain, own = 1.0, jax.random.fold_in(key, 6)
    for axis_at, parts in cuts:
        draws = jnp.exp(jax.random.uniform(jax.random.fold_in(own, axis_at), (parts,), jnp.float32, smallest / len(cuts), largest / len(cuts)))
        gain = gain * jnp.repeat(draws, extent[axis_at] // parts).reshape([-1 if axis == axis_at else 1 for axis in range(len(extent))])
    return gain


def normal_values(stream_key, dims, width, reach, pieces=(), held_as=jnp.bfloat16):
    loudness = level_of(stream_key, dims, pieces, -0.22, 0.18) if pieces else 1.0
    values = jax.random.normal(stream_key, dims, jnp.float32) * width * loudness
    return jnp.minimum(jnp.maximum(values, -reach), reach).astype(held_as)


def setup_inputs(seed: int = 0) -> dict:
    seeds = jax.random.split(jax.random.key(seed), 12)
    return {
        "inputs": normal_values(seeds[0], (WINDOWS, SEQ_LEN, D), 1.0, 6.0, ((0, 8), (1, 4))),
        "ends": draw_ends(jax.random.fold_in(seeds[11], 71), 0),
        "ln_gain": jnp.clip(1.0 + 0.1 * jax.random.normal(seeds[2], (D,), jnp.float32), 0.5, 1.5).astype(jnp.bfloat16),
        "ln_bias": normal_values(seeds[3], (D,), 0.3, 1.5, ((0, 32),)),
        "w_qkv": normal_values(seeds[4], (D, 3 * D), D ** -0.5, 0.1875, ((0, 32),)),
        "w_attn": normal_values(seeds[5], (D, D), (D * 8 // SEQ_LEN) ** -0.5, 2.0, ((0, 32),)),
        "w_in": normal_values(seeds[6], (D, FF), D ** -0.5, 0.1875, ((0, 32),)),
        "b_in": normal_values(seeds[7], (FF,), 0.5, 2.5, ((0, 32),)),
        "w_out": normal_values(seeds[8], (FF, D), FF ** -0.5, 0.09375, ((0, 32),)),
        "b_out": normal_values(seeds[9], (D,), 0.5, 2.5, ((0, 32),)),
        "cotangent": normal_values(seeds[10], (WINDOWS, SEQ_LEN, D), 1.0, 6.0, ((0, 8), (1, 4))),
    }


@jax.custom_vjp
def low(v):
    return lax.optimization_barrier(v.astype(jnp.bfloat16)).astype(jnp.float32)

@jax.custom_vjp
def low_back(v):
    return v

def low_keep(v):
    return (low(v), None)

def low_pass(kept, grad):
    return (grad,)

def back_keep(v):
    return (v, None)

def back_low(kept, grad):
    return (low(grad),)
low.defvjp(low_keep, low_pass)
low_back.defvjp(back_keep, back_low)
norm_eps = 1e-05
gelu_factor = 0.7978845608028654
masked_score = -1e+30

def gelu_tanh(values):
    return 0.5 * values * (1.0 + jnp.tanh(gelu_factor * (values + 0.044715 * values * values * values)))

def layer_norm(row_values, norm_gain, norm_shift):
    average = lax.optimization_barrier(jnp.mean(row_values, axis=-1, keepdims=True))
    centered = row_values - average
    variance = lax.optimization_barrier(jnp.mean(centered * centered, axis=-1, keepdims=True))
    return centered * lax.rsqrt(variance + norm_eps) * norm_gain + norm_shift

def rotary_tables(positions):
    pair_index = jnp.arange(ROTARY // 2, dtype=jnp.float32)
    inverse = 10000.0 ** (-2.0 * pair_index / ROTARY)
    angles = positions[:, None] * inverse[None, :]
    return (jnp.cos(angles), jnp.sin(angles))

def rotate(vectors, cosine, sine_table):
    rotated = vectors[..., :ROTARY]
    even_part = rotated[..., 0::2]
    odd_part = rotated[..., 1::2]
    cosine_wide = cosine[:, None, :]
    sine_wide = sine_table[:, None, :]
    new_even = even_part * cosine_wide - odd_part * sine_wide
    new_odd = odd_part * cosine_wide + even_part * sine_wide
    merged = jnp.stack([new_even, new_odd], axis=-1).reshape(rotated.shape)
    return jnp.concatenate([merged, vectors[..., ROTARY:]], axis=-1)

def visible(query_places, key_places, ending):
    query_after = query_places[:, None] >= ending
    key_after = key_places[None, :] >= ending
    return (key_places[None, :] <= query_places[:, None]) & (query_after == key_after)

def attend(bundle):
    queries, key_vectors, values, ending = bundle
    places = jnp.arange(SEQ_LEN, dtype=jnp.int32)
    scores = jnp.einsum('qhd,khd->hqk', queries, key_vectors, precision=lax.Precision.HIGHEST) * (1.0 / math.sqrt(HD))
    scores = low_back(scores)
    scores = jnp.where(visible(places, places, ending)[None], scores, masked_score)
    row_peak = lax.optimization_barrier(jnp.max(scores, axis=-1, keepdims=True))
    weights = jnp.exp(scores - row_peak)
    probabilities = weights / lax.optimization_barrier(jnp.sum(weights, axis=-1, keepdims=True))
    return jnp.einsum('hqk,khd->qhd', low(probabilities), values, precision=lax.Precision.HIGHEST)

def forward(inputs, ending, ln_gain, ln_bias, w_qkv, w_attn, w_in, b_in, w_out, b_out):
    highest = lax.Precision.HIGHEST
    windows = inputs.shape[0]
    normed = low(layer_norm(inputs, ln_gain, ln_bias))
    projected = low_back(jnp.einsum('wld,de->wle', normed, w_qkv, precision=highest))
    arranged = projected.reshape(windows, SEQ_LEN, HEADS, 3, HD)
    cosine, sine_table = rotary_tables(jnp.arange(SEQ_LEN, dtype=jnp.float32))
    queries = low(rotate(arranged[:, :, :, 0], cosine, sine_table))
    key_vectors = low(rotate(arranged[:, :, :, 1], cosine, sine_table))
    values = low(arranged[:, :, :, 2])
    heads_out = lax.map(jax.checkpoint(attend), (queries, key_vectors, values, ending))
    attended = low(low_back(heads_out)).reshape(windows, SEQ_LEN, D)
    branch_attn = jnp.einsum('wle,ed->wld', attended, w_attn, precision=highest)
    hidden = low_back(jnp.einsum('wld,di->wli', normed, w_in, precision=highest) + b_in)
    activated = low(gelu_tanh(hidden))
    branch_mlp = jnp.einsum('wli,id->wld', activated, w_out, precision=highest) + b_out
    return inputs + branch_attn + branch_mlp

def reference(inputs, ends, ln_gain, ln_bias, w_qkv, w_attn, w_in, b_in, w_out, b_out, cotangent):
    params = tuple((argument.astype(jnp.float32) for argument in (ln_gain, ln_bias, w_qkv, w_attn, w_in, b_in, w_out, b_out)))
    group_size = 4 if WINDOWS % 4 == 0 else 1
    groups = WINDOWS // group_size
    grouped_in = inputs.astype(jnp.float32).reshape(groups, group_size, SEQ_LEN, D)
    grouped_ends = ends.astype(jnp.int32).reshape(groups, group_size)
    grouped_cot = cotangent.astype(jnp.float32).reshape(groups, group_size, SEQ_LEN, D)

    def one_group(totals, bundle):
        block_in, block_ends, block_cot = bundle

        def apply(x_in, gain_f, shift_f, qkv_f, attn_f, in_f, bias_in_f, out_f, bias_out_f):
            return forward(x_in, block_ends, gain_f, shift_f, qkv_f, attn_f, in_f, bias_in_f, out_f, bias_out_f)
        result, pullback = jax.vjp(apply, block_in, params[0], params[1], params[2], params[3], params[4], params[5], params[6], params[7])
        gradients = pullback(block_cot)
        totals = tuple((running + extra for running, extra in zip(totals, gradients[1:])))
        return (totals, (result.astype(jnp.bfloat16), gradients[0]))
    zero_sums = tuple((jnp.zeros_like(argument) for argument in params))
    totals, (results, input_grads) = lax.scan(one_group, zero_sums, (grouped_in, grouped_ends, grouped_cot))
    output = results.reshape(WINDOWS, SEQ_LEN, D)
    grad_inputs = input_grads.reshape(WINDOWS, SEQ_LEN, D)
    return (output, grad_inputs, totals[0], totals[1], totals[2], totals[3], totals[4], totals[5], totals[6], totals[7])
```

```python
import math

import jax
import jax.numpy as jnp
import numpy as np
from jax import lax
from jax.experimental import pallas as pl
from jax.experimental.pallas import tpu as pltpu
from jax.sharding import PartitionSpec as P

HEADS = 16
HD = 64
ROTARY = 32
MICRO = 2


norm_eps = 1e-05
gelu_factor = 0.7978845608028654
masked_score = -1e30


def gelu_tanh(values):
    return (
        0.5
        * values
        * (1.0 + jnp.tanh(gelu_factor * (values + 0.044715 * values * values * values)))
    )


def layer_norm(row_values, norm_gain, norm_shift):
    average = jnp.mean(row_values, axis=-1, keepdims=True)
    centered = row_values - average
    variance = jnp.mean(centered * centered, axis=-1, keepdims=True)
    return centered * lax.rsqrt(variance + norm_eps) * norm_gain + norm_shift


def rotary_tables(positions):
    pair_index = jnp.arange(ROTARY // 2, dtype=jnp.float32)
    inverse = 10000.0 ** (-2.0 * pair_index / ROTARY)
    angles = positions[:, None] * inverse[None, :]
    return (jnp.cos(angles), jnp.sin(angles))


def rotate(vectors, cosine, sine_table):
    rotated = vectors[..., :ROTARY]
    even_part = rotated[..., 0::2]
    odd_part = rotated[..., 1::2]
    cosine_wide = cosine[:, None, :]
    sine_wide = sine_table[:, None, :]
    new_even = even_part * cosine_wide - odd_part * sine_wide
    new_odd = odd_part * cosine_wide + even_part * sine_wide
    merged = jnp.stack([new_even, new_odd], axis=-1).reshape(rotated.shape)
    return jnp.concatenate([merged, vectors[..., ROTARY:]], axis=-1)


def visible(query_places, key_places, ending):
    query_after = query_places[:, None] >= ending
    key_after = key_places[None, :] >= ending
    return (key_places[None, :] <= query_places[:, None]) & (query_after == key_after)


def block_scores(block_queries, key_vectors, query_places, key_places, ending, score_scale):
    scores = (
        jnp.einsum("qhd,khd->hqk", block_queries, key_vectors, preferred_element_type=jnp.float32)
        * score_scale
    )
    return jnp.where(visible(query_places, key_places, ending)[None], scores, masked_score)


def attend_forward(packed, ending):
    seq_len, head_count, triple = packed.shape
    head_size = triple // 3
    block_rows = min(512, seq_len)
    score_scale = 1.0 / math.sqrt(head_size)
    queries = packed[:, :, :head_size]
    key_vectors = packed[:, :, head_size : 2 * head_size]
    values = packed[:, :, 2 * head_size :]
    key_places = jnp.arange(seq_len, dtype=jnp.int32)

    def one_block(block_index):
        first_row = block_index * block_rows
        block_queries = lax.dynamic_slice_in_dim(queries, first_row, block_rows, 0)
        query_places = first_row + jnp.arange(block_rows, dtype=jnp.int32)
        scores = block_scores(
            block_queries, key_vectors, query_places, key_places, ending, score_scale
        )
        row_peak = jnp.max(scores, axis=-1, keepdims=True)
        weights = jnp.exp(scores - row_peak)
        row_total = jnp.sum(weights, axis=-1, keepdims=True)
        probabilities = (weights / row_total).astype(jnp.bfloat16)
        result = jnp.einsum(
            "hqk,khd->qhd", probabilities, values, preferred_element_type=jnp.float32
        )
        return (result.astype(jnp.bfloat16), row_peak, row_total)

    results, peaks, totals = lax.map(one_block, jnp.arange(seq_len // block_rows, dtype=jnp.int32))
    return (results.reshape(seq_len, head_count, head_size), peaks, totals)


def attend_backward(packed, d_attended, peaks, totals, ending, full_cosine, full_sine):
    seq_len, head_count, triple = packed.shape
    head_size = triple // 3
    block_rows = min(512, seq_len)
    score_scale = 1.0 / math.sqrt(head_size)
    queries = packed[:, :, :head_size]
    key_vectors = packed[:, :, head_size : 2 * head_size]
    values = packed[:, :, 2 * head_size :]
    key_places = jnp.arange(seq_len, dtype=jnp.int32)

    def one_block(running, block_inputs):
        key_grads, value_grads = running
        block_index, row_peak, row_total = block_inputs
        first_row = block_index * block_rows
        block_queries = lax.dynamic_slice_in_dim(queries, first_row, block_rows, 0)
        block_grads = lax.dynamic_slice_in_dim(d_attended, first_row, block_rows, 0)
        query_places = first_row + jnp.arange(block_rows, dtype=jnp.int32)
        scores = block_scores(
            block_queries, key_vectors, query_places, key_places, ending, score_scale
        )
        probabilities = jnp.exp(scores - row_peak) / row_total
        rounded_probs = probabilities.astype(jnp.bfloat16)
        d_probs = jnp.einsum(
            "qhd,khd->hqk", block_grads, values, preferred_element_type=jnp.float32
        )
        row_dot = jnp.sum(probabilities * d_probs, axis=-1, keepdims=True)
        d_scores = (probabilities * (d_probs - row_dot)).astype(jnp.bfloat16)
        query_grads = (
            jnp.einsum("hqk,khd->qhd", d_scores, key_vectors, preferred_element_type=jnp.float32)
            * score_scale
        )
        key_grads = (
            key_grads
            + jnp.einsum(
                "hqk,qhd->khd", d_scores, block_queries, preferred_element_type=jnp.float32
            )
            * score_scale
        )
        value_grads = value_grads + jnp.einsum(
            "hqk,qhd->khd", rounded_probs, block_grads, preferred_element_type=jnp.float32
        )
        return ((key_grads, value_grads), query_grads)

    zero_sums = jnp.zeros((seq_len, head_count, head_size), jnp.float32)
    block_ids = jnp.arange(seq_len // block_rows, dtype=jnp.int32)
    (key_grads, value_grads), query_grads = lax.scan(
        one_block, (zero_sums, zero_sums), (block_ids, peaks, totals)
    )
    query_grads = query_grads.reshape(seq_len, head_count, head_size)
    flipped_sine = -full_sine
    combined = jnp.stack(
        [
            rotate(query_grads, full_cosine, flipped_sine),
            rotate(key_grads, full_cosine, flipped_sine),
            value_grads,
        ],
        axis=2,
    )
    return combined.astype(jnp.bfloat16).reshape(seq_len, head_count, triple)


def collect(ln_gain, ln_bias, w_qkv, w_attn, w_in, b_in, w_out, b_out):
    return (
        lax.all_gather(ln_gain, ("batch", "seq"), axis=0, tiled=True),
        lax.all_gather(ln_bias, ("batch", "seq"), axis=0, tiled=True),
        lax.all_gather(w_qkv, ("batch", "seq"), axis=0, tiled=True),
        lax.all_gather(w_attn, ("batch", "seq"), axis=0, tiled=True),
        lax.all_gather(w_in, ("batch", "seq"), axis=0, tiled=True),
        lax.all_gather(b_in, ("batch", "seq"), axis=0, tiled=True),
        lax.all_gather(w_out, ("batch", "seq"), axis=0, tiled=True),
        lax.all_gather(b_out, ("batch", "seq"), axis=0, tiled=True),
    )


def reduce_grads(gradients):
    return (
        lax.psum_scatter(gradients[0], ("batch", "seq"), scatter_dimension=0, tiled=True),
        lax.psum_scatter(gradients[1], ("batch", "seq"), scatter_dimension=0, tiled=True),
        lax.psum_scatter(gradients[2], ("batch", "seq"), scatter_dimension=0, tiled=True),
        lax.psum_scatter(gradients[3], ("batch", "seq"), scatter_dimension=0, tiled=True),
        lax.psum_scatter(gradients[4], ("batch", "seq"), scatter_dimension=0, tiled=True),
        lax.psum_scatter(gradients[5], ("batch", "seq"), scatter_dimension=0, tiled=True),
        lax.psum_scatter(gradients[6], ("batch", "seq"), scatter_dimension=0, tiled=True),
        lax.psum_scatter(gradients[7], ("batch", "seq"), scatter_dimension=0, tiled=True),
    )


def shards(inputs, ends, ln_gain, ln_bias, w_qkv, w_attn, w_in, b_in, w_out, b_out, cotangent):
    seq_devices = lax.axis_size("seq")
    windows, local_len, model_width = inputs.shape
    seq_len = local_len * seq_devices
    per_micro = windows // MICRO
    offset = lax.axis_index("seq") * local_len
    cosine, sine_table = rotary_tables(
        (offset + jnp.arange(local_len, dtype=jnp.int32)).astype(jnp.float32)
    )
    full_cosine, full_sine = rotary_tables(jnp.arange(seq_len, dtype=jnp.float32))
    outputs = []
    input_grads = []
    shard_sums = None
    for micro_index in range(MICRO):
        gathered = collect(ln_gain, ln_bias, w_qkv, w_attn, w_in, b_in, w_out, b_out)
        (
            gain_full,
            shift_full,
            qkv_full,
            attn_full,
            in_full,
            bias_in_full,
            out_full,
            bias_out_full,
        ) = gathered
        lower = micro_index * per_micro
        row_values = inputs[lower : lower + per_micro].astype(jnp.float32)
        grad_rows = cotangent[lower : lower + per_micro]
        window_ends = ends[lower : lower + per_micro]
        normed_f, norm_pull = jax.vjp(
            layer_norm, row_values, gain_full.astype(jnp.float32), shift_full.astype(jnp.float32)
        )
        normed = normed_f.astype(jnp.bfloat16)
        projected = jnp.einsum("pld,de->ple", normed, qkv_full, preferred_element_type=jnp.float32)
        arranged = projected.reshape(per_micro, local_len, HEADS, 3, HD)
        query_rot = rotate(arranged[:, :, :, 0], cosine, sine_table)
        key_rot = rotate(arranged[:, :, :, 1], cosine, sine_table)
        packed = jnp.stack([query_rot, key_rot, arranged[:, :, :, 2]], axis=3).astype(jnp.bfloat16)
        packed = packed.reshape(per_micro, local_len, HEADS, 3 * HD)
        head_view = lax.all_to_all(packed, "seq", split_axis=2, concat_axis=1, tiled=True)
        attended, peaks, totals = lax.map(
            lambda bundle: attend_forward(bundle[0], bundle[1]), (head_view, window_ends)
        )
        position_view = lax.all_to_all(
            attended, "seq", split_axis=1, concat_axis=2, tiled=True
        ).reshape(per_micro, local_len, model_width)
        branch_attn = jnp.einsum(
            "ple,ed->pld", position_view, attn_full, preferred_element_type=jnp.float32
        )
        hidden = jnp.einsum(
            "pld,di->pli", normed, in_full, preferred_element_type=jnp.float32
        ) + bias_in_full.astype(jnp.float32)
        activ_f, gelu_pull = jax.vjp(gelu_tanh, hidden)
        activated = activ_f.astype(jnp.bfloat16)
        branch_mlp = jnp.einsum(
            "pli,id->pld", activated, out_full, preferred_element_type=jnp.float32
        ) + bias_out_full.astype(jnp.float32)
        outputs.append((row_values + branch_attn + branch_mlp).astype(jnp.bfloat16))
        grad_b_out = jnp.sum(grad_rows.astype(jnp.float32), axis=(0, 1))
        grad_w_out = jnp.einsum(
            "pli,pld->id", activated, grad_rows, preferred_element_type=jnp.float32
        )
        d_activated = jnp.einsum(
            "pld,id->pli", grad_rows, out_full, preferred_element_type=jnp.float32
        )
        d_hidden = gelu_pull(d_activated)[0].astype(jnp.bfloat16)
        grad_b_in = jnp.sum(d_hidden.astype(jnp.float32), axis=(0, 1))
        grad_w_in = jnp.einsum("pld,pli->di", normed, d_hidden, preferred_element_type=jnp.float32)
        grad_w_attn = jnp.einsum(
            "ple,pld->ed", position_view, grad_rows, preferred_element_type=jnp.float32
        )
        d_attended = jnp.einsum(
            "pld,ed->ple", grad_rows, attn_full, preferred_element_type=jnp.float32
        ).astype(jnp.bfloat16)
        d_attended = d_attended.reshape(per_micro, local_len, HEADS, HD)
        d_head_view = lax.all_to_all(d_attended, "seq", split_axis=2, concat_axis=1, tiled=True)
        d_packed = lax.map(
            lambda bundle: attend_backward(
                bundle[0], bundle[1], bundle[2], bundle[3], bundle[4], full_cosine, full_sine
            ),
            (head_view, d_head_view, peaks, totals, window_ends),
        )
        d_projected = lax.all_to_all(
            d_packed, "seq", split_axis=1, concat_axis=2, tiled=True
        ).reshape(per_micro, local_len, 3 * model_width)
        grad_w_qkv = jnp.einsum(
            "pld,ple->de", normed, d_projected, preferred_element_type=jnp.float32
        )
        d_normed = jnp.einsum("pli,di->pld", d_hidden, in_full, preferred_element_type=jnp.float32)
        d_normed = d_normed + jnp.einsum(
            "ple,de->pld", d_projected, qkv_full, preferred_element_type=jnp.float32
        )
        d_rows, grad_gain, grad_shift = norm_pull(d_normed)
        input_grads.append(grad_rows.astype(jnp.float32) + d_rows)
        local_grads = (
            grad_gain,
            grad_shift,
            grad_w_qkv,
            grad_w_attn,
            grad_w_in,
            grad_b_in,
            grad_w_out,
            grad_b_out,
        )
        reduced = reduce_grads(local_grads)
        if shard_sums is None:
            shard_sums = reduced
        else:
            shard_sums = tuple((running + extra for running, extra in zip(shard_sums, reduced)))
    output = jnp.concatenate(outputs, axis=0)
    grad_inputs = jnp.concatenate(input_grads, axis=0)
    return (
        output,
        grad_inputs,
        shard_sums[0],
        shard_sums[1],
        shard_sums[2],
        shard_sums[3],
        shard_sums[4],
        shard_sums[5],
        shard_sums[6],
        shard_sums[7],
    )


HB, SB = 4, 4
NEG = -1e30
BF, F32 = jnp.bfloat16, jnp.float32
MESH = pl.DeviceIdType.MESH


def dot(a, b, ca, cb):
    return lax.dot_general(a, b, (((ca,), (cb,)), ((), ())), preferred_element_type=F32)


def rows(start, size):
    return pl.ds(pl.multiple_of(start, size), size)


def lanes(start, size=128):
    return pl.ds(pl.multiple_of(start, size), size)


def halves(low_source, high_source):
    def piece(source, upper):
        array, first = source
        tile = array[:, first // 128 * 128 : first // 128 * 128 + 128]
        return pltpu.roll(tile, 64, 1) if (first % 128 == 64) != upper else tile

    lane = lax.broadcasted_iota(jnp.int32, (1, 128), 1)
    return jnp.where(lane < 64, piece(low_source, False), piece(high_source, True))


def head_of(owner, j):
    return 4 * j + 2 * (owner % 2) + owner // 2


class Link:
    def __init__(self, send_sems, recv_sems):
        self.send_sems, self.recv_sems = send_sems, recv_sems
        self.first = {}
        self.used = 0

    def index(self, name, at, count):
        if name not in self.first:
            self.first[name] = self.used
            self.used += count
        return self.first[name] + at

    def copy(self, name, at, count, src, dst, device):
        i = self.index(name, at, count)
        return pltpu.make_async_remote_copy(
            src_ref=src,
            dst_ref=dst,
            send_sem=self.send_sems.at[i],
            recv_sem=self.recv_sems.at[i],
            device_id=device,
            device_id_type=MESH,
        )


def gelu_pair(v):
    cube = v * v
    t = jnp.tanh(gelu_factor * (v + 0.044715 * (v * cube)))
    half = 0.5 * (1.0 + t)
    slope = half + 0.5 * v * (1.0 - t * t) * (gelu_factor * (1.0 + (3 * 0.044715) * cube))
    return v * half, slope


def fused_layer(
    ends, prm, wq, wa, wi, wo, cosine, sine, x_in, g_in,
    out, grad_in, grad_q, grad_a, grad_i, grad_o, grad_small, grad_bin,
    X, N, G, A, H, Wi, Wo, Wq, WaAll, Wa, PWI, PWQ, PRM, PR, QKV, att, dO,
    GO, XO, ZO, GI, XI, ZI, GQ, XQ, ZQ, GA, XA, ZA, GAS, GT, XT, ZT,
    YR, SWI, RWI, SWQ, RWQ, TAIL,
    khat, ktT, vtT, doT, oT, dqT, dkA, dvA,
    send_sems, recv_sems, local_sems,
):
    b = lax.axis_index("batch")
    s = lax.axis_index("seq")
    z, xx = b // 2, b % 2
    y, c = s // 2, s % 2
    oc, ox, oy = 1 - c, 1 - xx, 1 - y
    SL = 256
    S = 1024
    core = (b, 2 * y + oc)
    ypart = (b, 2 * oy + c)
    diag = (b, 2 * oy + oc)
    xpart = (2 * z + ox, s)

    def zdev(k):
        return (2 * ((z + k) % 4) + xx, s)

    def zfrom(k):
        return (z + 4 - k) % 4

    link = Link(send_sems, recv_sems)
    pending = []

    def start(make):
        make().start()
        pending.append(make)

    own = rows(SL * s, SL)
    locals_ = []
    for w in range(2):
        locals_.append(pltpu.make_async_copy(x_in.at[w], X.at[w, own], local_sems.at[3 * w]))
        locals_.append(pltpu.make_async_copy(g_in.at[w], G.at[w, own], local_sems.at[3 * w + 1]))
    for cp in locals_:
        cp.start()

    for r in range(SB):
        for blk in range(8):
            PWI[r, :, 128 * blk : 128 * blk + 128] = wi[:, 512 * blk + 128 * r : 512 * blk + 128 * r + 128]
    wq_f = wq[...].astype(F32)
    for r in range(SB):
        for kind in range(3):
            for p in range(2):
                lo = 192 * head_of(r, 2 * p) + 64 * kind
                hi = 192 * head_of(r, 2 * p + 1) + 64 * kind
                at = 256 * kind + 128 * p
                PWQ[r, :, at : at + 128] = halves((wq_f, lo), (wq_f, hi)).astype(BF)
    tile = prm[...].astype(F32)
    row = lax.broadcasted_iota(jnp.int32, (16, 128), 0)
    tile = jnp.where(row < 3, pltpu.roll(tile, 32 * s, 1), tile)
    PRM[b, rows(16 * s, 16), :] = tile.astype(BF)
    Wi[rows(128 * b + 32 * s, 32), :] = PWI[s]
    Wq[rows(128 * b + 32 * s, 32), :] = PWQ[s]
    Wo[rows(128 * b, 128), :] = wo[...]
    WaAll[z, xx] = wa[...]

    barrier = pltpu.get_barrier_semaphore()
    partners = [core, ypart, diag, xpart] + [zdev(k) for k in (1, 2, 3)]
    for device in partners:
        pl.semaphore_signal(barrier, inc=1, device_id=device, device_id_type=MESH)
    pl.semaphore_wait(barrier, len(partners))

    def seq_sends(name, src_of, dst):
        for i, (device, owner) in enumerate(
            ((core, 2 * y + oc), (ypart, 2 * oy + c), (diag, 2 * oy + oc))
        ):
            start(
                lambda i=i, device=device, owner=owner: link.copy(
                    name, i, 3, src_of(owner), dst(), device
                )
            )

    def seq_waits(name, src, dst_of):
        for i, owner in enumerate((2 * y + oc, 2 * oy + c, 2 * oy + oc)):
            link.copy(name, i, 3, src, dst_of(owner), core).wait_recv()

    def prm_block(owner):
        return PRM.at[b, rows(16 * owner, 16)]

    def wi_block(owner):
        return Wi.at[rows(128 * b + 32 * owner, 32)]

    def wq_block(owner):
        return Wq.at[rows(128 * b + 32 * owner, 32)]

    gathers = {
        "prm": lambda bb: PRM.at[bb],
        "wa": lambda bb: WaAll.at[bb // 2, bb % 2],
        "wi": lambda bb: Wi.at[rows(128 * bb, 128)],
        "wo": lambda bb: Wo.at[rows(128 * bb, 128)],
        "wq": lambda bb: Wq.at[rows(128 * bb, 128)],
    }

    def gather_start(name):
        block = gathers[name]
        for k in (1, 2, 3):
            start(lambda k=k: link.copy(name + "z", k - 1, 3, block(b), block(b), zdev(k)))
        start(lambda: link.copy(name + "x", 0, 4, block(b), block(b), xpart))

    def gather_pass(name, k):
        block = gathers[name]
        bb = 2 * zfrom(k) + xx
        link.copy(name + "z", k - 1, 3, block(bb), block(bb), core).wait_recv()

        def make():
            held = block(2 * zfrom(k) + xx)
            return link.copy(name + "x", k, 4, held, held, xpart)

        start(make)

    def gather_end(name, ks=(0, 1, 2, 3)):
        block = gathers[name]
        for k in ks:
            bb = 2 * zfrom(k) + ox
            link.copy(name + "x", k, 4, block(bb), block(bb), core).wait_recv()

    seq_sends("prms", lambda owner: prm_block(s), lambda: prm_block(s))
    seq_sends("wis", lambda owner: PWI.at[owner], lambda: wi_block(s))
    gather_start("wa")
    seq_sends("wqs", lambda owner: PWQ.at[owner], lambda: wq_block(s))

    def rows_start(name, src, dst):
        for w in range(2):
            start(lambda w=w: link.copy(name + "c", w, 2, src.at[w], dst.at[w, own], core))
            start(lambda w=w: link.copy(name + "y", w, 2, src.at[w], dst.at[w, own], ypart))

    def rows_pass(name, dst, w):
        block = dst.at[w, rows(SL * (2 * oy + c), SL)]
        link.copy(name + "y", w, 2, block, block, core).wait_recv()
        link.copy(name + "f", w, 2, block, block, core).start()

    def rows_left(name, dst, w):
        block = dst.at[w, rows(SL * (2 * oy + c), SL)]
        link.copy(name + "f", w, 2, block, block, core).wait_send()

    def rows_end_core(name, dst, w):
        block = dst.at[w, rows(SL * (2 * y + oc), SL)]
        link.copy(name + "c", w, 2, block, block, core).wait_recv()

    def rows_end_far(name, dst, w):
        block = dst.at[w, rows(SL * (2 * oy + oc), SL)]
        link.copy(name + "f", w, 2, block, block, core).wait_recv()

    rows_start("x", x_in, X)
    seq_waits("prms", PRM.at[b, rows(16 * s, 16)], prm_block)
    gather_start("prm")
    seq_waits("wis", PWI.at[0], wi_block)
    gather_start("wi")
    for k in (1, 2, 3):
        gather_pass("prm", k)
    for k in (1, 2, 3):
        gather_pass("wa", k)
    gather_end("prm")

    for bb in range(8):
        total = (
            PRM[bb, 0:16, :].astype(F32)
            + PRM[bb, 16:32, :].astype(F32)
            + PRM[bb, 32:48, :].astype(F32)
            + PRM[bb, 48:64, :].astype(F32)
        )
        mine = PRM[bb, rows(16 * s, 16), :].astype(F32)
        PR[:, 128 * bb : 128 * bb + 128] = jnp.where(row < 3, total, mine)[0:8]

    for cp in locals_:
        cp.wait()

    def norm_rows(w, owner):
        r = rows(SL * owner, SL)
        v = X[w, r, :].astype(F32)
        v = v - jnp.mean(v, axis=-1, keepdims=True)
        var = jnp.mean(v * v, axis=-1, keepdims=True)
        N[w, r, :] = (v * lax.rsqrt(var + norm_eps) * PR[0:1, :] + PR[1:2, :]).astype(BF)

    def norm_own(w, carry):
        norm_rows(w, s)
        norm_rows(w, 2 * y + oc)
        return carry

    def norm_far(w, carry):
        norm_rows(w, 2 * oy + c)
        norm_rows(w, 2 * oy + oc)
        return carry

    for w in range(2):
        rows_end_core("x", X, w)
    lax.fori_loop(0, 2, norm_own, 0)
    gather_pass("wi", 1)
    for w in range(2):
        rows_pass("x", X, w)
    rows_start("g", g_in, G)
    gather_pass("wi", 2)
    gather_pass("wi", 3)
    gather_start("wo")
    for w in range(2):
        rows_end_far("x", X, w)
    lax.fori_loop(0, 2, norm_far, 0)
    gather_end("wi")

    def hidden_step(i, carry):
        w, t, u = i // 8, (i // 4) % 2, i % 4
        r, l = rows(512 * t, 512), lanes(256 * u, 256)
        v = dot(N[w, r, :], Wi[:, l], 1, 0) + PR[3:4, l]
        value, slope = gelu_pair(v)
        A[w, r, l] = value.astype(BF)
        H[w, r, l] = slope.astype(BF)

        @pl.when(i == 3)
        def _():
            gather_pass("wo", 1)

        @pl.when(i == 7)
        def _():
            gather_pass("wo", 2)

        @pl.when(i == 11)
        def _():
            gather_pass("wo", 3)
            seq_waits("wqs", PWQ.at[0], wq_block)
            gather_start("wq")

        return carry

    lax.fori_loop(0, 16, hidden_step, 0)
    for w in range(2):
        rows_end_core("g", G, w)
        rows_pass("g", G, w)
    for w in range(2):
        rows_end_far("g", G, w)
    gather_end("wo")
    gather_end("wa")
    for w in range(2):
        rows_left("x", X, w)
    start(lambda: link.copy("wac", 0, 1, WaAll.at[:, oc], Wa.at[:, c], core))
    Wa[:, c] = WaAll[:, c]

    sums = {"o": (GO, XO, ZO), "i": (GI, XI, ZI), "q": (GQ, XQ, ZQ), "a": (GA, XA, ZA), "t": (GT, XT, ZT)}

    def add_into(dst, other):
        dst[...] = (dst[...].astype(F32) + other[...].astype(F32)).astype(BF)

    def o_z(q):
        link.copy("ox", q, 4, XO.at[q], XO.at[q], core).wait_recv()

        @pl.when(z != q)
        def _():
            add_into(GO.at[q, xx], XO.at[q])
            k = (q + 4 - z) % 4
            link.copy("oz", k - 1, 3, GO.at[q, xx], ZO.at[k - 1], (2 * q + xx, s)).start()

    def i_z(q):
        link.copy("ix", q, 4, XI.at[q], XI.at[q], core).wait_recv()
        for k in (1, 2, 3):
            zz = (z + k) % 4
            add_into(GI.at[q, xx, zz], XI.at[q, zz])
            link.copy("iz", 3 * q + k - 1, 12, GI.at[q, xx, zz], ZI.at[k - 1, q], zdev(k)).start()

    def back_step(q, carry):
        l = lanes(256 * q, 256)

        def dh_step(i, total):
            w, r = i // 2, rows(512 * (i % 2), 512)
            d = dot(G[w, r, :], Wo[rows(256 * q, 256), :], 1, 1) * H[w, r, l].astype(F32)
            d = d.astype(BF)
            H[w, r, l] = d
            return total + jnp.sum(d.astype(F32), axis=0, keepdims=True)

        TAIL[3:4, l] = lax.fori_loop(0, 4, dh_step, jnp.zeros((1, 256), F32))
        go = dot(A[0, :, l], G[0], 0, 0) + dot(A[1, :, l], G[1], 0, 0)
        GO[q, 0] = go[:128].astype(BF)
        GO[q, 1] = go[128:].astype(BF)
        link.copy("ox", q, 4, GO.at[q, ox], XO.at[q], xpart).start()
        gi = dot(H[0, :, l], N[0], 0, 0) + dot(H[1, :, l], N[1], 0, 0)
        for bb in range(8):
            GI[q, bb % 2, bb // 2] = gi[:, 128 * bb : 128 * bb + 128].astype(BF)
        link.copy("ix", q, 4, GI.at[q, ox], XI.at[q], xpart).start()

        @pl.when(q == 0)
        def _():
            gather_pass("wq", 1)

        @pl.when(q == 1)
        def _():
            gather_pass("wq", 2)

        @pl.when(q == 2)
        def _():
            gather_pass("wq", 3)

        @pl.when(q > 0)
        def _():
            o_z(q - 1)
            i_z(q - 1)

        return carry

    TAIL[...] = jnp.zeros_like(TAIL)
    lax.fori_loop(0, 4, back_step, 0)

    gather_end("wq")
    link.copy("wac", 0, 1, WaAll.at[:, oc], Wa.at[:, oc], core).wait_recv()
    even = lax.broadcasted_iota(jnp.int32, (1, 128), 1) % 2 == 0

    def turn(v, cos_rows, sin_rows):
        swapped = jnp.where(even, pltpu.roll(v, 127, 1), pltpu.roll(v, 1, 1))
        return v * cos_rows + swapped * sin_rows

    def qkv_step(i, total):
        w, r = i // 4, rows(256 * (i % 4), 256)
        n = N[w, r, :]
        cos_rows, sin_rows = cosine[r, :], sine[r, :]
        for kind in range(3):
            v = dot(n, Wq[:, 256 * kind : 256 * kind + 256], 1, 0)
            for p in range(2):
                tile_v = v[:, 128 * p : 128 * p + 128]
                if kind < 2:
                    tile_v = turn(tile_v, cos_rows, sin_rows)
                if kind == 0:
                    tile_v = tile_v * 0.125
                QKV[w, r, 256 * kind + 128 * p : 256 * kind + 128 * p + 128] = tile_v.astype(BF)
        g = G[w, r, :]
        dO[w, r, :] = dot(g, Wa[...].reshape(256, 1024), 1, 1).astype(BF)
        return total + jnp.sum(g.astype(F32), axis=0, keepdims=True)

    TAIL[2:3, :] = lax.fori_loop(0, 8, qkv_step, jnp.zeros((1, 1024), F32))
    o_z(3)
    i_z(3)

    lane = lax.broadcasted_iota(jnp.int32, (1, 128), 1)
    place = lax.broadcasted_iota(jnp.int32, (S, 1), 0)
    BQ = 512
    key_i = lax.broadcasted_iota(jnp.int32, (BQ, BQ), 0)
    query_i = lax.broadcasted_iota(jnp.int32, (BQ, BQ), 1)

    def attend(w, p):
        ending = ends[w]

        def part(kind):
            return lanes(256 * kind + 128 * p)

        pl_ = lanes(128 * p)
        keys, values = QKV[w, :, part(1)], QKV[w, :, part(2)]
        ktT[...] = keys.T
        vtT[...] = values.T
        doT[...] = dO[w, :, pl_].T
        dkA[...] = jnp.zeros_like(dkA)
        dvA[...] = jnp.zeros_like(dvA)

        def head(hh, carry):
            inside = (lane // 64) == hh
            feature = lane == (64 - 64 * hh)
            t = jnp.where(place < ending, NEG, 0.0)
            khat[...] = jnp.where(
                inside, keys.astype(F32), jnp.where(feature, t, 0.0)
            ).astype(BF)
            hr = rows(64 * hh, 64)
            for qb in range(S // BQ):
                nk = (qb + 1) * BQ
                qr = slice(qb * BQ, nk)
                q = QKV[w, qr, part(0)].astype(F32)
                u = jnp.where(place[qr] >= ending, 1.0, 0.0)
                q_in = jnp.where(inside, q, 0.0).astype(BF)
                q_hat = jnp.where(inside, q, jnp.where(feature, u, 0.0)).astype(BF)
                d_in = jnp.where(inside, dO[w, qr, pl_].astype(F32), 0.0).astype(BF)
                sc = dot(khat[0:nk, :], q_hat, 1, 1)
                last = jnp.where(key_i <= query_i, sc[nk - BQ :], NEG)
                sc = last if qb == 0 else jnp.concatenate([sc[: nk - BQ], last], axis=0)
                e = jnp.exp(sc - jnp.max(sc, axis=0, keepdims=True))
                pn = e * (1.0 / jnp.sum(e, axis=0, keepdims=True))
                pb = pn.astype(BF)
                o = dot(vtT[hr, 0:nk], pb, 1, 0)
                oT[hr, qr] = o
                dp = dot(values[0:nk], d_in, 1, 1)
                dd = jnp.sum(o * doT[hr, qr].astype(F32), axis=0, keepdims=True)
                ds = (pn * (dp - dd)).astype(BF)
                dqT[hr, qr] = dot(ktT[hr, 0:nk], ds, 1, 0)
                dkA[0:nk, :] += dot(ds, q_in, 1, 0)
                dvA[0:nk, :] += dot(pb, d_in, 1, 0)
            return carry

        lax.fori_loop(0, 2, head, 0)
        cos_rows, sin_rows = cosine[...], -sine[...]
        att[w, :, pl_] = oT[...].T.astype(BF)
        QKV[w, :, part(0)] = turn(dqT[...].T * 0.125, cos_rows, sin_rows).astype(BF)
        QKV[w, :, part(1)] = turn(dkA[...], cos_rows, sin_rows).astype(BF)
        QKV[w, :, part(2)] = dvA[...].astype(BF)

    def share_step(w):
        def step(i, total):
            r = rows(256 * i, 256)
            value = dot(A[w, r, :], Wo[...], 1, 0) + dot(att[w, r, :], Wa[...].reshape(256, 1024), 1, 0)
            A[w, r, :] = value.astype(BF)
            d = dot(H[w, r, :], Wi[...], 1, 1) + dot(QKV[w, r, :], Wq[...], 1, 1)
            H[w, r, :] = d.astype(BF)
            n = (N[w, r, :].astype(F32) - PR[1:2, :]) / PR[0:1, :]
            return (
                total[0] + jnp.sum(d, axis=0, keepdims=True),
                total[1] + jnp.sum(d * n, axis=0, keepdims=True),
            )

        zero = jnp.zeros((1, 1024), F32)
        first, second = lax.fori_loop(0, 4, step, (zero, zero))
        TAIL[0:1, :] += first
        TAIL[1:2, :] += second

    shares = (A, H)

    def share_c(w):
        for t in range(2):
            for yy in range(2):
                src = shares[t].at[w, rows(SL * (2 * yy + oc), SL)]
                dst = X.at[w, rows(SL * (2 * t + yy), SL)]
                link.copy("sc", 4 * w + 2 * t + yy, 8, src, dst, core).start()

    def share_y(w):
        for t in (1, 0):
            dst = X.at[w, rows(SL * (2 * t + oy), SL)]
            for yy in range(2):
                slot = X.at[w, rows(SL * (2 * t + yy), SL)]
                link.copy("sc", 4 * w + 2 * t + yy, 8, slot, slot, core).wait_recv()
            src = shares[t].at[w, rows(SL * (2 * oy + c), SL)]
            add_into(src, dst)
            link.copy("sy", 2 * w + t, 4, src, YR.at[w, t], ypart).start()

    def window(w, carry):
        def pair(p, inner):
            attend(w, p)

            @pl.when((w == 1) & (p == 0))
            def _():
                share_y(0)

            return inner

        lax.fori_loop(0, 2, pair, 0)
        share_step(w)
        share_c(w)
        return carry

    lax.fori_loop(0, 2, window, 0)

    def gq_step(kind, carry):
        l = lanes(256 * kind, 256)
        gq = dot(QKV[0, :, l], N[0], 0, 0) + dot(QKV[1, :, l], N[1], 0, 0)
        for bb in range(8):
            GQ[bb % 2, bb // 2, rows(256 * kind, 256), :] = gq[:, 128 * bb : 128 * bb + 128].astype(BF)
        return carry

    lax.fori_loop(0, 3, gq_step, 0)
    again = [
        pltpu.make_async_copy(x_in.at[w], N.at[w, 0:SL], local_sems.at[3 * w + 2]) for w in range(2)
    ]
    for cp in again:
        cp.start()
    start(lambda: link.copy("qx", 0, 1, GQ.at[ox], XQ, xpart))
    share_y(1)
    ga = dot(att[0], G[0], 0, 0) + dot(att[1], G[1], 0, 0)
    for j in range(4):
        for cc in range(2):
            at = 64 * j + 32 * cc
            GAS[cc, j] = ga[at : at + 32].astype(BF)
    start(lambda: link.copy("ac", 0, 1, GAS.at[oc], GA.at[c], core))
    GA[c] = GAS[c]
    tail = TAIL[...]
    for bb in range(8):
        GT[bb % 2, bb // 2] = tail[:, 128 * bb : 128 * bb + 128].astype(BF)
    start(lambda: link.copy("tx", 0, 1, GT.at[ox], XT, xpart))
    link.copy("ac", 0, 1, GAS.at[0], GA.at[oc], core).wait_recv()
    start(lambda: link.copy("ax", 0, 1, GA.at[ox], XA, xpart))

    def final_o():
        for k in (1, 2, 3):
            link.copy("oz", k - 1, 3, ZO.at[k - 1], ZO.at[k - 1], core).wait_recv()
        grad_o[...] = (
            GO[z, xx].astype(F32)
            + XO[z].astype(F32)
            + ZO[0].astype(F32)
            + ZO[1].astype(F32)
            + ZO[2].astype(F32)
        )

    def final_i():
        for q in range(4):
            for k in (1, 2, 3):
                link.copy("iz", 3 * q + k - 1, 12, ZI.at[k - 1, q], ZI.at[k - 1, q], core).wait_recv()
            total = GI[q, xx, z].astype(F32) + XI[q, z].astype(F32)
            for k in range(3):
                total = total + ZI[k, q].astype(F32)
            turned = total.T.astype(BF)
            for owner in range(4):
                SWI[owner, :, 256 * q : 256 * q + 256] = turned[32 * owner : 32 * owner + 32]

    def z_step(name):
        group, received, _ = sums[name]
        link.copy(name + "x", 0, 1, received, received, core).wait_recv()
        for k in (1, 2, 3):
            zz = (z + k) % 4
            add_into(group.at[xx, zz], received.at[zz])
            start(
                lambda k=k: link.copy(
                    name + "z", k - 1, 3, group.at[xx, (z + k) % 4], sums[name][2].at[k - 1], zdev(k)
                )
            )

    def z_total(name):
        group, received, landed = sums[name]
        for k in (1, 2, 3):
            link.copy(name + "z", k - 1, 3, landed.at[k - 1], landed.at[k - 1], core).wait_recv()
        total = group[xx, z].astype(F32) + received[z].astype(F32)
        for k in range(3):
            total = total + landed[k].astype(F32)
        return total

    final_o()
    final_i()
    RWI[s] = SWI[s]
    seq_sends("swi", lambda owner: SWI.at[owner], lambda: RWI.at[s])

    z_step("q")
    z_step("t")
    z_step("a")

    def final_rows(w, carry):
        again[w].wait()
        v = N[w, 0:SL, :].astype(F32)
        mine = rows(SL * s, SL)
        for t in (1, 0):
            link.copy("sy", 2 * w + t, 4, YR.at[w, t], YR.at[w, t], core).wait_recv()
        value = (
            A[w, mine, :].astype(F32)
            + X[w, rows(SL * y, SL), :].astype(F32)
            + YR[w, 0].astype(F32)
        )
        out[w] = (v + value + PR[2:3, :]).astype(BF)
        d = (
            H[w, mine, :].astype(F32)
            + X[w, rows(SL * (2 + y), SL), :].astype(F32)
            + YR[w, 1].astype(F32)
        )
        v = v - jnp.mean(v, axis=-1, keepdims=True)
        scale = lax.rsqrt(jnp.mean(v * v, axis=-1, keepdims=True) + norm_eps)
        v = v * scale
        d = d * PR[0:1, :]
        d = d - jnp.mean(d, axis=-1, keepdims=True) - v * jnp.mean(d * v, axis=-1, keepdims=True)
        grad_in[w] = G[w, mine, :].astype(F32) + scale * d
        return carry

    final_rows(0, 0)

    total_q = z_total("q")
    total_t = z_total("t")
    grad_bin[...] = total_t[0:8]
    turned_q = total_q.T.astype(BF)
    turned_t = jnp.concatenate([total_t, jnp.zeros((112, 128), F32)], axis=0).T.astype(BF)
    for owner in range(4):
        SWQ[owner, :, 0:768] = turned_q[32 * owner : 32 * owner + 32]
        SWQ[owner, :, 768:896] = turned_t[32 * owner : 32 * owner + 32]
    RWQ[s] = SWQ[s]
    seq_sends("swq", lambda owner: SWQ.at[owner], lambda: RWQ.at[s])
    grad_a[...] = z_total("a")

    def from_seq(name, landed):
        for i, owner in enumerate((2 * y + oc, 2 * oy + c, 2 * oy + oc)):
            link.copy(name, i, 3, landed.at[owner], landed.at[owner], core).wait_recv()

    from_seq("swi", RWI)
    for r in range(4):
        for blk in range(8):
            at = 512 * blk + 128 * r
            grad_i[:, at : at + 128] = RWI[r, :, 128 * blk : 128 * blk + 128].astype(F32)

    final_rows(1, 0)

    from_seq("swq", RWQ)
    got = [RWQ[r].astype(F32) for r in range(4)]
    place_of = {}
    for r in range(4):
        for j in range(4):
            for kind in range(3):
                place_of[3 * head_of(r, j) + kind] = (got[r], 256 * kind + 128 * (j // 2) + 64 * (j % 2))
    for at in range(24):
        grad_q[:, 128 * at : 128 * at + 128] = halves(place_of[2 * at], place_of[2 * at + 1])
    summed = got[0][:, 768:896] + got[1][:, 768:896] + got[2][:, 768:896] + got[3][:, 768:896]
    grad_small[...] = jnp.where(lane == 2, got[0][:, 768:896], summed)

    for make in pending:
        make().wait_send()
    for w in range(2):
        rows_left("g", G, w)
    for q in range(4):
        link.copy("ox", q, 4, GO.at[q, ox], XO.at[q], xpart).wait_send()
        link.copy("ix", q, 4, GI.at[q, ox], XI.at[q], xpart).wait_send()
        for k in (1, 2, 3):
            zz = (z + k) % 4
            link.copy("iz", 3 * q + k - 1, 12, GI.at[q, xx, zz], ZI.at[k - 1, q], zdev(k)).wait_send()
    for k in (1, 2, 3):
        zz = (z + k) % 4
        link.copy("oz", k - 1, 3, GO.at[zz, xx], ZO.at[k - 1], zdev(k)).wait_send()
    for w in range(2):
        for t in range(2):
            for yy in range(2):
                src = shares[t].at[w, rows(SL * (2 * yy + oc), SL)]
                dst = X.at[w, rows(SL * (2 * t + yy), SL)]
                link.copy("sc", 4 * w + 2 * t + yy, 8, src, dst, core).wait_send()
            src = shares[t].at[w, rows(SL * (2 * oy + c), SL)]
            link.copy("sy", 2 * w + t, 4, src, YR.at[w, t], ypart).wait_send()


def turn_tables(seq_len):
    inverse = 10000.0 ** (-2.0 * np.arange(ROTARY // 2) / ROTARY)
    angles = np.arange(seq_len)[:, None] * inverse[None, :]
    cosine = np.ones((seq_len, HD), np.float32)
    sine = np.zeros((seq_len, HD), np.float32)
    cosine[:, 0:ROTARY:2] = cosine[:, 1:ROTARY:2] = np.cos(angles)
    sine[:, 0:ROTARY:2] = -np.sin(angles)
    sine[:, 1:ROTARY:2] = np.sin(angles)
    return np.tile(cosine, (1, 2)), np.tile(sine, (1, 2))


def fused_shards(inputs, ends, ln_gain, ln_bias, w_qkv, w_attn, w_in, b_in, w_out, b_out, cotangent):
    def widen(v):
        return jnp.pad(v, (0, 128 - v.shape[0]))

    prm = jnp.pad(jnp.stack([widen(ln_gain), widen(ln_bias), widen(b_out), b_in]), ((0, 12), (0, 0)))
    cosine, sine = turn_tables(1024)
    in_vmem = pl.BlockSpec(memory_space=pltpu.VMEM)
    in_any = pl.BlockSpec(memory_space=pl.ANY)
    rows_type = (2, 1024, 1024)
    results = pl.pallas_call(
        fused_layer,
        out_shape=(
            jax.ShapeDtypeStruct((2, 256, 1024), BF),
            jax.ShapeDtypeStruct((2, 256, 1024), F32),
            jax.ShapeDtypeStruct((32, 3072), F32),
            jax.ShapeDtypeStruct((32, 1024), F32),
            jax.ShapeDtypeStruct((32, 4096), F32),
            jax.ShapeDtypeStruct((128, 1024), F32),
            jax.ShapeDtypeStruct((32, 128), F32),
            jax.ShapeDtypeStruct((8, 128), F32),
        ),
        in_specs=[pl.BlockSpec(memory_space=pltpu.SMEM)] + [in_vmem] * 7 + [in_any] * 2,
        out_specs=(in_vmem,) * 8,
        scratch_shapes=[
            pltpu.VMEM(rows_type, BF),
            pltpu.VMEM(rows_type, BF),
            pltpu.VMEM(rows_type, BF),
            pltpu.VMEM(rows_type, BF),
            pltpu.VMEM(rows_type, BF),
            pltpu.VMEM((1024, 1024), BF),
            pltpu.VMEM((1024, 1024), BF),
            pltpu.VMEM((1024, 768), BF),
            pltpu.VMEM((4, 2, 32, 1024), BF),
            pltpu.VMEM((4, 2, 32, 1024), BF),
            pltpu.VMEM((4, 32, 1024), BF),
            pltpu.VMEM((4, 32, 768), BF),
            pltpu.VMEM((8, 64, 128), BF),
            pltpu.VMEM((8, 1024), F32),
            pltpu.VMEM((2, 1024, 768), BF),
            pltpu.VMEM((2, 1024, 256), BF),
            pltpu.VMEM((2, 1024, 256), BF),
            pltpu.VMEM((4, 2, 128, 1024), BF),
            pltpu.VMEM((4, 128, 1024), BF),
            pltpu.VMEM((3, 128, 1024), BF),
            pltpu.VMEM((4, 2, 4, 256, 128), BF),
            pltpu.VMEM((4, 4, 256, 128), BF),
            pltpu.VMEM((3, 4, 256, 128), BF),
            pltpu.VMEM((2, 4, 768, 128), BF),
            pltpu.VMEM((4, 768, 128), BF),
            pltpu.VMEM((3, 768, 128), BF),
            pltpu.VMEM((2, 4, 32, 1024), BF),
            pltpu.VMEM((4, 32, 1024), BF),
            pltpu.VMEM((3, 32, 1024), BF),
            pltpu.VMEM((2, 4, 32, 1024), BF),
            pltpu.VMEM((2, 4, 16, 128), BF),
            pltpu.VMEM((4, 16, 128), BF),
            pltpu.VMEM((3, 16, 128), BF),
            pltpu.VMEM((2, 2, 256, 1024), BF),
            pltpu.VMEM((4, 32, 1024), BF),
            pltpu.VMEM((4, 32, 1024), BF),
            pltpu.VMEM((4, 32, 896), BF),
            pltpu.VMEM((4, 32, 896), BF),
            pltpu.VMEM((16, 1024), F32),
            pltpu.VMEM((1024, 128), BF),
            pltpu.VMEM((128, 1024), BF),
            pltpu.VMEM((128, 1024), BF),
            pltpu.VMEM((128, 1024), BF),
            pltpu.VMEM((128, 1024), F32),
            pltpu.VMEM((128, 1024), F32),
            pltpu.VMEM((1024, 128), F32),
            pltpu.VMEM((1024, 128), F32),
            pltpu.SemaphoreType.DMA((160,)),
            pltpu.SemaphoreType.DMA((160,)),
            pltpu.SemaphoreType.DMA((6,)),
        ],
        compiler_params=pltpu.CompilerParams(
            collective_id=0, has_side_effects=True, vmem_limit_bytes=63 * 2**20
        ),
        cost_estimate=pl.CostEstimate(flops=46 * 10**9, bytes_accessed=10**7, transcendentals=10**7),
    )(ends, prm, w_qkv, w_attn, w_in, w_out, cosine, sine, inputs, cotangent)
    out, grad_in, grad_q, grad_a, grad_i, grad_o, small, bias_in = results
    return (
        out,
        grad_in,
        small[:, 1],
        small[:, 0],
        grad_q,
        grad_a,
        grad_i,
        bias_in[3],
        grad_o,
        small[:, 2],
    )


def fits_fused(mesh):
    return mesh.shape["batch"] == 8 and mesh.shape["seq"] == 4


def solution(mesh):
    return jax.shard_map(
        fused_shards if fits_fused(mesh) else shards,
        mesh=mesh,
        in_specs=(
            P("batch", "seq", None),
            P("batch"),
            P(("batch", "seq")),
            P(("batch", "seq")),
            P(("batch", "seq"), None),
            P(("batch", "seq"), None),
            P(("batch", "seq"), None),
            P(("batch", "seq")),
            P(("batch", "seq"), None),
            P(("batch", "seq")),
            P("batch", "seq", None),
        ),
        out_specs=(
            P("batch", "seq", None),
            P("batch", "seq", None),
            P(("batch", "seq")),
            P(("batch", "seq")),
            P(("batch", "seq"), None),
            P(("batch", "seq"), None),
            P(("batch", "seq"), None),
            P(("batch", "seq")),
            P(("batch", "seq"), None),
            P(("batch", "seq")),
        ),
        check_vma=False,
    )
```

```python
import math

import jax
import jax.numpy as jnp
import numpy as np
from jax import lax
from jax.experimental import pallas as pl
from jax.experimental.pallas import tpu as pltpu
from jax.sharding import PartitionSpec as P

HEADS = 16
HD = 64
ROTARY = 32
MICRO = 2


norm_eps = 1e-05
gelu_factor = 0.7978845608028654
masked_score = -1e30


def gelu_tanh(values):
    return (
        0.5
        * values
        * (1.0 + jnp.tanh(gelu_factor * (values + 0.044715 * values * values * values)))
    )


def layer_norm(row_values, norm_gain, norm_shift):
    average = jnp.mean(row_values, axis=-1, keepdims=True)
    centered = row_values - average
    variance = jnp.mean(centered * centered, axis=-1, keepdims=True)
    return centered * lax.rsqrt(variance + norm_eps) * norm_gain + norm_shift


def rotary_tables(positions):
    pair_index = jnp.arange(ROTARY // 2, dtype=jnp.float32)
    inverse = 10000.0 ** (-2.0 * pair_index / ROTARY)
    angles = positions[:, None] * inverse[None, :]
    return (jnp.cos(angles), jnp.sin(angles))


def rotate(vectors, cosine, sine_table):
    rotated = vectors[..., :ROTARY]
    even_part = rotated[..., 0::2]
    odd_part = rotated[..., 1::2]
    cosine_wide = cosine[:, None, :]
    sine_wide = sine_table[:, None, :]
    new_even = even_part * cosine_wide - odd_part * sine_wide
    new_odd = odd_part * cosine_wide + even_part * sine_wide
    merged = jnp.stack([new_even, new_odd], axis=-1).reshape(rotated.shape)
    return jnp.concatenate([merged, vectors[..., ROTARY:]], axis=-1)


def visible(query_places, key_places, ending):
    query_after = query_places[:, None] >= ending
    key_after = key_places[None, :] >= ending
    return (key_places[None, :] <= query_places[:, None]) & (query_after == key_after)


def block_scores(block_queries, key_vectors, query_places, key_places, ending, score_scale):
    scores = (
        jnp.einsum("qhd,khd->hqk", block_queries, key_vectors, preferred_element_type=jnp.float32)
        * score_scale
    )
    return jnp.where(visible(query_places, key_places, ending)[None], scores, masked_score)


def attend_forward(packed, ending):
    seq_len, head_count, triple = packed.shape
    head_size = triple // 3
    block_rows = min(512, seq_len)
    score_scale = 1.0 / math.sqrt(head_size)
    queries = packed[:, :, :head_size]
    key_vectors = packed[:, :, head_size : 2 * head_size]
    values = packed[:, :, 2 * head_size :]
    key_places = jnp.arange(seq_len, dtype=jnp.int32)

    def one_block(block_index):
        first_row = block_index * block_rows
        block_queries = lax.dynamic_slice_in_dim(queries, first_row, block_rows, 0)
        query_places = first_row + jnp.arange(block_rows, dtype=jnp.int32)
        scores = block_scores(
            block_queries, key_vectors, query_places, key_places, ending, score_scale
        )
        row_peak = jnp.max(scores, axis=-1, keepdims=True)
        weights = jnp.exp(scores - row_peak)
        row_total = jnp.sum(weights, axis=-1, keepdims=True)
        probabilities = (weights / row_total).astype(jnp.bfloat16)
        result = jnp.einsum(
            "hqk,khd->qhd", probabilities, values, preferred_element_type=jnp.float32
        )
        return (result.astype(jnp.bfloat16), row_peak, row_total)

    results, peaks, totals = lax.map(one_block, jnp.arange(seq_len // block_rows, dtype=jnp.int32))
    return (results.reshape(seq_len, head_count, head_size), peaks, totals)


def attend_backward(packed, d_attended, peaks, totals, ending, full_cosine, full_sine):
    seq_len, head_count, triple = packed.shape
    head_size = triple // 3
    block_rows = min(512, seq_len)
    score_scale = 1.0 / math.sqrt(head_size)
    queries = packed[:, :, :head_size]
    key_vectors = packed[:, :, head_size : 2 * head_size]
    values = packed[:, :, 2 * head_size :]
    key_places = jnp.arange(seq_len, dtype=jnp.int32)

    def one_block(running, block_inputs):
        key_grads, value_grads = running
        block_index, row_peak, row_total = block_inputs
        first_row = block_index * block_rows
        block_queries = lax.dynamic_slice_in_dim(queries, first_row, block_rows, 0)
        block_grads = lax.dynamic_slice_in_dim(d_attended, first_row, block_rows, 0)
        query_places = first_row + jnp.arange(block_rows, dtype=jnp.int32)
        scores = block_scores(
            block_queries, key_vectors, query_places, key_places, ending, score_scale
        )
        probabilities = jnp.exp(scores - row_peak) / row_total
        rounded_probs = probabilities.astype(jnp.bfloat16)
        d_probs = jnp.einsum(
            "qhd,khd->hqk", block_grads, values, preferred_element_type=jnp.float32
        )
        row_dot = jnp.sum(probabilities * d_probs, axis=-1, keepdims=True)
        d_scores = (probabilities * (d_probs - row_dot)).astype(jnp.bfloat16)
        query_grads = (
            jnp.einsum("hqk,khd->qhd", d_scores, key_vectors, preferred_element_type=jnp.float32)
            * score_scale
        )
        key_grads = (
            key_grads
            + jnp.einsum(
                "hqk,qhd->khd", d_scores, block_queries, preferred_element_type=jnp.float32
            )
            * score_scale
        )
        value_grads = value_grads + jnp.einsum(
            "hqk,qhd->khd", rounded_probs, block_grads, preferred_element_type=jnp.float32
        )
        return ((key_grads, value_grads), query_grads)

    zero_sums = jnp.zeros((seq_len, head_count, head_size), jnp.float32)
    block_ids = jnp.arange(seq_len // block_rows, dtype=jnp.int32)
    (key_grads, value_grads), query_grads = lax.scan(
        one_block, (zero_sums, zero_sums), (block_ids, peaks, totals)
    )
    query_grads = query_grads.reshape(seq_len, head_count, head_size)
    flipped_sine = -full_sine
    combined = jnp.stack(
        [
            rotate(query_grads, full_cosine, flipped_sine),
            rotate(key_grads, full_cosine, flipped_sine),
            value_grads,
        ],
        axis=2,
    )
    return combined.astype(jnp.bfloat16).reshape(seq_len, head_count, triple)


def collect(ln_gain, ln_bias, w_qkv, w_attn, w_in, b_in, w_out, b_out):
    return (
        lax.all_gather(ln_gain, ("batch", "seq"), axis=0, tiled=True),
        lax.all_gather(ln_bias, ("batch", "seq"), axis=0, tiled=True),
        lax.all_gather(w_qkv, ("batch", "seq"), axis=0, tiled=True),
        lax.all_gather(w_attn, ("batch", "seq"), axis=0, tiled=True),
        lax.all_gather(w_in, ("batch", "seq"), axis=0, tiled=True),
        lax.all_gather(b_in, ("batch", "seq"), axis=0, tiled=True),
        lax.all_gather(w_out, ("batch", "seq"), axis=0, tiled=True),
        lax.all_gather(b_out, ("batch", "seq"), axis=0, tiled=True),
    )


def reduce_grads(gradients):
    return (
        lax.psum_scatter(gradients[0], ("batch", "seq"), scatter_dimension=0, tiled=True),
        lax.psum_scatter(gradients[1], ("batch", "seq"), scatter_dimension=0, tiled=True),
        lax.psum_scatter(gradients[2], ("batch", "seq"), scatter_dimension=0, tiled=True),
        lax.psum_scatter(gradients[3], ("batch", "seq"), scatter_dimension=0, tiled=True),
        lax.psum_scatter(gradients[4], ("batch", "seq"), scatter_dimension=0, tiled=True),
        lax.psum_scatter(gradients[5], ("batch", "seq"), scatter_dimension=0, tiled=True),
        lax.psum_scatter(gradients[6], ("batch", "seq"), scatter_dimension=0, tiled=True),
        lax.psum_scatter(gradients[7], ("batch", "seq"), scatter_dimension=0, tiled=True),
    )


def shards(inputs, ends, ln_gain, ln_bias, w_qkv, w_attn, w_in, b_in, w_out, b_out, cotangent):
    seq_devices = lax.axis_size("seq")
    windows, local_len, model_width = inputs.shape
    seq_len = local_len * seq_devices
    per_micro = windows // MICRO
    offset = lax.axis_index("seq") * local_len
    cosine, sine_table = rotary_tables(
        (offset + jnp.arange(local_len, dtype=jnp.int32)).astype(jnp.float32)
    )
    full_cosine, full_sine = rotary_tables(jnp.arange(seq_len, dtype=jnp.float32))
    outputs = []
    input_grads = []
    shard_sums = None
    for micro_index in range(MICRO):
        gathered = collect(ln_gain, ln_bias, w_qkv, w_attn, w_in, b_in, w_out, b_out)
        (
            gain_full,
            shift_full,
            qkv_full,
            attn_full,
            in_full,
            bias_in_full,
            out_full,
            bias_out_full,
        ) = gathered
        lower = micro_index * per_micro
        row_values = inputs[lower : lower + per_micro].astype(jnp.float32)
        grad_rows = cotangent[lower : lower + per_micro]
        window_ends = ends[lower : lower + per_micro]
        normed_f, norm_pull = jax.vjp(
            layer_norm, row_values, gain_full.astype(jnp.float32), shift_full.astype(jnp.float32)
        )
        normed = normed_f.astype(jnp.bfloat16)
        projected = jnp.einsum("pld,de->ple", normed, qkv_full, preferred_element_type=jnp.float32)
        arranged = projected.reshape(per_micro, local_len, HEADS, 3, HD)
        query_rot = rotate(arranged[:, :, :, 0], cosine, sine_table)
        key_rot = rotate(arranged[:, :, :, 1], cosine, sine_table)
        packed = jnp.stack([query_rot, key_rot, arranged[:, :, :, 2]], axis=3).astype(jnp.bfloat16)
        packed = packed.reshape(per_micro, local_len, HEADS, 3 * HD)
        head_view = lax.all_to_all(packed, "seq", split_axis=2, concat_axis=1, tiled=True)
        attended, peaks, totals = lax.map(
            lambda bundle: attend_forward(bundle[0], bundle[1]), (head_view, window_ends)
        )
        position_view = lax.all_to_all(
            attended, "seq", split_axis=1, concat_axis=2, tiled=True
        ).reshape(per_micro, local_len, model_width)
        branch_attn = jnp.einsum(
            "ple,ed->pld", position_view, attn_full, preferred_element_type=jnp.float32
        )
        hidden = jnp.einsum(
            "pld,di->pli", normed, in_full, preferred_element_type=jnp.float32
        ) + bias_in_full.astype(jnp.float32)
        activ_f, gelu_pull = jax.vjp(gelu_tanh, hidden)
        activated = activ_f.astype(jnp.bfloat16)
        branch_mlp = jnp.einsum(
            "pli,id->pld", activated, out_full, preferred_element_type=jnp.float32
        ) + bias_out_full.astype(jnp.float32)
        outputs.append((row_values + branch_attn + branch_mlp).astype(jnp.bfloat16))
        grad_b_out = jnp.sum(grad_rows.astype(jnp.float32), axis=(0, 1))
        grad_w_out = jnp.einsum(
            "pli,pld->id", activated, grad_rows, preferred_element_type=jnp.float32
        )
        d_activated = jnp.einsum(
            "pld,id->pli", grad_rows, out_full, preferred_element_type=jnp.float32
        )
        d_hidden = gelu_pull(d_activated)[0].astype(jnp.bfloat16)
        grad_b_in = jnp.sum(d_hidden.astype(jnp.float32), axis=(0, 1))
        grad_w_in = jnp.einsum("pld,pli->di", normed, d_hidden, preferred_element_type=jnp.float32)
        grad_w_attn = jnp.einsum(
            "ple,pld->ed", position_view, grad_rows, preferred_element_type=jnp.float32
        )
        d_attended = jnp.einsum(
            "pld,ed->ple", grad_rows, attn_full, preferred_element_type=jnp.float32
        ).astype(jnp.bfloat16)
        d_attended = d_attended.reshape(per_micro, local_len, HEADS, HD)
        d_head_view = lax.all_to_all(d_attended, "seq", split_axis=2, concat_axis=1, tiled=True)
        d_packed = lax.map(
            lambda bundle: attend_backward(
                bundle[0], bundle[1], bundle[2], bundle[3], bundle[4], full_cosine, full_sine
            ),
            (head_view, d_head_view, peaks, totals, window_ends),
        )
        d_projected = lax.all_to_all(
            d_packed, "seq", split_axis=1, concat_axis=2, tiled=True
        ).reshape(per_micro, local_len, 3 * model_width)
        grad_w_qkv = jnp.einsum(
            "pld,ple->de", normed, d_projected, preferred_element_type=jnp.float32
        )
        d_normed = jnp.einsum("pli,di->pld", d_hidden, in_full, preferred_element_type=jnp.float32)
        d_normed = d_normed + jnp.einsum(
            "ple,de->pld", d_projected, qkv_full, preferred_element_type=jnp.float32
        )
        d_rows, grad_gain, grad_shift = norm_pull(d_normed)
        input_grads.append(grad_rows.astype(jnp.float32) + d_rows)
        local_grads = (
            grad_gain,
            grad_shift,
            grad_w_qkv,
            grad_w_attn,
            grad_w_in,
            grad_b_in,
            grad_w_out,
            grad_b_out,
        )
        reduced = reduce_grads(local_grads)
        if shard_sums is None:
            shard_sums = reduced
        else:
            shard_sums = tuple((running + extra for running, extra in zip(shard_sums, reduced)))
    output = jnp.concatenate(outputs, axis=0)
    grad_inputs = jnp.concatenate(input_grads, axis=0)
    return (
        output,
        grad_inputs,
        shard_sums[0],
        shard_sums[1],
        shard_sums[2],
        shard_sums[3],
        shard_sums[4],
        shard_sums[5],
        shard_sums[6],
        shard_sums[7],
    )


HB, SB = 4, 4
NEG = -1e30
BF, F32 = jnp.bfloat16, jnp.float32
MESH = pl.DeviceIdType.MESH


def dot(a, b, ca, cb):
    return lax.dot_general(a, b, (((ca,), (cb,)), ((), ())), preferred_element_type=F32)


def rows(start, size):
    return pl.ds(pl.multiple_of(start, size), size)


def lanes(start, size=128):
    return pl.ds(pl.multiple_of(start, size), size)


def halves(low_source, high_source):
    def piece(source, upper):
        array, first = source
        tile = array[:, first // 128 * 128 : first // 128 * 128 + 128]
        return pltpu.roll(tile, 64, 1) if (first % 128 == 64) != upper else tile

    lane = lax.broadcasted_iota(jnp.int32, (1, 128), 1)
    return jnp.where(lane < 64, piece(low_source, False), piece(high_source, True))


def head_of(owner, j):
    return 4 * j + 2 * (owner % 2) + owner // 2


class Link:
    def __init__(self, send_sems, recv_sems):
        self.send_sems, self.recv_sems = send_sems, recv_sems
        self.first = {}
        self.used = 0

    def index(self, name, at, count):
        if name not in self.first:
            self.first[name] = self.used
            self.used += count
        return self.first[name] + at

    def copy(self, name, at, count, src, dst, device):
        i = self.index(name, at, count)
        return pltpu.make_async_remote_copy(
            src_ref=src,
            dst_ref=dst,
            send_sem=self.send_sems.at[i],
            recv_sem=self.recv_sems.at[i],
            device_id=device,
            device_id_type=MESH,
        )


def gelu_pair(v):
    square = v * v
    half = 0.5 + 0.5 * jnp.tanh(v * (gelu_factor + (gelu_factor * 0.044715) * square))
    value = v * half
    return value, half + (value - value * half) * (
        2.0 * gelu_factor + (6.0 * gelu_factor * 0.044715) * square
    )


def fused_layer(
    ends, prm, wq, wa, wi, wo, turns, x_in, g_in,
    out_hbm, grad_in_hbm, grad_q_hbm, grad_a_hbm, grad_i_hbm, grad_o_hbm, grad_small_hbm,
    X, N, G, A, H, Wi, Wo, Wq, WaAll, Wa, PWI, PWQ, PRS, PRM, PR, QKV, att, dO,
    GO, XO, ZO, CO, GI, XI, ZI, GQ, XQ, ZQ, GA, XA, ZA, GT, XT, ZT,
    YR, SWI, RWI, SWQ, RWQ, TAIL,
    khat, ktT, vtT, doT, oT, dqT, dkA, dvA,
    grad_in, grad_q, grad_a, grad_small,
    send_sems, recv_sems, local_sems, out_sems,
):
    b = lax.axis_index("batch")
    s = lax.axis_index("seq")
    z, xx = b // 2, b % 2
    y, c = s // 2, s % 2
    oc, ox, oy = 1 - c, 1 - xx, 1 - y
    SL = 256
    S = 1024
    core = (b, 2 * y + oc)
    ypart = (b, 2 * oy + c)
    diag = (b, 2 * oy + oc)
    xpart = (2 * z + ox, s)

    def zdev(k):
        return (2 * ((z + k) % 4) + xx, s)

    def zfrom(k):
        return (z + 4 - k) % 4

    link = Link(send_sems, recv_sems)
    pending = []

    def start(make):
        make().start()
        pending.append(make)

    barrier = pltpu.get_barrier_semaphore()
    others = [xpart] + [zdev(k) for k in (1, 2, 3)]
    others += [(2 * ((z + k) % 4) + ox, s) for k in (1, 2, 3)]
    partners = [core, ypart, diag] + others
    for device in partners:
        pl.semaphore_signal(barrier, inc=1, device_id=device, device_id_type=MESH)

    own = rows(SL * s, SL)
    locals_ = []
    for w in range(2):
        locals_.append(pltpu.make_async_copy(x_in.at[w], X.at[w, own], local_sems.at[3 * w]))
        locals_.append(pltpu.make_async_copy(g_in.at[w], G.at[w, own], local_sems.at[3 * w + 1]))
    for cp in locals_:
        cp.start()

    for r in range(SB):
        for blk in range(8):
            PWI[r, :, 128 * blk : 128 * blk + 128] = wi[:, 512 * blk + 128 * r : 512 * blk + 128 * r + 128]
    tile = prm[...].astype(F32)
    row = lax.broadcasted_iota(jnp.int32, (16, 128), 0)
    tile = jnp.where(row < 3, pltpu.roll(tile, 32 * s, 1), tile)
    PRS[s] = tile.astype(BF)
    Wi[rows(128 * b + 32 * s, 32), :] = PWI[s]
    Wo[rows(128 * b, 128), :] = wo[...]
    WaAll[z, xx] = wa[...]

    wq_f = wq[...].astype(F32)
    for r in range(SB):
        for kind in range(3):
            for p in range(2):
                lo = 192 * head_of(r, 2 * p) + 64 * kind
                hi = 192 * head_of(r, 2 * p + 1) + 64 * kind
                at = 384 * p + 128 * kind
                PWQ[r, :, at : at + 128] = halves((wq_f, lo), (wq_f, hi)).astype(BF)
    Wq[rows(128 * b + 32 * s, 32), :] = PWQ[s]

    pl.semaphore_wait(barrier, len(partners))

    def seq_sends(name, src_of, dst):
        for i, (device, owner) in enumerate(
            ((core, 2 * y + oc), (ypart, 2 * oy + c), (diag, 2 * oy + oc))
        ):
            link.copy(name, i, 3, src_of(owner), dst(), device).start()

    def seq_left(name, src_of, dst):
        for i, (device, owner) in enumerate(
            ((core, 2 * y + oc), (ypart, 2 * oy + c), (diag, 2 * oy + oc))
        ):
            link.copy(name, i, 3, src_of(owner), dst(), device).wait_send()

    def seq_waits(name, src, dst_of):
        for i, owner in enumerate((2 * y + oc, 2 * oy + c, 2 * oy + oc)):
            link.copy(name, i, 3, src, dst_of(owner), core).wait_recv()

    def prm_block(owner):
        return PRS.at[owner]

    def wi_block(owner, u):
        return Wi.at[rows(128 * b + 32 * owner, 32), 256 * u : 256 * u + 256]

    def wq_block(owner):
        return Wq.at[rows(128 * b + 32 * owner, 32)]

    gathers = {
        "wi": (4, lambda bb, u: Wi.at[rows(128 * bb, 128), lanes(256 * u, 256)]),
        "wo": (2, lambda bb, u: Wo.at[rows(128 * bb + 64 * u, 64)]),
        "wq": (2, lambda bb, u: Wq.at[rows(128 * bb, 128), 384 * u : 384 * u + 384]),
        "wa": (1, lambda bb, u: WaAll.at[bb // 2, bb % 2]),
    }
    pair = z + 1 - 2 * (z % 2)

    def gather_copy(name, way, at, count, zz, side, u, device):
        held = gathers[name][1](2 * zz + side, u)
        return link.copy(name + way, count * u + at, count * gathers[name][0], held, held, device)

    def up_copy(name, zz, u):
        return gather_copy(name, "l", zz, 5, zz, xx, u, (2 * (z + 1) + xx, s))

    def down_copy(name, zz, u):
        return gather_copy(name, "l", zz + 1, 5, zz, xx, u, (2 * (z - 1) + xx, s))

    def z_copy(name, zz, k, u):
        return gather_copy(name, "z", k - 1, 3, zz, xx, u, zdev(k))

    def x_copy(name, zz, side, u):
        return gather_copy(name, "x", zz, 4, zz, side, u, xpart)

    def pair_copy(name, zz, u):
        return gather_copy(name, "p", 0, 1, zz, ox, u, (2 * pair + xx, s))

    def by_pair(name, u):
        return name in ("wi", "wo") and 2 * u >= gathers[name][0]

    def gather_z(name, u):
        if name == "wi":

            @pl.when(z < 3)
            def _():
                up_copy(name, z, u).start()

            @pl.when(z > 0)
            def _():
                down_copy(name, z, u).start()

            return
        for far in (1, 2, 3):

            @pl.when(z + far <= 3)
            def _():
                z_copy(name, z, far, u).start()

            @pl.when(z >= far)
            def _():
                z_copy(name, z, 4 - far, u).start()

    def gather_x(name, u):
        x_copy(name, z, xx, u).start()

    def hand_over(name, zz, u):
        if by_pair(name, u):

            @pl.when(zz != pair)
            def _():
                x_copy(name, zz, xx, u).start()

        else:
            x_copy(name, zz, xx, u).start()

    def gather_pass(name, far, u):
        @pl.when(z >= far)
        def _():
            if name == "wi":
                up_copy(name, z - far, u).wait_recv()

                @pl.when(z < 3)
                def _():
                    up_copy(name, z - far, u).start()

            else:
                z_copy(name, z - far, far, u).wait_recv()
            hand_over(name, z - far, u)

        @pl.when(z + far <= 3)
        def _():
            if name == "wi":
                down_copy(name, z + far, u).wait_recv()

                @pl.when(z > 0)
                def _():
                    down_copy(name, z + far, u).start()

            else:
                z_copy(name, z + far, 4 - far, u).wait_recv()
            hand_over(name, z + far, u)

    def gather_pair(name, u):
        x_copy(name, z, ox, u).wait_recv()
        pair_copy(name, z, u).start()

    def gather_block(name, zz, u):
        if by_pair(name, u):

            @pl.when((zz != pair) & (zz != z))
            def _():
                x_copy(name, zz, ox, u).wait_recv()

            @pl.when(zz == pair)
            def _():
                pair_copy(name, pair, u).wait_recv()

        else:
            x_copy(name, zz, ox, u).wait_recv()

    def gather_end(name, u):
        for zz in range(4):
            gather_block(name, zz, u)

    def gather_left(name, u):
        if name != "wi":
            for k in (1, 2, 3):
                z_copy(name, z, k, u).wait_send()
        for zz in range(4):
            if name == "wi":

                @pl.when((zz <= z) & (z < 3))
                def _():
                    up_copy(name, zz, u).wait_send()

                @pl.when((zz >= z) & (z > 0))
                def _():
                    down_copy(name, zz, u).wait_send()

            if by_pair(name, u):

                @pl.when(zz != pair)
                def _():
                    x_copy(name, zz, xx, u).wait_send()

            else:
                x_copy(name, zz, xx, u).wait_send()

        if by_pair(name, u):
            pair_copy(name, z, u).wait_send()

    def rows_start(name, src, dst):
        for w in range(2):
            start(lambda w=w: link.copy(name + "c", w, 2, src.at[w], dst.at[w, own], core))
            start(lambda w=w: link.copy(name + "y", w, 2, src.at[w], dst.at[w, own], ypart))

    def rows_pass(name, dst, w):
        block = dst.at[w, rows(SL * (2 * oy + c), SL)]
        link.copy(name + "y", w, 2, block, block, core).wait_recv()
        link.copy(name + "f", w, 2, block, block, core).start()

    def rows_left(name, dst, w):
        block = dst.at[w, rows(SL * (2 * oy + c), SL)]
        link.copy(name + "f", w, 2, block, block, core).wait_send()

    def rows_end_core(name, dst, w):
        block = dst.at[w, rows(SL * (2 * y + oc), SL)]
        link.copy(name + "c", w, 2, block, block, core).wait_recv()

    def rows_end_far(name, dst, w):
        block = dst.at[w, rows(SL * (2 * oy + oc), SL)]
        link.copy(name + "f", w, 2, block, block, core).wait_recv()

    seq_sends("prms", lambda owner: prm_block(s), lambda: prm_block(s))
    for u in range(4):
        seq_sends(
            "wis%d" % u, lambda owner: PWI.at[owner, :, 256 * u : 256 * u + 256], lambda: wi_block(s, u)
        )
    gather_z("wa", 0)
    gather_x("wa", 0)
    gather_x("wo", 0)
    seq_sends("wqs", lambda owner: PWQ.at[owner], lambda: wq_block(s))
    rows_start("x", x_in, X)
    seq_waits("prms", prm_block(s), prm_block)
    total = PRS[0].astype(F32) + PRS[1].astype(F32) + PRS[2].astype(F32) + PRS[3].astype(F32)
    PRM[b] = jnp.where(row < 3, total, tile).astype(BF)
    for i, device in enumerate(others):
        start(lambda i=i, device=device: link.copy("prm", i, 7, PRM.at[b], PRM.at[b], device))
    for u in range(4):
        seq_waits("wis%d" % u, wi_block(s, u), lambda owner: wi_block(owner, u))
        gather_z("wi", u)
        gather_x("wi", u)
    rows_start("g", g_in, G)
    gather_pass("wi", 1, 0)
    gather_pass("wi", 1, 1)
    for far in (1, 2, 3):
        gather_pass("wa", far, 0)

    for i in range(7):
        k = (0, 1, 2, 3, 1, 2, 3)[i]
        bb = 2 * zfrom(k) + (ox if i in (0, 4, 5, 6) else xx)
        link.copy("prm", i, 7, PRM.at[bb], PRM.at[bb], core).wait_recv()
    for bb in range(8):
        PR[:, 128 * bb : 128 * bb + 128] = PRM[bb].astype(F32)[0:8]

    for cp in locals_:
        cp.wait()

    def norm_rows(w, owner):
        r = rows(SL * owner, SL)
        v = X[w, r, :].astype(F32)
        v = v - jnp.mean(v, axis=-1, keepdims=True)
        var = jnp.mean(v * v, axis=-1, keepdims=True)
        N[w, r, :] = (v * lax.rsqrt(var + norm_eps) * PR[0:1, :] + PR[1:2, :]).astype(BF)

    def norm_near(w, carry):
        norm_rows(w, s)
        norm_rows(w, 2 * y + oc)
        return carry

    def norm_far(w):
        rows_end_far("x", X, w)
        norm_rows(w, 2 * oy + c)
        norm_rows(w, 2 * oy + oc)

    for w in range(2):
        rows_end_core("x", X, w)
    lax.fori_loop(0, 2, norm_near, 0)
    gather_pass("wi", 2, 0)
    gather_pass("wi", 1, 2)
    gather_pass("wi", 1, 3)
    gather_pass("wi", 2, 1)
    gather_pass("wi", 3, 0)
    gather_pass("wi", 2, 2)
    gather_pair("wi", 2)
    gather_pass("wi", 3, 1)
    rows_pass("x", X, 0)
    gather_pass("wi", 2, 3)
    gather_pair("wi", 3)
    seq_waits("wqs", wq_block(s), wq_block)
    gather_z("wq", 0)

    def hidden_step(i, carry):
        early = i < 12
        u = jnp.where(early, i // 3, i - 12)
        at = jnp.where(early, i % 3, 3)
        w = at % 2
        t = jnp.where(at < 2, y, oy)

        @pl.when(i == 0)
        def _():
            gather_end("wi", 0)

        @pl.when(i == 2)
        def _():
            norm_far(0)

        @pl.when(i == 3)
        def _():
            gather_pass("wi", 3, 2)
            gather_x("wq", 0)
            gather_end("wi", 1)

        @pl.when(i == 5)
        def _():
            gather_pass("wi", 3, 3)
            gather_z("wq", 1)

        @pl.when(i == 6)
        def _():
            gather_end("wi", 2)

        @pl.when(i == 7)
        def _():
            rows_pass("x", X, 1)

        @pl.when(i == 9)
        def _():
            gather_pass("wq", 1, 0)
            gather_end("wi", 3)

        @pl.when(i == 12)
        def _():
            gather_pass("wq", 2, 0)
            gather_pass("wq", 3, 0)
            gather_x("wq", 1)
            norm_far(1)

        r, l = rows(512 * t, 512), lanes(256 * u, 256)
        v = dot(N[w, r, :], Wi[:, l], 1, 0) + PR[3:4, l]
        value, slope = gelu_pair(v)
        A[w, r, l] = value.astype(BF)
        H[w, r, l] = slope.astype(BF)
        return carry

    lax.fori_loop(0, 16, hidden_step, 0)
    for u in range(2):
        gather_z("wo", u)
    for w in range(2):
        rows_left("x", X, w)
    gather_end("wa", 0)
    start(lambda: link.copy("wac", 0, 1, WaAll.at[:, oc], Wa.at[:, c], core))
    Wa[:, c] = WaAll[:, c]
    for far in (1, 2, 3):
        gather_pass("wq", far, 1)
    gather_x("wo", 1)

    def add_into(dst, other):
        dst[...] = (dst[...].astype(F32) + other[...].astype(F32)).astype(BF)

    inner = (z == 1) | (z == 2)

    def far_chip(tt):
        return 2 * (1 - z // 2) + tt

    def zchip(zz):
        return (2 * zz + xx, s)

    def o_near(q):
        return link.copy("op", 0, 1, GO.at[q, xx], ZO.at[0], zchip(pair))

    def o_comb(q):
        return link.copy("oc", q % 2, 2, GO.at[q, xx], CO.at[q % 2], zchip(pair))

    def o_far(q):
        return link.copy("of", q % 2, 2, GO.at[q, xx], ZO.at[1], zchip(q))

    def i_z(q, k):
        return link.copy("iz", 3 * q + k - 1, 12, GI.at[q, xx, (z + k) % 4], ZI.at[k - 1, q], zdev(k))

    def first_z(q):
        link.copy("ox", q, 4, XO.at[q], XO.at[q], core).wait_recv()

        @pl.when(z != q)
        def _():
            add_into(GO.at[q, xx], XO.at[q])

            @pl.when(q == pair)
            def _():
                o_near(q).start()

            @pl.when((q != pair) & ~inner)
            def _():
                o_comb(q).start()

        link.copy("ix", q, 4, XI.at[q], XI.at[q], core).wait_recv()
        for k in (1, 2, 3):
            zz = (z + k) % 4
            add_into(GI.at[q, xx, zz], XI.at[q, zz])
            i_z(q, k).start()

    def second_z(q):
        @pl.when(inner)
        def _():
            o_comb(q).wait_recv()
            add_into(GO.at[q, xx], CO.at[q % 2])
            o_far(q).start()

    def z_left():
        o_near(pair).wait_send()
        for tt in range(2):

            @pl.when(inner)
            def _():
                o_far(far_chip(tt)).wait_send()

            @pl.when(~inner)
            def _():
                o_comb(far_chip(tt)).wait_send()

        for q in range(4):
            for k in (1, 2, 3):
                i_z(q, k).wait_send()

    def chunk(j):
        return jnp.where(j == 0, z, jnp.where(j == 3, pair, far_chip(0) + j - 1))

    def send_x(q):
        link.copy("ox", q, 4, GO.at[q, ox], XO.at[q], xpart).start()
        link.copy("ix", q, 4, GI.at[q, ox], XI.at[q], xpart).start()

    even = lax.broadcasted_iota(jnp.int32, (1, 128), 1) % 2 == 0

    def turn_rows(r):
        table = turns[r, :]
        other = pltpu.roll(table, 64, 1)
        low = lax.broadcasted_iota(jnp.int32, (1, 128), 1) < 64
        return jnp.where(low, table, other), jnp.where(low, other, table)

    def turn(v, cos_rows, sin_rows):
        swapped = jnp.where(even, pltpu.roll(v, 127, 1), pltpu.roll(v, 1, 1))
        return v * cos_rows + swapped * sin_rows

    def qkv_step(p):
        gather_end("wq", p)
        l = slice(384 * p, 384 * p + 384)

        def step(i, carry):
            w, r = i // 4, rows(256 * (i % 4), 256)
            v = dot(N[w, r, :], Wq[:, l], 1, 0)
            cos_rows, sin_rows = turn_rows(r)
            for kind in range(3):
                tile_v = v[:, 128 * kind : 128 * kind + 128]
                if kind < 2:
                    tile_v = turn(tile_v, cos_rows, sin_rows)
                if kind == 0:
                    tile_v = tile_v * 0.125
                QKV[w, r, 384 * p + 128 * kind : 384 * p + 128 * kind + 128] = tile_v.astype(BF)
            return carry

        lax.fori_loop(0, 8, step, 0)

    qkv_step(0)
    for w in range(2):
        rows_end_core("g", G, w)
    rows_pass("g", G, 0)
    for u in range(4):
        seq_left(
            "wis%d" % u, lambda owner: PWI.at[owner, :, 256 * u : 256 * u + 256], lambda: wi_block(s, u)
        )
    link.copy("wac", 0, 1, WaAll.at[:, oc], Wa.at[:, oc], core).wait_recv()
    TAIL[...] = jnp.zeros_like(TAIL)

    def do_step(w):
        def step(i, total):
            r = rows(512 * i, 512)
            g = G[w, r, :]
            dO[w, r, :] = dot(g, Wa[...].reshape(256, 1024), 1, 1).astype(BF)
            return total + jnp.sum(g.astype(F32), axis=0, keepdims=True)

        TAIL[2:3, :] += lax.fori_loop(0, 2, step, jnp.zeros((1, 1024), F32))

    rows_end_far("g", G, 0)
    do_step(0)

    def back_step(j, carry):
        q = chunk(j)
        l = lanes(256 * q, 256)
        gather_block("wo", q, 0)
        gather_block("wo", q, 1)

        def dh_step(i, total):
            w, r = i // 2, rows(512 * (i % 2), 512)
            d = dot(G[w, r, :], Wo[rows(256 * q, 256), :], 1, 1) * H[w, r, l].astype(F32)
            d = d.astype(BF)
            H[w, r, l] = d
            return total + jnp.sum(d.astype(F32), axis=0, keepdims=True)

        TAIL[3:4, l] = lax.fori_loop(0, 4, dh_step, jnp.zeros((1, 256), F32))
        go = dot(A[0, :, l], G[0], 0, 0) + dot(A[1, :, l], G[1], 0, 0)
        GO[q, 0] = go[:128].astype(BF)
        GO[q, 1] = go[128:].astype(BF)
        gi = dot(H[0, :, l], N[0], 0, 0) + dot(H[1, :, l], N[1], 0, 0)
        for bb in range(8):
            GI[q, bb % 2, bb // 2] = gi[:, 128 * bb : 128 * bb + 128].astype(BF)

        send_x(q)

        return carry

    lane = lax.broadcasted_iota(jnp.int32, (1, 128), 1)
    place = lax.broadcasted_iota(jnp.int32, (S, 1), 0)
    BQ = 256
    key_i = lax.broadcasted_iota(jnp.int32, (BQ, BQ), 0)
    query_i = lax.broadcasted_iota(jnp.int32, (BQ, BQ), 1)
    inside = [(lane // 64) == hh for hh in range(2)]
    feature = [lane == (64 - 64 * hh) for hh in range(2)]

    def attend(w, p):
        ending = ends[w]

        def part(kind):
            return lanes(384 * p + 128 * kind)

        pl_ = lanes(128 * p)
        keys = QKV[w, :, part(1)]
        ktT[...] = keys.T
        vtT[...] = QKV[w, :, part(2)].T
        doT[...] = dO[w, :, pl_].T
        dkA[...] = jnp.zeros_like(dkA)
        dvA[...] = jnp.zeros_like(dvA)
        keys_f = keys.astype(F32)
        before = jnp.where(place < ending, NEG, 0.0)
        for hh in range(2):
            khat[hh] = jnp.where(inside[hh], keys_f, jnp.where(feature[hh], before, 0.0)).astype(BF)

        def begin(qb, hh):
            qr, nk = slice(qb * BQ, (qb + 1) * BQ), (qb + 1) * BQ
            q = QKV[w, qr, part(0)].astype(F32)
            after = jnp.where(place[qr] >= ending, 1.0, 0.0)
            q_in = jnp.where(inside[hh], q, 0.0).astype(BF)
            q_hat = jnp.where(inside[hh], q, jnp.where(feature[hh], after, 0.0)).astype(BF)
            d_in = jnp.where(inside[hh], dO[w, qr, pl_].astype(F32), 0.0).astype(BF)
            return dot(khat[hh, 0:nk, :], q_hat, 1, 1), dot(QKV[w, 0:nk, part(2)], d_in, 1, 1), q_in, d_in

        units = [(qb, hh) for qb in range(S // BQ) for hh in range(2)]
        upcoming, late = begin(*units[0]), None
        for i, (qb, hh) in enumerate(units):
            sc, dp, q_in, d_in = upcoming
            qr, nk = slice(qb * BQ, (qb + 1) * BQ), (qb + 1) * BQ
            hr = slice(64 * hh, 64 * hh + 64)
            if i + 1 < len(units):
                upcoming = begin(*units[i + 1])
            last = jnp.where(key_i <= query_i, sc[nk - BQ :], NEG)
            sc = last if qb == 0 else jnp.concatenate([sc[: nk - BQ], last], axis=0)
            e = jnp.exp(sc - jnp.max(sc, axis=0, keepdims=True))
            pn = e * (1.0 / jnp.sum(e, axis=0, keepdims=True))
            pb = pn.astype(BF)
            o = dot(vtT[hr, 0:nk], pb, 1, 0)
            if late is not None:
                late()
            oT[hr, qr] = o
            dd = jnp.sum(o * doT[hr, qr].astype(F32), axis=0, keepdims=True)
            ds = (pn * (dp - dd)).astype(BF)

            def late(hr=hr, qr=qr, nk=nk, ds=ds, pb=pb, q_in=q_in, d_in=d_in):
                dqT[hr, qr] = dot(ktT[hr, 0:nk], ds, 1, 0)
                dkA[0:nk, :] += dot(ds, q_in, 1, 0)
                dvA[0:nk, :] += dot(pb, d_in, 1, 0)

        late()
        cos_rows, sin_rows = turn_rows(slice(None))
        sin_rows = -sin_rows
        att[w, :, pl_] = oT[...].T.astype(BF)
        QKV[w, :, part(0)] = turn(dqT[...].T * 0.125, cos_rows, sin_rows).astype(BF)
        QKV[w, :, part(1)] = turn(dkA[...], cos_rows, sin_rows).astype(BF)
        QKV[w, :, part(2)] = dvA[...].astype(BF)

    shares = (A, H)

    def share_c(w, yy):
        for t in range(2):
            src = shares[t].at[w, rows(SL * (2 * yy + oc), SL)]
            dst = X.at[w, rows(SL * (2 * t + yy), SL)]
            link.copy("sc", 4 * w + 2 * t + yy, 8, src, dst, core).start()

    def share_got(w, t, yy):
        slot = X.at[w, rows(SL * (2 * t + yy), SL)]
        link.copy("sc", 4 * w + 2 * t + yy, 8, slot, slot, core).wait_recv()
        return slot

    def share_y(w):
        for t in (1, 0):
            src = shares[t].at[w, rows(SL * (2 * oy + c), SL)]
            add_into(src, share_got(w, t, oy))
            link.copy("sy", 2 * w + t, 4, src, YR.at[w, t], ypart).start()

    def share_step(w, hooks=()):
        def step(i, carry):
            yy = jnp.where(i < 2, oy, y)
            cc = jnp.where(i % 2 == 0, oc, c)
            r = rows(SL * (2 * yy + cc), SL)
            value = dot(A[w, r, :], Wo[...], 1, 0) + dot(att[w, r, :], Wa[...].reshape(256, 1024), 1, 0)
            A[w, r, :] = value.astype(BF)
            d = dot(H[w, r, :], Wi[...], 1, 1) + dot(QKV[w, r, :], Wq[...], 1, 1)
            H[w, r, :] = d.astype(BF)
            n = (N[w, r, :].astype(F32) - PR[1:2, :]) / PR[0:1, :]
            TAIL[0:1, :] += jnp.sum(d, axis=0, keepdims=True)
            TAIL[1:2, :] += jnp.sum(d * n, axis=0, keepdims=True)

            @pl.when(i == 0)
            def _():
                share_c(w, oy)

            @pl.when(i == 2)
            def _():
                share_y(w)
                share_c(w, y)

            for at, hook in hooks:
                pl.when(i == at)(hook)

            return carry

        lax.fori_loop(0, 4, step, 0)

    def gq_step(p):
        for kind in range(3):
            e = 3 * p + kind
            l = slice(128 * e, 128 * e + 128)
            gq = dot(QKV[0, :, l], N[0], 0, 0) + dot(QKV[1, :, l], N[1], 0, 0)
            for bb in range(8):
                GQ[e, bb % 2, bb // 2] = gq[:, 128 * bb : 128 * bb + 128].astype(BF)
            link.copy("qx", e, 6, GQ.at[e, ox], XQ.at[e], xpart).start()

    def ga_c(p):
        two = slice(2 * p, 2 * p + 2)
        return link.copy("ac", p, 2, PWI.at[two], GA.at[c, two], core)

    def ga_x(p):
        two = slice(2 * p, 2 * p + 2)
        return link.copy("ax", p, 2, GA.at[ox, two], XA.at[two], xpart)

    def ga_step(p):
        l = slice(128 * p, 128 * p + 128)
        ga = dot(att[0, :, l], G[0], 0, 0) + dot(att[1, :, l], G[1], 0, 0)
        for j in range(2):
            for cc in range(2):
                piece = ga[64 * j + 32 * cc : 64 * j + 32 * cc + 32].astype(BF)

                @pl.when(cc == c)
                def _():
                    GA[c, 2 * p + j] = piece

                @pl.when(cc != c)
                def _():
                    PWI[2 * p + j] = piece

        ga_c(p).start()

    def ga_send(p):
        ga_c(p).wait_recv()
        ga_x(p).start()

    def z_step(name, group, received, landed, at=0, count=1, waits=None):
        if waits is None:
            link.copy(name + "x", at, count, received, received, core).wait_recv()
        else:
            waits()
        for k in (1, 2, 3):
            zz = (z + k) % 4
            add_into(group.at[xx, zz], received.at[zz])
            start(
                lambda k=k: link.copy(
                    name + "z",
                    3 * at + k - 1,
                    3 * count,
                    group.at[xx, (z + k) % 4],
                    landed.at[k - 1],
                    zdev(k),
                )
            )

    def of_piece(e):
        return "q", GQ.at[e], XQ.at[e], ZQ.at[e], e, 6

    def attend_step(i, carry):
        w, p = i // 2, i % 2

        @pl.when(i == 1)
        def _():
            qkv_step(1)

        @pl.when(i == 2)
        def _():
            do_step(1)

        attend(w, p)

        @pl.when(i == 0)
        def _():
            rows_pass("g", G, 1)
            gather_pass("wo", 1, 0)
            gather_pass("wo", 1, 1)

        @pl.when(i == 1)
        def _():
            rows_end_far("g", G, 1)
            gather_pair("wo", 1)
            for far in (2, 3):
                for u in range(2):
                    gather_pass("wo", far, u)
            lax.fori_loop(0, 4, back_step, 0)
            first_z(chunk(0))
            share_step(0)
            first_z(chunk(1))

        @pl.when(i == 2)
        def _():
            gq_step(0)
            ga_step(0)
            second_z(chunk(1))
            first_z(chunk(2))
            ga_send(0)

        @pl.when(i == 3)
        def _():
            gq_step(1)
            ga_step(1)
            second_z(chunk(2))
            ga_send(1)
            share_step(1, hooks=[(0, lambda: first_z(chunk(3)))])

        return carry

    lax.fori_loop(0, 4, attend_step, 0)
    for e in range(3):
        z_step(*of_piece(e))
    again = [
        pltpu.make_async_copy(x_in.at[w], N.at[w, 0:SL], local_sems.at[3 * w + 2]) for w in range(2)
    ]
    for cp in again:
        cp.start()
    tail = TAIL[...]
    for bb in range(8):
        GT[bb % 2, bb // 2] = tail[:, 128 * bb : 128 * bb + 128].astype(BF)
    start(lambda: link.copy("tx", 0, 1, GT.at[ox], XT, xpart))

    written = []

    def write(src, dst):
        cp = pltpu.make_async_copy(src, dst, out_sems.at[len(written)])
        cp.start()
        written.append(cp)
        return cp

    def final_o():
        o_near(z).wait_recv()
        link.copy("of", z % 2, 2, ZO.at[1], ZO.at[1], core).wait_recv()
        dqT[...] = (
            GO[z, xx].astype(F32) + XO[z].astype(F32) + ZO[0].astype(F32) + ZO[1].astype(F32)
        )

    def final_i():
        for q in range(4):
            total = GI[q, xx, z].astype(F32) + XI[q, z].astype(F32)
            for k in (1, 2, 3):
                i_z(q, k).wait_recv()
                total = total + ZI[k - 1, q].astype(F32)
            turned = total.T.astype(BF)
            for owner in range(4):
                SWI[owner, :, 256 * q : 256 * q + 256] = turned[32 * owner : 32 * owner + 32]

    def z_total(name, group, received, landed, at=0, count=1):
        for k in (1, 2, 3):
            link.copy(
                name + "z", 3 * at + k - 1, 3 * count, landed.at[k - 1], landed.at[k - 1], core
            ).wait_recv()
        total = group[xx, z].astype(F32) + received[z].astype(F32)
        for k in range(3):
            total = total + landed[k].astype(F32)
        return total

    for e in range(3, 6):
        z_step(*of_piece(e))
    z_step("t", GT, XT, ZT)
    ga_x(0).wait_recv()
    z_step("a", GA, XA, ZA, waits=lambda: ga_x(1).wait_recv())
    final_o()
    write(dqT, grad_o_hbm)
    final_i()
    RWI[s] = SWI[s]
    seq_sends("swi", lambda owner: SWI.at[owner], lambda: RWI.at[s])


    def final_rows(w, carry):
        again[w].wait()
        v = N[w, 0:SL, :].astype(F32)
        mine = rows(SL * s, SL)
        for t in (1, 0):
            share_got(w, t, y)
            link.copy("sy", 2 * w + t, 4, YR.at[w, t], YR.at[w, t], core).wait_recv()
        value = (
            A[w, mine, :].astype(F32)
            + X[w, rows(SL * y, SL), :].astype(F32)
            + YR[w, 0].astype(F32)
        )
        A[w, mine, :] = (v + value + PR[2:3, :]).astype(BF)
        d = (
            H[w, mine, :].astype(F32)
            + X[w, rows(SL * (2 + y), SL), :].astype(F32)
            + YR[w, 1].astype(F32)
        )
        v = v - jnp.mean(v, axis=-1, keepdims=True)
        scale = lax.rsqrt(jnp.mean(v * v, axis=-1, keepdims=True) + norm_eps)
        v = v * scale
        d = d * PR[0:1, :]
        d = d - jnp.mean(d, axis=-1, keepdims=True) - v * jnp.mean(d * v, axis=-1, keepdims=True)
        grad_in[...] = G[w, mine, :].astype(F32) + scale * d
        return carry

    final_rows(0, 0)
    write(A.at[0, own], out_hbm.at[0])
    first_rows = write(grad_in, grad_in_hbm.at[0])

    for e in range(6):
        total_q = z_total(*of_piece(e)).T.astype(BF)
        for owner in range(4):
            SWQ[owner, :, 128 * e : 128 * e + 128] = total_q[32 * owner : 32 * owner + 32]
    total_t = z_total("t", GT, XT, ZT)
    turned_t = jnp.concatenate([total_t, jnp.zeros((112, 128), F32)], axis=0).T.astype(BF)
    for owner in range(4):
        SWQ[owner, :, 768:896] = turned_t[32 * owner : 32 * owner + 32]
    RWQ[s] = SWQ[s]
    seq_sends("swq", lambda owner: SWQ.at[owner], lambda: RWQ.at[s])
    grad_a[...] = z_total("a", GA, XA, ZA)
    write(grad_a, grad_a_hbm)

    def from_seq(name, landed):
        for i, owner in enumerate((2 * y + oc, 2 * oy + c, 2 * oy + oc)):
            link.copy(name, i, 3, landed.at[owner], landed.at[owner], core).wait_recv()

    from_seq("swi", RWI)
    for r in range(4):
        for blk in range(8):
            at = 512 * blk + 128 * r
            oT[32 * (at // 1024) : 32 * (at // 1024) + 32, at % 1024 : at % 1024 + 128] = RWI[
                r, :, 128 * blk : 128 * blk + 128
            ].astype(F32)

    for q in range(4):
        write(oT.at[32 * q : 32 * q + 32], grad_i_hbm.at[:, 1024 * q : 1024 * q + 1024])
    first_rows.wait()
    final_rows(1, 0)
    write(A.at[1, own], out_hbm.at[1])
    write(grad_in, grad_in_hbm.at[1])

    from_seq("swq", RWQ)
    got = [RWQ[r].astype(F32) for r in range(4)]
    place_of = {}
    for r in range(4):
        for j in range(4):
            for kind in range(3):
                place_of[3 * head_of(r, j) + kind] = (got[r], 384 * (j // 2) + 128 * kind + 64 * (j % 2))
    for at in range(24):
        grad_q[:, 128 * at : 128 * at + 128] = halves(place_of[2 * at], place_of[2 * at + 1])
    write(grad_q, grad_q_hbm)
    summed = got[0][:, 768:896] + got[1][:, 768:896] + got[2][:, 768:896] + got[3][:, 768:896]
    summed = jnp.where(lane == 2, got[0][:, 768:896], summed)
    summed = jnp.concatenate([summed, jnp.zeros((96, 128), F32)], axis=0).T
    grad_small[...] = jnp.where(lax.broadcasted_iota(jnp.int32, (8, 128), 0) < 3, summed[0:8], total_t[0:8])
    write(grad_small, grad_small_hbm)

    for make in pending:
        make().wait_send()
    seq_left("prms", lambda owner: prm_block(s), lambda: prm_block(s))
    seq_left("wqs", lambda owner: PWQ.at[owner], lambda: wq_block(s))
    seq_left("swi", lambda owner: SWI.at[owner], lambda: RWI.at[s])
    seq_left("swq", lambda owner: SWQ.at[owner], lambda: RWQ.at[s])
    for name, (parts, _) in gathers.items():
        for u in range(parts):
            gather_left(name, u)
    for w in range(2):
        rows_left("g", G, w)
    for q in range(4):
        link.copy("ox", q, 4, GO.at[q, ox], XO.at[q], xpart).wait_send()
        link.copy("ix", q, 4, GI.at[q, ox], XI.at[q], xpart).wait_send()
    z_left()
    for w in range(2):
        for t in range(2):
            for yy in range(2):
                src = shares[t].at[w, rows(SL * (2 * yy + oc), SL)]
                dst = X.at[w, rows(SL * (2 * t + yy), SL)]
                link.copy("sc", 4 * w + 2 * t + yy, 8, src, dst, core).wait_send()
            src = shares[t].at[w, rows(SL * (2 * oy + c), SL)]
            link.copy("sy", 2 * w + t, 4, src, YR.at[w, t], ypart).wait_send()
    for e in range(6):
        link.copy("qx", e, 6, GQ.at[e, ox], XQ.at[e], xpart).wait_send()
    for p in range(2):
        ga_c(p).wait_send()
        ga_x(p).wait_send()
    for cp in written:
        if cp is not first_rows:
            cp.wait()


def publish(*refs):
    sources, small, targets, row_targets = refs[:6], refs[6], refs[7:13], refs[13:17]
    held, (in_sems, out_sems) = refs[17:23], refs[23:]
    arrive = [
        pltpu.make_async_copy(sources[i], held[i], in_sems.at[i]) for i in range(6)
    ]
    leave = [
        pltpu.make_async_copy(held[i], targets[i], out_sems.at[i]) for i in range(6)
    ]
    for cp in arrive:
        cp.start()
    for i, target in enumerate(row_targets):
        target[...] = small[i : i + 1, 0 : target.shape[1]]
    for i in range(6):
        arrive[i].wait()
        leave[i].start()
    for cp in leave:
        cp.wait()


def turn_tables(seq_len):
    inverse = 10000.0 ** (-2.0 * np.arange(ROTARY // 2) / ROTARY)
    angles = np.arange(seq_len)[:, None] * inverse[None, :]
    cosine = np.ones((seq_len, HD), np.float32)
    sine = np.zeros((seq_len, HD), np.float32)
    cosine[:, 0:ROTARY:2] = cosine[:, 1:ROTARY:2] = np.cos(angles)
    sine[:, 0:ROTARY:2] = -np.sin(angles)
    sine[:, 1:ROTARY:2] = np.sin(angles)
    return np.concatenate([cosine, sine], axis=1)


def fused_shards(inputs, ends, ln_gain, ln_bias, w_qkv, w_attn, w_in, b_in, w_out, b_out, cotangent):
    def widen(v):
        return jnp.pad(v, (0, 128 - v.shape[0]))

    prm = jnp.pad(jnp.stack([widen(ln_gain), widen(ln_bias), widen(b_out), b_in]), ((0, 12), (0, 0)))
    in_vmem = pl.BlockSpec(memory_space=pltpu.VMEM)
    in_any = pl.BlockSpec(memory_space=pl.ANY)
    rows_type = (2, 1024, 1024)
    shapes = (
        jax.ShapeDtypeStruct((2, 256, 1024), BF),
        jax.ShapeDtypeStruct((2, 256, 1024), F32),
        jax.ShapeDtypeStruct((32, 3072), F32),
        jax.ShapeDtypeStruct((32, 1024), F32),
        jax.ShapeDtypeStruct((32, 4096), F32),
        jax.ShapeDtypeStruct((128, 1024), F32),
    )
    results = pl.pallas_call(
        fused_layer,
        out_shape=shapes + (jax.ShapeDtypeStruct((8, 128), F32),),
        in_specs=[pl.BlockSpec(memory_space=pltpu.SMEM)] + [in_vmem] * 6 + [in_any] * 2,
        out_specs=(in_any,) * 7,
        scratch_shapes=[
            pltpu.VMEM(rows_type, BF),
            pltpu.VMEM(rows_type, BF),
            pltpu.VMEM(rows_type, BF),
            pltpu.VMEM(rows_type, BF),
            pltpu.VMEM(rows_type, BF),
            pltpu.VMEM((1024, 1024), BF),
            pltpu.VMEM((1024, 1024), BF),
            pltpu.VMEM((1024, 768), BF),
            pltpu.VMEM((4, 2, 32, 1024), BF),
            pltpu.VMEM((4, 2, 32, 1024), BF),
            pltpu.VMEM((4, 32, 1024), BF),
            pltpu.VMEM((4, 32, 768), BF),
            pltpu.VMEM((4, 16, 128), BF),
            pltpu.VMEM((8, 16, 128), BF),
            pltpu.VMEM((8, 1024), F32),
            pltpu.VMEM((2, 1024, 768), BF),
            pltpu.VMEM((2, 1024, 256), BF),
            pltpu.VMEM((2, 1024, 256), BF),
            pltpu.VMEM((4, 2, 128, 1024), BF),
            pltpu.VMEM((4, 128, 1024), BF),
            pltpu.VMEM((2, 128, 1024), BF),
            pltpu.VMEM((2, 128, 1024), BF),
            pltpu.VMEM((4, 2, 4, 256, 128), BF),
            pltpu.VMEM((4, 4, 256, 128), BF),
            pltpu.VMEM((3, 4, 256, 128), BF),
            pltpu.VMEM((6, 2, 4, 128, 128), BF),
            pltpu.VMEM((6, 4, 128, 128), BF),
            pltpu.VMEM((6, 3, 128, 128), BF),
            pltpu.VMEM((2, 4, 32, 1024), BF),
            pltpu.VMEM((4, 32, 1024), BF),
            pltpu.VMEM((3, 32, 1024), BF),
            pltpu.VMEM((2, 4, 16, 128), BF),
            pltpu.VMEM((4, 16, 128), BF),
            pltpu.VMEM((3, 16, 128), BF),
            pltpu.VMEM((2, 2, 256, 1024), BF),
            pltpu.VMEM((4, 32, 1024), BF),
            pltpu.VMEM((4, 32, 1024), BF),
            pltpu.VMEM((4, 32, 896), BF),
            pltpu.VMEM((4, 32, 896), BF),
            pltpu.VMEM((16, 1024), F32),
            pltpu.VMEM((2, 1024, 128), BF),
            pltpu.VMEM((128, 1024), BF),
            pltpu.VMEM((128, 1024), BF),
            pltpu.VMEM((128, 1024), BF),
            pltpu.VMEM((128, 1024), F32),
            pltpu.VMEM((128, 1024), F32),
            pltpu.VMEM((1024, 128), F32),
            pltpu.VMEM((1024, 128), F32),
            pltpu.VMEM((256, 1024), F32),
            pltpu.VMEM((32, 3072), F32),
            pltpu.VMEM((32, 1024), F32),
            pltpu.VMEM((8, 128), F32),
            pltpu.SemaphoreType.DMA((210,)),
            pltpu.SemaphoreType.DMA((210,)),
            pltpu.SemaphoreType.DMA((6,)),
            pltpu.SemaphoreType.DMA((12,)),
        ],
        compiler_params=pltpu.CompilerParams(
            collective_id=0, has_side_effects=True, vmem_limit_bytes=65400 * 2**10
        ),
        cost_estimate=pl.CostEstimate(flops=46 * 10**9, bytes_accessed=10**7, transcendentals=10**7),
    )(ends, prm, w_qkv, w_attn, w_in, w_out, turn_tables(1024), inputs, cotangent)
    row = jax.ShapeDtypeStruct((1, 32), F32)
    final = pl.pallas_call(
        publish,
        out_shape=shapes + (row, row, row, jax.ShapeDtypeStruct((1, 128), F32)),
        in_specs=[in_any] * 6 + [in_vmem],
        out_specs=(in_any,) * 6 + (in_vmem,) * 4,
        scratch_shapes=[pltpu.VMEM(v.shape, v.dtype) for v in shapes]
        + [pltpu.SemaphoreType.DMA((6,)), pltpu.SemaphoreType.DMA((6,))],
        compiler_params=pltpu.CompilerParams(vmem_limit_bytes=60 * 2**20),
    )(*results)
    out, grad_in, grad_q, grad_a, grad_i, grad_o, bias, gain, bias_out, bias_in = final
    return (
        out,
        grad_in,
        gain.reshape(32),
        bias.reshape(32),
        grad_q,
        grad_a,
        grad_i,
        bias_in.reshape(128),
        grad_o,
        bias_out.reshape(32),
    )


def fits_fused(mesh):
    return mesh.shape["batch"] == 8 and mesh.shape["seq"] == 4


def solution(mesh):
    return jax.shard_map(
        fused_shards if fits_fused(mesh) else shards,
        mesh=mesh,
        in_specs=(
            P("batch", "seq", None),
            P("batch"),
            P(("batch", "seq")),
            P(("batch", "seq")),
            P(("batch", "seq"), None),
            P(("batch", "seq"), None),
            P(("batch", "seq"), None),
            P(("batch", "seq")),
            P(("batch", "seq"), None),
            P(("batch", "seq")),
            P("batch", "seq", None),
        ),
        out_specs=(
            P("batch", "seq", None),
            P("batch", "seq", None),
            P(("batch", "seq")),
            P(("batch", "seq")),
            P(("batch", "seq"), None),
            P(("batch", "seq"), None),
            P(("batch", "seq"), None),
            P(("batch", "seq")),
            P(("batch", "seq"), None),
            P(("batch", "seq")),
        ),
        check_vma=False,
    )
```

```python
import math

import jax
import jax.numpy as jnp
import numpy as np
from jax import lax
from jax.experimental import pallas as pl
from jax.experimental.pallas import tpu as pltpu
from jax.sharding import PartitionSpec as P

HEADS = 16
HD = 64
ROTARY = 32
MICRO = 2


norm_eps = 1e-05
gelu_factor = 0.7978845608028654
masked_score = -1e30


def gelu_tanh(values):
    return (
        0.5
        * values
        * (1.0 + jnp.tanh(gelu_factor * (values + 0.044715 * values * values * values)))
    )


def layer_norm(row_values, norm_gain, norm_shift):
    average = jnp.mean(row_values, axis=-1, keepdims=True)
    centered = row_values - average
    variance = jnp.mean(centered * centered, axis=-1, keepdims=True)
    return centered * lax.rsqrt(variance + norm_eps) * norm_gain + norm_shift


def rotary_tables(positions):
    pair_index = jnp.arange(ROTARY // 2, dtype=jnp.float32)
    inverse = 10000.0 ** (-2.0 * pair_index / ROTARY)
    angles = positions[:, None] * inverse[None, :]
    return (jnp.cos(angles), jnp.sin(angles))


def rotate(vectors, cosine, sine_table):
    rotated = vectors[..., :ROTARY]
    even_part = rotated[..., 0::2]
    odd_part = rotated[..., 1::2]
    cosine_wide = cosine[:, None, :]
    sine_wide = sine_table[:, None, :]
    new_even = even_part * cosine_wide - odd_part * sine_wide
    new_odd = odd_part * cosine_wide + even_part * sine_wide
    merged = jnp.stack([new_even, new_odd], axis=-1).reshape(rotated.shape)
    return jnp.concatenate([merged, vectors[..., ROTARY:]], axis=-1)


def visible(query_places, key_places, ending):
    query_after = query_places[:, None] >= ending
    key_after = key_places[None, :] >= ending
    return (key_places[None, :] <= query_places[:, None]) & (query_after == key_after)


def block_scores(block_queries, key_vectors, query_places, key_places, ending, score_scale):
    scores = (
        jnp.einsum("qhd,khd->hqk", block_queries, key_vectors, preferred_element_type=jnp.float32)
        * score_scale
    )
    return jnp.where(visible(query_places, key_places, ending)[None], scores, masked_score)


def attend_forward(packed, ending):
    seq_len, head_count, triple = packed.shape
    head_size = triple // 3
    block_rows = min(512, seq_len)
    score_scale = 1.0 / math.sqrt(head_size)
    queries = packed[:, :, :head_size]
    key_vectors = packed[:, :, head_size : 2 * head_size]
    values = packed[:, :, 2 * head_size :]
    key_places = jnp.arange(seq_len, dtype=jnp.int32)

    def one_block(block_index):
        first_row = block_index * block_rows
        block_queries = lax.dynamic_slice_in_dim(queries, first_row, block_rows, 0)
        query_places = first_row + jnp.arange(block_rows, dtype=jnp.int32)
        scores = block_scores(
            block_queries, key_vectors, query_places, key_places, ending, score_scale
        )
        row_peak = jnp.max(scores, axis=-1, keepdims=True)
        weights = jnp.exp(scores - row_peak)
        row_total = jnp.sum(weights, axis=-1, keepdims=True)
        probabilities = (weights / row_total).astype(jnp.bfloat16)
        result = jnp.einsum(
            "hqk,khd->qhd", probabilities, values, preferred_element_type=jnp.float32
        )
        return (result.astype(jnp.bfloat16), row_peak, row_total)

    results, peaks, totals = lax.map(one_block, jnp.arange(seq_len // block_rows, dtype=jnp.int32))
    return (results.reshape(seq_len, head_count, head_size), peaks, totals)


def attend_backward(packed, d_attended, peaks, totals, ending, full_cosine, full_sine):
    seq_len, head_count, triple = packed.shape
    head_size = triple // 3
    block_rows = min(512, seq_len)
    score_scale = 1.0 / math.sqrt(head_size)
    queries = packed[:, :, :head_size]
    key_vectors = packed[:, :, head_size : 2 * head_size]
    values = packed[:, :, 2 * head_size :]
    key_places = jnp.arange(seq_len, dtype=jnp.int32)

    def one_block(running, block_inputs):
        key_grads, value_grads = running
        block_index, row_peak, row_total = block_inputs
        first_row = block_index * block_rows
        block_queries = lax.dynamic_slice_in_dim(queries, first_row, block_rows, 0)
        block_grads = lax.dynamic_slice_in_dim(d_attended, first_row, block_rows, 0)
        query_places = first_row + jnp.arange(block_rows, dtype=jnp.int32)
        scores = block_scores(
            block_queries, key_vectors, query_places, key_places, ending, score_scale
        )
        probabilities = jnp.exp(scores - row_peak) / row_total
        rounded_probs = probabilities.astype(jnp.bfloat16)
        d_probs = jnp.einsum(
            "qhd,khd->hqk", block_grads, values, preferred_element_type=jnp.float32
        )
        row_dot = jnp.sum(probabilities * d_probs, axis=-1, keepdims=True)
        d_scores = (probabilities * (d_probs - row_dot)).astype(jnp.bfloat16)
        query_grads = (
            jnp.einsum("hqk,khd->qhd", d_scores, key_vectors, preferred_element_type=jnp.float32)
            * score_scale
        )
        key_grads = (
            key_grads
            + jnp.einsum(
                "hqk,qhd->khd", d_scores, block_queries, preferred_element_type=jnp.float32
            )
            * score_scale
        )
        value_grads = value_grads + jnp.einsum(
            "hqk,qhd->khd", rounded_probs, block_grads, preferred_element_type=jnp.float32
        )
        return ((key_grads, value_grads), query_grads)

    zero_sums = jnp.zeros((seq_len, head_count, head_size), jnp.float32)
    block_ids = jnp.arange(seq_len // block_rows, dtype=jnp.int32)
    (key_grads, value_grads), query_grads = lax.scan(
        one_block, (zero_sums, zero_sums), (block_ids, peaks, totals)
    )
    query_grads = query_grads.reshape(seq_len, head_count, head_size)
    flipped_sine = -full_sine
    combined = jnp.stack(
        [
            rotate(query_grads, full_cosine, flipped_sine),
            rotate(key_grads, full_cosine, flipped_sine),
            value_grads,
        ],
        axis=2,
    )
    return combined.astype(jnp.bfloat16).reshape(seq_len, head_count, triple)


def collect(ln_gain, ln_bias, w_qkv, w_attn, w_in, b_in, w_out, b_out):
    return (
        lax.all_gather(ln_gain, ("batch", "seq"), axis=0, tiled=True),
        lax.all_gather(ln_bias, ("batch", "seq"), axis=0, tiled=True),
        lax.all_gather(w_qkv, ("batch", "seq"), axis=0, tiled=True),
        lax.all_gather(w_attn, ("batch", "seq"), axis=0, tiled=True),
        lax.all_gather(w_in, ("batch", "seq"), axis=0, tiled=True),
        lax.all_gather(b_in, ("batch", "seq"), axis=0, tiled=True),
        lax.all_gather(w_out, ("batch", "seq"), axis=0, tiled=True),
        lax.all_gather(b_out, ("batch", "seq"), axis=0, tiled=True),
    )


def reduce_grads(gradients):
    return (
        lax.psum_scatter(gradients[0], ("batch", "seq"), scatter_dimension=0, tiled=True),
        lax.psum_scatter(gradients[1], ("batch", "seq"), scatter_dimension=0, tiled=True),
        lax.psum_scatter(gradients[2], ("batch", "seq"), scatter_dimension=0, tiled=True),
        lax.psum_scatter(gradients[3], ("batch", "seq"), scatter_dimension=0, tiled=True),
        lax.psum_scatter(gradients[4], ("batch", "seq"), scatter_dimension=0, tiled=True),
        lax.psum_scatter(gradients[5], ("batch", "seq"), scatter_dimension=0, tiled=True),
        lax.psum_scatter(gradients[6], ("batch", "seq"), scatter_dimension=0, tiled=True),
        lax.psum_scatter(gradients[7], ("batch", "seq"), scatter_dimension=0, tiled=True),
    )


def shards(inputs, ends, ln_gain, ln_bias, w_qkv, w_attn, w_in, b_in, w_out, b_out, cotangent):
    seq_devices = lax.axis_size("seq")
    windows, local_len, model_width = inputs.shape
    seq_len = local_len * seq_devices
    per_micro = windows // MICRO
    offset = lax.axis_index("seq") * local_len
    cosine, sine_table = rotary_tables(
        (offset + jnp.arange(local_len, dtype=jnp.int32)).astype(jnp.float32)
    )
    full_cosine, full_sine = rotary_tables(jnp.arange(seq_len, dtype=jnp.float32))
    outputs = []
    input_grads = []
    shard_sums = None
    for micro_index in range(MICRO):
        gathered = collect(ln_gain, ln_bias, w_qkv, w_attn, w_in, b_in, w_out, b_out)
        (
            gain_full,
            shift_full,
            qkv_full,
            attn_full,
            in_full,
            bias_in_full,
            out_full,
            bias_out_full,
        ) = gathered
        lower = micro_index * per_micro
        row_values = inputs[lower : lower + per_micro].astype(jnp.float32)
        grad_rows = cotangent[lower : lower + per_micro]
        window_ends = ends[lower : lower + per_micro]
        normed_f, norm_pull = jax.vjp(
            layer_norm, row_values, gain_full.astype(jnp.float32), shift_full.astype(jnp.float32)
        )
        normed = normed_f.astype(jnp.bfloat16)
        projected = jnp.einsum("pld,de->ple", normed, qkv_full, preferred_element_type=jnp.float32)
        arranged = projected.reshape(per_micro, local_len, HEADS, 3, HD)
        query_rot = rotate(arranged[:, :, :, 0], cosine, sine_table)
        key_rot = rotate(arranged[:, :, :, 1], cosine, sine_table)
        packed = jnp.stack([query_rot, key_rot, arranged[:, :, :, 2]], axis=3).astype(jnp.bfloat16)
        packed = packed.reshape(per_micro, local_len, HEADS, 3 * HD)
        head_view = lax.all_to_all(packed, "seq", split_axis=2, concat_axis=1, tiled=True)
        attended, peaks, totals = lax.map(
            lambda bundle: attend_forward(bundle[0], bundle[1]), (head_view, window_ends)
        )
        position_view = lax.all_to_all(
            attended, "seq", split_axis=1, concat_axis=2, tiled=True
        ).reshape(per_micro, local_len, model_width)
        branch_attn = jnp.einsum(
            "ple,ed->pld", position_view, attn_full, preferred_element_type=jnp.float32
        )
        hidden = jnp.einsum(
            "pld,di->pli", normed, in_full, preferred_element_type=jnp.float32
        ) + bias_in_full.astype(jnp.float32)
        activ_f, gelu_pull = jax.vjp(gelu_tanh, hidden)
        activated = activ_f.astype(jnp.bfloat16)
        branch_mlp = jnp.einsum(
            "pli,id->pld", activated, out_full, preferred_element_type=jnp.float32
        ) + bias_out_full.astype(jnp.float32)
        outputs.append((row_values + branch_attn + branch_mlp).astype(jnp.bfloat16))
        grad_b_out = jnp.sum(grad_rows.astype(jnp.float32), axis=(0, 1))
        grad_w_out = jnp.einsum(
            "pli,pld->id", activated, grad_rows, preferred_element_type=jnp.float32
        )
        d_activated = jnp.einsum(
            "pld,id->pli", grad_rows, out_full, preferred_element_type=jnp.float32
        )
        d_hidden = gelu_pull(d_activated)[0].astype(jnp.bfloat16)
        grad_b_in = jnp.sum(d_hidden.astype(jnp.float32), axis=(0, 1))
        grad_w_in = jnp.einsum("pld,pli->di", normed, d_hidden, preferred_element_type=jnp.float32)
        grad_w_attn = jnp.einsum(
            "ple,pld->ed", position_view, grad_rows, preferred_element_type=jnp.float32
        )
        d_attended = jnp.einsum(
            "pld,ed->ple", grad_rows, attn_full, preferred_element_type=jnp.float32
        ).astype(jnp.bfloat16)
        d_attended = d_attended.reshape(per_micro, local_len, HEADS, HD)
        d_head_view = lax.all_to_all(d_attended, "seq", split_axis=2, concat_axis=1, tiled=True)
        d_packed = lax.map(
            lambda bundle: attend_backward(
                bundle[0], bundle[1], bundle[2], bundle[3], bundle[4], full_cosine, full_sine
            ),
            (head_view, d_head_view, peaks, totals, window_ends),
        )
        d_projected = lax.all_to_all(
            d_packed, "seq", split_axis=1, concat_axis=2, tiled=True
        ).reshape(per_micro, local_len, 3 * model_width)
        grad_w_qkv = jnp.einsum(
            "pld,ple->de", normed, d_projected, preferred_element_type=jnp.float32
        )
        d_normed = jnp.einsum("pli,di->pld", d_hidden, in_full, preferred_element_type=jnp.float32)
        d_normed = d_normed + jnp.einsum(
            "ple,de->pld", d_projected, qkv_full, preferred_element_type=jnp.float32
        )
        d_rows, grad_gain, grad_shift = norm_pull(d_normed)
        input_grads.append(grad_rows.astype(jnp.float32) + d_rows)
        local_grads = (
            grad_gain,
            grad_shift,
            grad_w_qkv,
            grad_w_attn,
            grad_w_in,
            grad_b_in,
            grad_w_out,
            grad_b_out,
        )
        reduced = reduce_grads(local_grads)
        if shard_sums is None:
            shard_sums = reduced
        else:
            shard_sums = tuple((running + extra for running, extra in zip(shard_sums, reduced)))
    output = jnp.concatenate(outputs, axis=0)
    grad_inputs = jnp.concatenate(input_grads, axis=0)
    return (
        output,
        grad_inputs,
        shard_sums[0],
        shard_sums[1],
        shard_sums[2],
        shard_sums[3],
        shard_sums[4],
        shard_sums[5],
        shard_sums[6],
        shard_sums[7],
    )


HB, SB = 4, 4
NEG = -1e30
BF, F32 = jnp.bfloat16, jnp.float32
MESH = pl.DeviceIdType.MESH


def dot(a, b, ca, cb):
    return lax.dot_general(a, b, (((ca,), (cb,)), ((), ())), preferred_element_type=F32)


def rows(start, size):
    return pl.ds(pl.multiple_of(start, size), size)


def lanes(start, size=128):
    return pl.ds(pl.multiple_of(start, size), size)


def halves(low_source, high_source):
    def piece(source, upper):
        array, first = source
        tile = array[:, first // 128 * 128 : first // 128 * 128 + 128]
        return pltpu.roll(tile, 64, 1) if (first % 128 == 64) != upper else tile

    lane = lax.broadcasted_iota(jnp.int32, (1, 128), 1)
    return jnp.where(lane < 64, piece(low_source, False), piece(high_source, True))


def head_of(owner, j):
    return 4 * j + 2 * (owner % 2) + owner // 2


class Link:
    def __init__(self, send_sems, recv_sems):
        self.send_sems, self.recv_sems = send_sems, recv_sems
        self.first = {}
        self.used = 0

    def index(self, name, at, count):
        if name not in self.first:
            self.first[name] = self.used
            self.used += count
        return self.first[name] + at

    def copy(self, name, at, count, src, dst, device):
        i = self.index(name, at, count)
        return pltpu.make_async_remote_copy(
            src_ref=src,
            dst_ref=dst,
            send_sem=self.send_sems.at[i],
            recv_sem=self.recv_sems.at[i],
            device_id=device,
            device_id_type=MESH,
        )


def gelu_pair(v):
    square = v * v
    half = 0.5 + 0.5 * jnp.tanh(v * (gelu_factor + (gelu_factor * 0.044715) * square))
    value = v * half
    return value, half + (value - value * half) * (
        2.0 * gelu_factor + (6.0 * gelu_factor * 0.044715) * square
    )


def fused_layer(
    ends, prm, wq, wa, wi, wo, turns, x_in, g_in,
    out_hbm, grad_in_hbm, grad_q_hbm, grad_a_hbm, grad_i_hbm, grad_o_hbm, grad_small_hbm,
    X, N, G, A, H, Wi, Wo, Wq, WaAll, Wa, PWI, PWQ, PRS, PRM, PR, QKV, att, dO,
    GO, XO, ZO, CO, GI, XI, ZI, GQ, XQ, ZQ, GA, XA, ZA, GT, XT, ZT,
    YR, SWI, RWI, SWQ, RWQ, SWT, RWT, TAIL,
    khat, ktT, vtT, doT, oT, dqT, dkA, dvA,
    grad_in, grad_q, grad_a, grad_small,
    send_sems, recv_sems, local_sems, out_sems,
):
    b = lax.axis_index("batch")
    s = lax.axis_index("seq")
    z, xx = b // 2, b % 2
    y, c = s // 2, s % 2
    oc, ox, oy = 1 - c, 1 - xx, 1 - y
    SL = 256
    S = 1024
    core = (b, 2 * y + oc)
    ypart = (b, 2 * oy + c)
    diag = (b, 2 * oy + oc)
    xpart = (2 * z + ox, s)

    def zdev(k):
        return (2 * ((z + k) % 4) + xx, s)

    def zfrom(k):
        return (z + 4 - k) % 4

    link = Link(send_sems, recv_sems)
    pending = []

    def start(make):
        make().start()
        pending.append(make)

    barrier = pltpu.get_barrier_semaphore()
    others = [xpart] + [zdev(k) for k in (1, 2, 3)]
    others += [(2 * ((z + k) % 4) + ox, s) for k in (1, 2, 3)]
    partners = [core, ypart, diag] + others
    for device in partners:
        pl.semaphore_signal(barrier, inc=1, device_id=device, device_id_type=MESH)

    own = rows(SL * s, SL)
    locals_ = []
    for w in range(2):
        locals_.append(pltpu.make_async_copy(x_in.at[w], X.at[w, own], local_sems.at[3 * w]))
        locals_.append(pltpu.make_async_copy(g_in.at[w], G.at[w, own], local_sems.at[3 * w + 1]))
    for cp in locals_:
        cp.start()

    for r in range(SB):
        for blk in range(8):
            PWI[r, :, 128 * blk : 128 * blk + 128] = wi[:, 512 * blk + 128 * r : 512 * blk + 128 * r + 128]
    tile = prm[...].astype(F32)
    row = lax.broadcasted_iota(jnp.int32, (16, 128), 0)
    tile = jnp.where(row < 3, pltpu.roll(tile, 32 * s, 1), tile)
    PRS[s] = tile.astype(BF)
    Wi[rows(128 * b + 32 * s, 32), :] = PWI[s]
    Wo[rows(128 * b, 128), :] = wo[...]
    WaAll[z, xx] = wa[...]

    wq_f = wq[...].astype(F32)
    for r in range(SB):
        for kind in range(3):
            for p in range(2):
                lo = 192 * head_of(r, 2 * p) + 64 * kind
                hi = 192 * head_of(r, 2 * p + 1) + 64 * kind
                at = 384 * p + 128 * kind
                PWQ[r, :, at : at + 128] = halves((wq_f, lo), (wq_f, hi)).astype(BF)
    Wq[rows(128 * b + 32 * s, 32), :] = PWQ[s]

    pl.semaphore_wait(barrier, len(partners))

    def seq_sends(name, src_of, dst):
        for i, (device, owner) in enumerate(
            ((core, 2 * y + oc), (ypart, 2 * oy + c), (diag, 2 * oy + oc))
        ):
            link.copy(name, i, 3, src_of(owner), dst(), device).start()

    def seq_left(name, src_of, dst):
        for i, (device, owner) in enumerate(
            ((core, 2 * y + oc), (ypart, 2 * oy + c), (diag, 2 * oy + oc))
        ):
            link.copy(name, i, 3, src_of(owner), dst(), device).wait_send()

    def seq_waits(name, src, dst_of):
        for i, owner in enumerate((2 * y + oc, 2 * oy + c, 2 * oy + oc)):
            link.copy(name, i, 3, src, dst_of(owner), core).wait_recv()

    def prm_block(owner):
        return PRS.at[owner]

    def wi_block(owner, u):
        return Wi.at[rows(128 * b + 32 * owner, 32), 256 * u : 256 * u + 256]

    def wq_block(owner):
        return Wq.at[rows(128 * b + 32 * owner, 32)]

    gathers = {
        "wi": (4, lambda bb, u: Wi.at[rows(128 * bb, 128), lanes(256 * u, 256)]),
        "wo": (2, lambda bb, u: Wo.at[rows(128 * bb + 64 * u, 64)]),
        "wq": (2, lambda bb, u: Wq.at[rows(128 * bb, 128), 384 * u : 384 * u + 384]),
        "wa": (1, lambda bb, u: WaAll.at[bb // 2, bb % 2]),
    }
    pair = z + 1 - 2 * (z % 2)

    def gather_copy(name, way, at, count, zz, side, u, device):
        held = gathers[name][1](2 * zz + side, u)
        return link.copy(name + way, count * u + at, count * gathers[name][0], held, held, device)

    def up_copy(name, zz, u):
        return gather_copy(name, "l", zz, 5, zz, xx, u, (2 * (z + 1) + xx, s))

    def down_copy(name, zz, u):
        return gather_copy(name, "l", zz + 1, 5, zz, xx, u, (2 * (z - 1) + xx, s))

    def z_copy(name, zz, k, u):
        return gather_copy(name, "z", k - 1, 3, zz, xx, u, zdev(k))

    def x_copy(name, zz, side, u):
        return gather_copy(name, "x", zz, 4, zz, side, u, xpart)

    def gather_z(name, u):
        if name == "wi":

            @pl.when(z < 3)
            def _():
                up_copy(name, z, u).start()

            @pl.when(z > 0)
            def _():
                down_copy(name, z, u).start()

            return
        for far in (1, 2, 3):

            @pl.when(z + far <= 3)
            def _():
                z_copy(name, z, far, u).start()

            @pl.when(z >= far)
            def _():
                z_copy(name, z, 4 - far, u).start()

    def gather_x(name, u):
        x_copy(name, z, xx, u).start()

    def gather_pass(name, far, u):
        @pl.when(z >= far)
        def _():
            if name == "wi":
                up_copy(name, z - far, u).wait_recv()

                @pl.when(z < 3)
                def _():
                    up_copy(name, z - far, u).start()

            else:
                z_copy(name, z - far, far, u).wait_recv()
            x_copy(name, z - far, xx, u).start()

        @pl.when(z + far <= 3)
        def _():
            if name == "wi":
                down_copy(name, z + far, u).wait_recv()

                @pl.when(z > 0)
                def _():
                    down_copy(name, z + far, u).start()

            else:
                z_copy(name, z + far, 4 - far, u).wait_recv()
            x_copy(name, z + far, xx, u).start()

    def gather_block(name, zz, u):
        x_copy(name, zz, ox, u).wait_recv()

    def gather_end(name, u):
        for zz in range(4):
            gather_block(name, zz, u)

    def gather_left(name, u):
        if name != "wi":
            for k in (1, 2, 3):
                z_copy(name, z, k, u).wait_send()
        for zz in range(4):
            if name == "wi":

                @pl.when((zz <= z) & (z < 3))
                def _():
                    up_copy(name, zz, u).wait_send()

                @pl.when((zz >= z) & (z > 0))
                def _():
                    down_copy(name, zz, u).wait_send()

            x_copy(name, zz, xx, u).wait_send()

    def rows_start(name, src, dst):
        for w in range(2):
            start(lambda w=w: link.copy(name + "c", w, 2, src.at[w], dst.at[w, own], core))
            start(lambda w=w: link.copy(name + "y", w, 2, src.at[w], dst.at[w, own], ypart))

    def rows_pass(name, dst, w):
        block = dst.at[w, rows(SL * (2 * oy + c), SL)]
        link.copy(name + "y", w, 2, block, block, core).wait_recv()
        link.copy(name + "f", w, 2, block, block, core).start()

    def rows_left(name, dst, w):
        block = dst.at[w, rows(SL * (2 * oy + c), SL)]
        link.copy(name + "f", w, 2, block, block, core).wait_send()

    def rows_end_core(name, dst, w):
        block = dst.at[w, rows(SL * (2 * y + oc), SL)]
        link.copy(name + "c", w, 2, block, block, core).wait_recv()

    def rows_end_far(name, dst, w):
        block = dst.at[w, rows(SL * (2 * oy + oc), SL)]
        link.copy(name + "f", w, 2, block, block, core).wait_recv()

    seq_sends("prms", lambda owner: prm_block(s), lambda: prm_block(s))
    for u in range(4):
        seq_sends(
            "wis%d" % u, lambda owner: PWI.at[owner, :, 256 * u : 256 * u + 256], lambda: wi_block(s, u)
        )
    gather_z("wa", 0)
    gather_x("wa", 0)
    gather_x("wo", 0)
    seq_sends("wqs", lambda owner: PWQ.at[owner], lambda: wq_block(s))
    rows_start("x", x_in, X)
    seq_waits("prms", prm_block(s), prm_block)
    total = PRS[0].astype(F32) + PRS[1].astype(F32) + PRS[2].astype(F32) + PRS[3].astype(F32)
    PRM[b] = jnp.where(row < 3, total, tile).astype(BF)
    for i, device in enumerate(others):
        start(lambda i=i, device=device: link.copy("prm", i, 7, PRM.at[b], PRM.at[b], device))
    for u in range(4):
        seq_waits("wis%d" % u, wi_block(s, u), lambda owner: wi_block(owner, u))
        gather_z("wi", u)
        gather_x("wi", u)
    rows_start("g", g_in, G)
    gather_pass("wi", 1, 0)
    gather_pass("wi", 1, 1)
    for far in (1, 2, 3):
        gather_pass("wa", far, 0)

    for i in range(7):
        k = (0, 1, 2, 3, 1, 2, 3)[i]
        bb = 2 * zfrom(k) + (ox if i in (0, 4, 5, 6) else xx)
        link.copy("prm", i, 7, PRM.at[bb], PRM.at[bb], core).wait_recv()
    for bb in range(8):
        PR[:, 128 * bb : 128 * bb + 128] = PRM[bb].astype(F32)[0:8]

    for cp in locals_:
        cp.wait()

    def norm_rows(w, owner):
        r = rows(SL * owner, SL)
        v = X[w, r, :].astype(F32)
        v = v - jnp.mean(v, axis=-1, keepdims=True)
        var = jnp.mean(v * v, axis=-1, keepdims=True)
        N[w, r, :] = (v * lax.rsqrt(var + norm_eps) * PR[0:1, :] + PR[1:2, :]).astype(BF)

    def norm_near(w, carry):
        norm_rows(w, s)
        norm_rows(w, 2 * y + oc)
        return carry

    def norm_far(w):
        rows_end_far("x", X, w)
        norm_rows(w, 2 * oy + c)
        norm_rows(w, 2 * oy + oc)

    for w in range(2):
        rows_end_core("x", X, w)
    lax.fori_loop(0, 2, norm_near, 0)
    gather_pass("wi", 2, 0)
    gather_pass("wi", 1, 2)
    gather_pass("wi", 1, 3)
    seq_waits("wqs", wq_block(s), wq_block)
    gather_z("wq", 0)
    gather_x("wq", 0)
    gather_pass("wi", 2, 1)
    gather_pass("wi", 3, 0)
    gather_pass("wi", 2, 2)
    gather_pass("wi", 3, 1)
    rows_pass("x", X, 0)
    gather_pass("wi", 2, 3)
    gather_z("wq", 1)
    gather_x("wq", 1)

    def hidden_step(i, carry):
        early = i < 12
        u = jnp.where(early, i // 3, i - 12)
        at = jnp.where(early, i % 3, 3)
        w = at % 2
        t = jnp.where(at < 2, y, oy)

        @pl.when(i == 0)
        def _():
            gather_end("wi", 0)

        @pl.when(i == 2)
        def _():
            norm_far(0)

        @pl.when(i == 3)
        def _():
            gather_pass("wi", 3, 2)
            gather_end("wi", 1)

        @pl.when(i == 5)
        def _():
            gather_pass("wi", 3, 3)
            gather_z("wo", 0)
            gather_z("wo", 1)
            gather_pass("wq", 1, 0)

        @pl.when(i == 6)
        def _():
            gather_end("wi", 2)

        @pl.when(i == 7)
        def _():
            rows_pass("x", X, 1)

        @pl.when(i == 9)
        def _():
            gather_pass("wq", 2, 0)
            gather_end("wi", 3)

        @pl.when(i == 11)
        def _():
            gather_pass("wq", 3, 0)

        @pl.when(i == 12)
        def _():
            norm_far(1)

        @pl.when(i == 14)
        def _():
            gather_pass("wq", 1, 1)
            gather_x("wo", 1)

        r, l = rows(512 * t, 512), lanes(256 * u, 256)
        v = dot(N[w, r, :], Wi[:, l], 1, 0) + PR[3:4, l]
        value, slope = gelu_pair(v)
        A[w, r, l] = value.astype(BF)
        H[w, r, l] = slope.astype(BF)
        return carry

    lax.fori_loop(0, 16, hidden_step, 0)
    for w in range(2):
        rows_left("x", X, w)
    gather_end("wa", 0)
    start(lambda: link.copy("wac", 0, 1, WaAll.at[:, oc], Wa.at[:, c], core))
    Wa[:, c] = WaAll[:, c]
    for far in (2, 3):
        gather_pass("wq", far, 1)

    def add_into(dst, other):
        dst[...] = (dst[...].astype(F32) + other[...].astype(F32)).astype(BF)

    inner = (z == 1) | (z == 2)

    def far_chip(tt):
        return 2 * (1 - z // 2) + tt

    def zchip(zz):
        return (2 * zz + xx, s)

    def o_near(q):
        return link.copy("op", 0, 1, GO.at[q, xx], ZO.at[0], zchip(pair))

    def o_comb(q):
        return link.copy("oc", q % 2, 2, GO.at[q, xx], CO.at[q % 2], zchip(pair))

    def o_far(q):
        return link.copy("of", q % 2, 2, GO.at[q, xx], ZO.at[1], zchip(q))

    def i_z(q, k):
        return link.copy("iz", 3 * q + k - 1, 12, GI.at[q, xx, (z + k) % 4], ZI.at[k - 1, q], zdev(k))

    def first_o(q):
        o_x(q).wait_recv()

        @pl.when(z != q)
        def _():
            add_into(GO.at[q, xx], XO.at[q])

            @pl.when(q == pair)
            def _():
                o_near(q).start()

            @pl.when((q != pair) & ~inner)
            def _():
                o_comb(q).start()

    def first_i(q):
        i_x(q).wait_recv()
        for k in (1, 2, 3):
            zz = (z + k) % 4
            add_into(GI.at[q, xx, zz], XI.at[q, zz])
            i_z(q, k).start()

    def second_z(q):
        @pl.when(inner)
        def _():
            o_comb(q).wait_recv()
            add_into(GO.at[q, xx], CO.at[q % 2])
            o_far(q).start()

    def z_left():
        o_near(pair).wait_send()
        for tt in range(2):

            @pl.when(inner)
            def _():
                o_far(far_chip(tt)).wait_send()

            @pl.when(~inner)
            def _():
                o_comb(far_chip(tt)).wait_send()

        for q in range(4):
            for k in (1, 2, 3):
                i_z(q, k).wait_send()

    def chunk(j):
        return jnp.where(j == 3, z, jnp.where(j == 2, pair, far_chip(0) + j))

    def o_x(q):
        return link.copy("ox", q, 4, GO.at[q, ox], XO.at[q], xpart)

    def i_x(q):
        return link.copy("ix", q, 4, GI.at[q, ox], XI.at[q], xpart)

    even = lax.broadcasted_iota(jnp.int32, (1, 128), 1) % 2 == 0

    def turn_rows(r):
        table = turns[r, :]
        other = pltpu.roll(table, 64, 1)
        low = lax.broadcasted_iota(jnp.int32, (1, 128), 1) < 64
        return jnp.where(low, table, other), jnp.where(low, other, table)

    def turn(v, cos_rows, sin_rows):
        swapped = jnp.where(even, pltpu.roll(v, 127, 1), pltpu.roll(v, 1, 1))
        return v * cos_rows + swapped * sin_rows

    def qkv_step(p):
        gather_end("wq", p)
        l = slice(384 * p, 384 * p + 384)

        def step(i, carry):
            w, r = i // 4, rows(256 * (i % 4), 256)
            v = dot(N[w, r, :], Wq[:, l], 1, 0)
            cos_rows, sin_rows = turn_rows(r)
            for kind in range(3):
                tile_v = v[:, 128 * kind : 128 * kind + 128]
                if kind < 2:
                    tile_v = turn(tile_v, cos_rows, sin_rows)
                if kind == 0:
                    tile_v = tile_v * 0.125
                QKV[w, r, 384 * p + 128 * kind : 384 * p + 128 * kind + 128] = tile_v.astype(BF)
            return carry

        lax.fori_loop(0, 8, step, 0)

    qkv_step(0)
    for w in range(2):
        rows_end_core("g", G, w)
    rows_pass("g", G, 0)
    for u in range(4):
        seq_left(
            "wis%d" % u, lambda owner: PWI.at[owner, :, 256 * u : 256 * u + 256], lambda: wi_block(s, u)
        )
    link.copy("wac", 0, 1, WaAll.at[:, oc], Wa.at[:, oc], core).wait_recv()
    TAIL[...] = jnp.zeros_like(TAIL)

    def do_step(w):
        def step(i, total):
            r = rows(512 * i, 512)
            g = G[w, r, :]
            dO[w, r, :] = dot(g, Wa[...].reshape(256, 1024), 1, 1).astype(BF)
            return total + jnp.sum(g.astype(F32), axis=0, keepdims=True)

        TAIL[2:3, :] += lax.fori_loop(0, 2, step, jnp.zeros((1, 1024), F32))

    rows_end_far("g", G, 0)
    do_step(0)

    def units_back(j):
        q = chunk(j)
        l = lanes(256 * q, 256)

        def step(i, total):
            w, r = i // 2, rows(512 * (i % 2), 512)
            d = dot(G[w, r, :], Wo[rows(256 * q, 256), :], 1, 1) * H[w, r, l].astype(F32)
            d = d.astype(BF)
            H[w, r, l] = d
            return total + jnp.sum(d.astype(F32), axis=0, keepdims=True)

        TAIL[3:4, l] = lax.fori_loop(0, 4, step, jnp.zeros((1, 256), F32))

    def units_out(j):
        q = chunk(j)
        l = lanes(256 * q, 256)
        go = dot(A[0, :, l], G[0], 0, 0) + dot(A[1, :, l], G[1], 0, 0)
        GO[q, 0] = go[:128].astype(BF)
        GO[q, 1] = go[128:].astype(BF)

    def units_in(j):
        q = chunk(j)
        l = lanes(256 * q, 256)
        gi = dot(H[0, :, l], N[0], 0, 0) + dot(H[1, :, l], N[1], 0, 0)
        for bb in range(8):
            GI[q, bb % 2, bb // 2] = gi[:, 128 * bb : 128 * bb + 128].astype(BF)

    lane = lax.broadcasted_iota(jnp.int32, (1, 128), 1)
    place = lax.broadcasted_iota(jnp.int32, (S, 1), 0)
    BQ = 256
    key_i = lax.broadcasted_iota(jnp.int32, (BQ, BQ), 0)
    query_i = lax.broadcasted_iota(jnp.int32, (BQ, BQ), 1)
    inside = [(lane // 64) == hh for hh in range(2)]
    feature = [lane == (64 - 64 * hh) for hh in range(2)]

    def attend(w, p):
        ending = ends[w]

        def part(kind):
            return lanes(384 * p + 128 * kind)

        pl_ = lanes(128 * p)
        keys = QKV[w, :, part(1)]
        ktT[...] = keys.T
        vtT[...] = QKV[w, :, part(2)].T
        doT[...] = dO[w, :, pl_].T
        dkA[...] = jnp.zeros_like(dkA)
        dvA[...] = jnp.zeros_like(dvA)
        keys_f = keys.astype(F32)
        before = jnp.where(place < ending, NEG, 0.0)
        for hh in range(2):
            khat[hh] = jnp.where(inside[hh], keys_f, jnp.where(feature[hh], before, 0.0)).astype(BF)

        def begin(qb, hh):
            qr, nk = slice(qb * BQ, (qb + 1) * BQ), (qb + 1) * BQ
            q = QKV[w, qr, part(0)].astype(F32)
            after = jnp.where(place[qr] >= ending, 1.0, 0.0)
            q_in = jnp.where(inside[hh], q, 0.0).astype(BF)
            q_hat = jnp.where(inside[hh], q, jnp.where(feature[hh], after, 0.0)).astype(BF)
            d_in = jnp.where(inside[hh], dO[w, qr, pl_].astype(F32), 0.0).astype(BF)
            return dot(khat[hh, 0:nk, :], q_hat, 1, 1), dot(QKV[w, 0:nk, part(2)], d_in, 1, 1), q_in, d_in

        units = [(qb, hh) for qb in range(S // BQ) for hh in range(2)]
        upcoming, late = begin(*units[0]), None
        for i, (qb, hh) in enumerate(units):
            sc, dp, q_in, d_in = upcoming
            qr, nk = slice(qb * BQ, (qb + 1) * BQ), (qb + 1) * BQ
            hr = slice(64 * hh, 64 * hh + 64)
            if i + 1 < len(units):
                upcoming = begin(*units[i + 1])
            last = jnp.where(key_i <= query_i, sc[nk - BQ :], NEG)
            sc = last if qb == 0 else jnp.concatenate([sc[: nk - BQ], last], axis=0)
            e = jnp.exp(sc - jnp.max(sc, axis=0, keepdims=True))
            pn = e * (1.0 / jnp.sum(e, axis=0, keepdims=True))
            pb = pn.astype(BF)
            o = dot(vtT[hr, 0:nk], pb, 1, 0)
            if late is not None:
                late()
            oT[hr, qr] = o
            dd = jnp.sum(o * doT[hr, qr].astype(F32), axis=0, keepdims=True)
            ds = (pn * (dp - dd)).astype(BF)

            def late(hr=hr, qr=qr, nk=nk, ds=ds, pb=pb, q_in=q_in, d_in=d_in):
                dqT[hr, qr] = dot(ktT[hr, 0:nk], ds, 1, 0)
                dkA[0:nk, :] += dot(ds, q_in, 1, 0)
                dvA[0:nk, :] += dot(pb, d_in, 1, 0)

        late()
        cos_rows, sin_rows = turn_rows(slice(None))
        sin_rows = -sin_rows
        att[w, :, pl_] = oT[...].T.astype(BF)
        QKV[w, :, part(0)] = turn(dqT[...].T * 0.125, cos_rows, sin_rows).astype(BF)
        QKV[w, :, part(1)] = turn(dkA[...], cos_rows, sin_rows).astype(BF)
        QKV[w, :, part(2)] = dvA[...].astype(BF)

    shares = (A, H)

    def share_c(w, t, yy):
        src = shares[t].at[w, rows(SL * (2 * yy + oc), SL)]
        dst = X.at[w, rows(SL * (2 * t + yy), SL)]
        link.copy("sc", 4 * w + 2 * t + yy, 8, src, dst, core).start()

    def share_got(w, t, yy):
        slot = X.at[w, rows(SL * (2 * t + yy), SL)]
        link.copy("sc", 4 * w + 2 * t + yy, 8, slot, slot, core).wait_recv()
        return slot

    def share_y(w, t):
        src = shares[t].at[w, rows(SL * (2 * oy + c), SL)]
        add_into(src, share_got(w, t, oy))
        link.copy("sy", 2 * w + t, 4, src, YR.at[w, t], ypart).start()

    def share_out(w, r):
        value = dot(A[w, r, :], Wo[...], 1, 0) + dot(att[w, r, :], Wa[...].reshape(256, 1024), 1, 0)
        A[w, r, :] = value.astype(BF)

    def share_normed(w, r):
        d = dot(H[w, r, :], Wi[...], 1, 1) + dot(QKV[w, r, :], Wq[...], 1, 1)
        H[w, r, :] = d.astype(BF)
        n = (N[w, r, :].astype(F32) - PR[1:2, :]) / PR[0:1, :]
        TAIL[0:1, :] += jnp.sum(d, axis=0, keepdims=True)
        TAIL[1:2, :] += jnp.sum(d * n, axis=0, keepdims=True)

    def share_step(w, t):
        def step(i, carry):
            yy = jnp.where(i < 2, oy, y)
            cc = jnp.where(i % 2 == 0, oc, c)
            (share_out, share_normed)[t](w, rows(SL * (2 * yy + cc), SL))

            @pl.when(i == 0)
            def _():
                share_c(w, t, oy)

            @pl.when(i == 2)
            def _():
                share_y(w, t)
                share_c(w, t, y)

            return carry

        lax.fori_loop(0, 4, step, 0)

    def gq_step(p):
        for kind in range(3):
            e = 3 * p + kind
            l = slice(128 * e, 128 * e + 128)
            gq = dot(QKV[0, :, l], N[0], 0, 0) + dot(QKV[1, :, l], N[1], 0, 0)
            for bb in range(8):
                GQ[e, bb % 2, bb // 2] = gq[:, 128 * bb : 128 * bb + 128].astype(BF)
            link.copy("qx", e, 6, GQ.at[e, ox], XQ.at[e], xpart).start()

    def ga_c(p):
        two = slice(2 * p, 2 * p + 2)
        return link.copy("ac", p, 2, PWI.at[two], GA.at[c, two], core)

    def ga_x(p):
        two = slice(2 * p, 2 * p + 2)
        return link.copy("ax", p, 2, GA.at[ox, two], XA.at[two], xpart)

    def ga_step(p):
        l = slice(128 * p, 128 * p + 128)
        ga = dot(att[0, :, l], G[0], 0, 0) + dot(att[1, :, l], G[1], 0, 0)
        for j in range(2):
            for cc in range(2):
                piece = ga[64 * j + 32 * cc : 64 * j + 32 * cc + 32].astype(BF)

                @pl.when(cc == c)
                def _():
                    GA[c, 2 * p + j] = piece

                @pl.when(cc != c)
                def _():
                    PWI[2 * p + j] = piece

        ga_c(p).start()

    def ga_send(p):
        ga_c(p).wait_recv()
        ga_x(p).start()

    def z_send(get, k):
        name, group, _, landed, at, count = get()
        src = group.at[xx, (z + k) % 4]
        return link.copy(name + "z", 3 * at + k - 1, 3 * count, src, landed.at[k - 1], zdev(k))

    def z_step(get, waits=None):
        name, group, received, _, at, count = get()
        if waits is None:
            link.copy(name + "x", at, count, received, received, core).wait_recv()
        else:
            waits()
        for k in (1, 2, 3):
            zz = (z + k) % 4
            add_into(group.at[xx, zz], received.at[zz])
            start(lambda k=k: z_send(get, k))

    def of_piece(e):
        return lambda: ("q", GQ.at[e], XQ.at[e], ZQ.at[e], e, 6)

    def of_attn():
        return "a", GA, XA, ZA, 0, 1

    def attend_step(i, carry):
        w, p = i // 2, i % 2
        attend(w, p)

        @pl.when(i == 0)
        def _():
            for u in range(2):
                gather_pass("wo", 1, u)
            rows_pass("g", G, 1)
            qkv_step(1)
            for far in (2, 3):
                for u in range(2):
                    gather_pass("wo", far, u)

        @pl.when(i == 1)
        def _():
            rows_end_far("g", G, 1)
            do_step(1)

        @pl.when(i == 2)
        def _():
            gq_step(0)
            ga_step(0)

        return carry

    lax.fori_loop(0, 4, attend_step, 0)
    ga_send(0)
    gq_step(1)
    ga_step(1)
    def out_step(j, carry):
        units_out(j)

        @pl.when(j == 0)
        def _():
            z_step(of_piece(0))
            z_step(of_piece(1))
            ga_send(1)

        @pl.when(j == 2)
        def _():
            z_step(of_piece(2))

        return carry

    def in_step(j, carry):
        units_back(j)
        units_in(j)
        i_x(chunk(j)).start()

        @pl.when(j == 0)
        def _():
            z_step(of_piece(4))
            z_step(of_piece(5))

        @pl.when(j == 1)
        def _():
            ga_x(0).wait_recv()
            z_step(of_attn, waits=lambda: ga_x(1).wait_recv())

        return carry

    written = []

    def write(src, dst):
        cp = pltpu.make_async_copy(src, dst, out_sems.at[len(written)])
        cp.start()
        written.append(cp)
        return cp

    def z_total(get):
        name, group, received, landed, at, count = get()
        for k in (1, 2, 3):
            link.copy(
                name + "z", 3 * at + k - 1, 3 * count, landed.at[k - 1], landed.at[k - 1], core
            ).wait_recv()
        total = group[xx, z].astype(F32) + received[z].astype(F32)
        for k in range(3):
            total = total + landed[k].astype(F32)
        return total

    def to_seq(name, held, landed):
        landed[s] = held[s]
        seq_sends(name, lambda owner: held.at[owner], lambda: landed.at[s])

    def from_seq(name, landed):
        for i, owner in enumerate((2 * y + oc, 2 * oy + c, 2 * oy + oc)):
            link.copy(name, i, 3, landed.at[owner], landed.at[owner], core).wait_recv()

    lax.fori_loop(0, 4, out_step, 0)
    for u in range(2):
        for zz in range(4):
            gather_block("wo", zz, u)
    share_step(0, 0)
    z_step(of_piece(3))
    lax.fori_loop(0, 2, in_step, 0)
    share_step(1, 0)
    first_i(chunk(0))
    lax.fori_loop(2, 4, in_step, 0)
    for j in range(4):
        o_x(chunk(j)).start()
    first_i(chunk(1))
    for e in range(6):
        total_q = z_total(of_piece(e)).T.astype(BF)
        for owner in range(4):
            SWQ[owner, :, 128 * e : 128 * e + 128] = total_q[32 * owner : 32 * owner + 32]
    to_seq("swq", SWQ, RWQ)
    grad_a[...] = z_total(of_attn)
    write(grad_a, grad_a_hbm)
    share_step(0, 1)
    first_i(chunk(2))
    share_step(1, 1)
    again = [
        pltpu.make_async_copy(x_in.at[w], N.at[w, 0:SL], local_sems.at[3 * w + 2]) for w in range(2)
    ]
    for cp in again:
        cp.start()
    tail = TAIL[...]
    for bb in range(8):
        GT[bb % 2, bb // 2] = tail[:, 128 * bb : 128 * bb + 128].astype(BF)
    for k in (1, 2, 3):
        start(lambda k=k: link.copy("tz", k - 1, 3, GT.at[:, (z + k) % 4], ZT.at[k - 1], zdev(k)))

    def tail_x():
        for k in (1, 2, 3):
            link.copy("tz", k - 1, 3, ZT.at[k - 1], ZT.at[k - 1], core).wait_recv()
        add_into(ZT.at[0], GT.at[:, z])
        add_into(ZT.at[1], ZT.at[2])
        add_into(ZT.at[0], ZT.at[1])
        start(lambda: link.copy("tx", 0, 1, ZT.at[0, ox], XT, xpart))

    def final_o():
        o_near(z).wait_recv()
        link.copy("of", z % 2, 2, ZO.at[1], ZO.at[1], core).wait_recv()
        dqT[...] = (
            GO[z, xx].astype(F32) + XO[z].astype(F32) + ZO[0].astype(F32) + ZO[1].astype(F32)
        )

    def final_i():
        for q in range(4):
            total = GI[q, xx, z].astype(F32) + XI[q, z].astype(F32)
            for k in (1, 2, 3):
                i_z(q, k).wait_recv()
                total = total + ZI[k - 1, q].astype(F32)
            turned = total.T.astype(BF)
            for owner in range(4):
                SWI[owner, :, 256 * q : 256 * q + 256] = turned[32 * owner : 32 * owner + 32]

    def final_rows(w):
        again[w].wait()
        v = N[w, 0:SL, :].astype(F32)
        mine = rows(SL * s, SL)
        for t in (1, 0):
            share_got(w, t, y)
            link.copy("sy", 2 * w + t, 4, YR.at[w, t], YR.at[w, t], core).wait_recv()
        value = (
            A[w, mine, :].astype(F32)
            + X[w, rows(SL * y, SL), :].astype(F32)
            + YR[w, 0].astype(F32)
        )
        A[w, mine, :] = (v + value + PR[2:3, :]).astype(BF)
        d = (
            H[w, mine, :].astype(F32)
            + X[w, rows(SL * (2 + y), SL), :].astype(F32)
            + YR[w, 1].astype(F32)
        )
        v = v - jnp.mean(v, axis=-1, keepdims=True)
        scale = lax.rsqrt(jnp.mean(v * v, axis=-1, keepdims=True) + norm_eps)
        v = v * scale
        d = d * PR[0:1, :]
        d = d - jnp.mean(d, axis=-1, keepdims=True) - v * jnp.mean(d * v, axis=-1, keepdims=True)
        grad_in[...] = G[w, mine, :].astype(F32) + scale * d
        write(A.at[w, own], out_hbm.at[w])
        return write(grad_in, grad_in_hbm.at[w])

    first_i(chunk(3))
    first_o(chunk(0))
    first_o(chunk(1))
    second_z(chunk(0))
    first_rows = final_rows(0)
    first_o(chunk(2))
    final_i()
    to_seq("swi", SWI, RWI)
    second_z(chunk(1))
    tail_x()
    from_seq("swq", RWQ)
    got = [RWQ[r].astype(F32) for r in range(4)]
    place_of = {}
    for r in range(4):
        for j in range(4):
            for kind in range(3):
                place_of[3 * head_of(r, j) + kind] = (got[r], 384 * (j // 2) + 128 * kind + 64 * (j % 2))
    for at in range(24):
        grad_q[:, 128 * at : 128 * at + 128] = halves(place_of[2 * at], place_of[2 * at + 1])
    write(grad_q, grad_q_hbm)
    first_rows.wait()
    final_rows(1)
    link.copy("tx", 0, 1, XT, XT, core).wait_recv()
    total_t = ZT[0, xx].astype(F32) + XT[...].astype(F32)
    turned_t = jnp.concatenate([total_t, jnp.zeros((112, 128), F32)], axis=0).T.astype(BF)
    for owner in range(4):
        SWT[owner] = turned_t[32 * owner : 32 * owner + 32]
    to_seq("swt", SWT, RWT)
    first_o(chunk(3))
    final_o()
    write(dqT, grad_o_hbm)
    from_seq("swi", RWI)
    for r in range(4):
        for blk in range(8):
            at = 512 * blk + 128 * r
            oT[32 * (at // 1024) : 32 * (at // 1024) + 32, at % 1024 : at % 1024 + 128] = RWI[
                r, :, 128 * blk : 128 * blk + 128
            ].astype(F32)
    for q in range(4):
        write(oT.at[32 * q : 32 * q + 32], grad_i_hbm.at[:, 1024 * q : 1024 * q + 1024])

    from_seq("swt", RWT)
    mine = RWT[0].astype(F32)
    summed = mine + RWT[1].astype(F32) + RWT[2].astype(F32) + RWT[3].astype(F32)
    summed = jnp.where(lane == 2, mine, summed)
    summed = jnp.concatenate([summed, jnp.zeros((96, 128), F32)], axis=0).T
    grad_small[...] = jnp.where(lax.broadcasted_iota(jnp.int32, (8, 128), 0) < 3, summed[0:8], total_t[0:8])
    write(grad_small, grad_small_hbm)

    for make in pending:
        make().wait_send()
    seq_left("prms", lambda owner: prm_block(s), lambda: prm_block(s))
    seq_left("wqs", lambda owner: PWQ.at[owner], lambda: wq_block(s))
    seq_left("swi", lambda owner: SWI.at[owner], lambda: RWI.at[s])
    seq_left("swq", lambda owner: SWQ.at[owner], lambda: RWQ.at[s])
    seq_left("swt", lambda owner: SWT.at[owner], lambda: RWT.at[s])
    for name, (parts, _) in gathers.items():
        for u in range(parts):
            gather_left(name, u)
    for w in range(2):
        rows_left("g", G, w)
    for q in range(4):
        link.copy("ox", q, 4, GO.at[q, ox], XO.at[q], xpart).wait_send()
        link.copy("ix", q, 4, GI.at[q, ox], XI.at[q], xpart).wait_send()
    z_left()
    for w in range(2):
        for t in range(2):
            for yy in range(2):
                src = shares[t].at[w, rows(SL * (2 * yy + oc), SL)]
                dst = X.at[w, rows(SL * (2 * t + yy), SL)]
                link.copy("sc", 4 * w + 2 * t + yy, 8, src, dst, core).wait_send()
            src = shares[t].at[w, rows(SL * (2 * oy + c), SL)]
            link.copy("sy", 2 * w + t, 4, src, YR.at[w, t], ypart).wait_send()
    for e in range(6):
        link.copy("qx", e, 6, GQ.at[e, ox], XQ.at[e], xpart).wait_send()
    for p in range(2):
        ga_c(p).wait_send()
        ga_x(p).wait_send()
    for cp in written:
        if cp is not first_rows:
            cp.wait()


def publish(*refs):
    sources, small, targets, row_targets = refs[:6], refs[6], refs[7:13], refs[13:17]
    held, (in_sems, out_sems) = refs[17:23], refs[23:]
    arrive = [
        pltpu.make_async_copy(sources[i], held[i], in_sems.at[i]) for i in range(6)
    ]
    leave = [
        pltpu.make_async_copy(held[i], targets[i], out_sems.at[i]) for i in range(6)
    ]
    for cp in arrive:
        cp.start()
    for i, target in enumerate(row_targets):
        target[...] = small[i : i + 1, 0 : target.shape[1]]
    for i in range(6):
        arrive[i].wait()
        leave[i].start()
    for cp in leave:
        cp.wait()


def turn_tables(seq_len):
    inverse = 10000.0 ** (-2.0 * np.arange(ROTARY // 2) / ROTARY)
    angles = np.arange(seq_len)[:, None] * inverse[None, :]
    cosine = np.ones((seq_len, HD), np.float32)
    sine = np.zeros((seq_len, HD), np.float32)
    cosine[:, 0:ROTARY:2] = cosine[:, 1:ROTARY:2] = np.cos(angles)
    sine[:, 0:ROTARY:2] = -np.sin(angles)
    sine[:, 1:ROTARY:2] = np.sin(angles)
    return np.concatenate([cosine, sine], axis=1)


def fused_shards(inputs, ends, ln_gain, ln_bias, w_qkv, w_attn, w_in, b_in, w_out, b_out, cotangent):
    def widen(v):
        return jnp.pad(v, (0, 128 - v.shape[0]))

    prm = jnp.pad(jnp.stack([widen(ln_gain), widen(ln_bias), widen(b_out), b_in]), ((0, 12), (0, 0)))
    in_vmem = pl.BlockSpec(memory_space=pltpu.VMEM)
    in_any = pl.BlockSpec(memory_space=pl.ANY)
    rows_type = (2, 1024, 1024)
    shapes = (
        jax.ShapeDtypeStruct((2, 256, 1024), BF),
        jax.ShapeDtypeStruct((2, 256, 1024), F32),
        jax.ShapeDtypeStruct((32, 3072), F32),
        jax.ShapeDtypeStruct((32, 1024), F32),
        jax.ShapeDtypeStruct((32, 4096), F32),
        jax.ShapeDtypeStruct((128, 1024), F32),
    )
    results = pl.pallas_call(
        fused_layer,
        out_shape=shapes + (jax.ShapeDtypeStruct((8, 128), F32),),
        in_specs=[pl.BlockSpec(memory_space=pltpu.SMEM)] + [in_vmem] * 6 + [in_any] * 2,
        out_specs=(in_any,) * 7,
        scratch_shapes=[
            pltpu.VMEM(rows_type, BF),
            pltpu.VMEM(rows_type, BF),
            pltpu.VMEM(rows_type, BF),
            pltpu.VMEM(rows_type, BF),
            pltpu.VMEM(rows_type, BF),
            pltpu.VMEM((1024, 1024), BF),
            pltpu.VMEM((1024, 1024), BF),
            pltpu.VMEM((1024, 768), BF),
            pltpu.VMEM((4, 2, 32, 1024), BF),
            pltpu.VMEM((4, 2, 32, 1024), BF),
            pltpu.VMEM((4, 32, 1024), BF),
            pltpu.VMEM((4, 32, 768), BF),
            pltpu.VMEM((4, 16, 128), BF),
            pltpu.VMEM((8, 16, 128), BF),
            pltpu.VMEM((8, 1024), F32),
            pltpu.VMEM((2, 1024, 768), BF),
            pltpu.VMEM((2, 1024, 256), BF),
            pltpu.VMEM((2, 1024, 256), BF),
            pltpu.VMEM((4, 2, 128, 1024), BF),
            pltpu.VMEM((4, 128, 1024), BF),
            pltpu.VMEM((2, 128, 1024), BF),
            pltpu.VMEM((2, 128, 1024), BF),
            pltpu.VMEM((4, 2, 4, 256, 128), BF),
            pltpu.VMEM((4, 4, 256, 128), BF),
            pltpu.VMEM((3, 4, 256, 128), BF),
            pltpu.VMEM((6, 2, 4, 128, 128), BF),
            pltpu.VMEM((6, 4, 128, 128), BF),
            pltpu.VMEM((6, 3, 128, 128), BF),
            pltpu.VMEM((2, 4, 32, 1024), BF),
            pltpu.VMEM((4, 32, 1024), BF),
            pltpu.VMEM((3, 32, 1024), BF),
            pltpu.VMEM((2, 4, 16, 128), BF),
            pltpu.VMEM((16, 128), BF),
            pltpu.VMEM((3, 2, 16, 128), BF),
            pltpu.VMEM((2, 2, 256, 1024), BF),
            pltpu.VMEM((4, 32, 1024), BF),
            pltpu.VMEM((4, 32, 1024), BF),
            pltpu.VMEM((4, 32, 768), BF),
            pltpu.VMEM((4, 32, 768), BF),
            pltpu.VMEM((4, 32, 128), BF),
            pltpu.VMEM((4, 32, 128), BF),
            pltpu.VMEM((16, 1024), F32),
            pltpu.VMEM((2, 1024, 128), BF),
            pltpu.VMEM((128, 1024), BF),
            pltpu.VMEM((128, 1024), BF),
            pltpu.VMEM((128, 1024), BF),
            pltpu.VMEM((128, 1024), F32),
            pltpu.VMEM((128, 1024), F32),
            pltpu.VMEM((1024, 128), F32),
            pltpu.VMEM((1024, 128), F32),
            pltpu.VMEM((256, 1024), F32),
            pltpu.VMEM((32, 3072), F32),
            pltpu.VMEM((32, 1024), F32),
            pltpu.VMEM((8, 128), F32),
            pltpu.SemaphoreType.DMA((200,)),
            pltpu.SemaphoreType.DMA((200,)),
            pltpu.SemaphoreType.DMA((6,)),
            pltpu.SemaphoreType.DMA((14,)),
        ],
        compiler_params=pltpu.CompilerParams(
            collective_id=0, has_side_effects=True, vmem_limit_bytes=65400 * 2**10
        ),
        cost_estimate=pl.CostEstimate(flops=46 * 10**9, bytes_accessed=10**7, transcendentals=10**7),
    )(ends, prm, w_qkv, w_attn, w_in, w_out, turn_tables(1024), inputs, cotangent)
    row = jax.ShapeDtypeStruct((1, 32), F32)
    final = pl.pallas_call(
        publish,
        out_shape=shapes + (row, row, row, jax.ShapeDtypeStruct((1, 128), F32)),
        in_specs=[in_any] * 6 + [in_vmem],
        out_specs=(in_any,) * 6 + (in_vmem,) * 4,
        scratch_shapes=[pltpu.VMEM(v.shape, v.dtype) for v in shapes]
        + [pltpu.SemaphoreType.DMA((6,)), pltpu.SemaphoreType.DMA((6,))],
        compiler_params=pltpu.CompilerParams(vmem_limit_bytes=60 * 2**20),
    )(*results)
    out, grad_in, grad_q, grad_a, grad_i, grad_o, bias, gain, bias_out, bias_in = final
    return (
        out,
        grad_in,
        gain.reshape(32),
        bias.reshape(32),
        grad_q,
        grad_a,
        grad_i,
        bias_in.reshape(128),
        grad_o,
        bias_out.reshape(32),
    )


def fits_fused(mesh):
    return mesh.shape["batch"] == 8 and mesh.shape["seq"] == 4


def solution(mesh):
    return jax.shard_map(
        fused_shards if fits_fused(mesh) else shards,
        mesh=mesh,
        in_specs=(
            P("batch", "seq", None),
            P("batch"),
            P(("batch", "seq")),
            P(("batch", "seq")),
            P(("batch", "seq"), None),
            P(("batch", "seq"), None),
            P(("batch", "seq"), None),
            P(("batch", "seq")),
            P(("batch", "seq"), None),
            P(("batch", "seq")),
            P("batch", "seq", None),
        ),
        out_specs=(
            P("batch", "seq", None),
            P("batch", "seq", None),
            P(("batch", "seq")),
            P(("batch", "seq")),
            P(("batch", "seq"), None),
            P(("batch", "seq"), None),
            P(("batch", "seq"), None),
            P(("batch", "seq")),
            P(("batch", "seq"), None),
            P(("batch", "seq")),
        ),
        check_vma=False,
    )
```

```python
import math

import jax
import jax.numpy as jnp
import numpy as np
from jax import lax
from jax.experimental import pallas as pl
from jax.experimental.pallas import tpu as pltpu
from jax.sharding import PartitionSpec as P

HEADS = 16
HD = 64
ROTARY = 32
MICRO = 2


norm_eps = 1e-05
gelu_factor = 0.7978845608028654
masked_score = -1e30


def gelu_tanh(values):
    return (
        0.5
        * values
        * (1.0 + jnp.tanh(gelu_factor * (values + 0.044715 * values * values * values)))
    )


def layer_norm(row_values, norm_gain, norm_shift):
    average = jnp.mean(row_values, axis=-1, keepdims=True)
    centered = row_values - average
    variance = jnp.mean(centered * centered, axis=-1, keepdims=True)
    return centered * lax.rsqrt(variance + norm_eps) * norm_gain + norm_shift


def rotary_tables(positions):
    pair_index = jnp.arange(ROTARY // 2, dtype=jnp.float32)
    inverse = 10000.0 ** (-2.0 * pair_index / ROTARY)
    angles = positions[:, None] * inverse[None, :]
    return (jnp.cos(angles), jnp.sin(angles))


def rotate(vectors, cosine, sine_table):
    rotated = vectors[..., :ROTARY]
    even_part = rotated[..., 0::2]
    odd_part = rotated[..., 1::2]
    cosine_wide = cosine[:, None, :]
    sine_wide = sine_table[:, None, :]
    new_even = even_part * cosine_wide - odd_part * sine_wide
    new_odd = odd_part * cosine_wide + even_part * sine_wide
    merged = jnp.stack([new_even, new_odd], axis=-1).reshape(rotated.shape)
    return jnp.concatenate([merged, vectors[..., ROTARY:]], axis=-1)


def visible(query_places, key_places, ending):
    query_after = query_places[:, None] >= ending
    key_after = key_places[None, :] >= ending
    return (key_places[None, :] <= query_places[:, None]) & (query_after == key_after)


def block_scores(block_queries, key_vectors, query_places, key_places, ending, score_scale):
    scores = (
        jnp.einsum("qhd,khd->hqk", block_queries, key_vectors, preferred_element_type=jnp.float32)
        * score_scale
    )
    return jnp.where(visible(query_places, key_places, ending)[None], scores, masked_score)


def attend_forward(packed, ending):
    seq_len, head_count, triple = packed.shape
    head_size = triple // 3
    block_rows = min(512, seq_len)
    score_scale = 1.0 / math.sqrt(head_size)
    queries = packed[:, :, :head_size]
    key_vectors = packed[:, :, head_size : 2 * head_size]
    values = packed[:, :, 2 * head_size :]
    key_places = jnp.arange(seq_len, dtype=jnp.int32)

    def one_block(block_index):
        first_row = block_index * block_rows
        block_queries = lax.dynamic_slice_in_dim(queries, first_row, block_rows, 0)
        query_places = first_row + jnp.arange(block_rows, dtype=jnp.int32)
        scores = block_scores(
            block_queries, key_vectors, query_places, key_places, ending, score_scale
        )
        row_peak = jnp.max(scores, axis=-1, keepdims=True)
        weights = jnp.exp(scores - row_peak)
        row_total = jnp.sum(weights, axis=-1, keepdims=True)
        probabilities = (weights / row_total).astype(jnp.bfloat16)
        result = jnp.einsum(
            "hqk,khd->qhd", probabilities, values, preferred_element_type=jnp.float32
        )
        return (result.astype(jnp.bfloat16), row_peak, row_total)

    results, peaks, totals = lax.map(one_block, jnp.arange(seq_len // block_rows, dtype=jnp.int32))
    return (results.reshape(seq_len, head_count, head_size), peaks, totals)


def attend_backward(packed, d_attended, peaks, totals, ending, full_cosine, full_sine):
    seq_len, head_count, triple = packed.shape
    head_size = triple // 3
    block_rows = min(512, seq_len)
    score_scale = 1.0 / math.sqrt(head_size)
    queries = packed[:, :, :head_size]
    key_vectors = packed[:, :, head_size : 2 * head_size]
    values = packed[:, :, 2 * head_size :]
    key_places = jnp.arange(seq_len, dtype=jnp.int32)

    def one_block(running, block_inputs):
        key_grads, value_grads = running
        block_index, row_peak, row_total = block_inputs
        first_row = block_index * block_rows
        block_queries = lax.dynamic_slice_in_dim(queries, first_row, block_rows, 0)
        block_grads = lax.dynamic_slice_in_dim(d_attended, first_row, block_rows, 0)
        query_places = first_row + jnp.arange(block_rows, dtype=jnp.int32)
        scores = block_scores(
            block_queries, key_vectors, query_places, key_places, ending, score_scale
        )
        probabilities = jnp.exp(scores - row_peak) / row_total
        rounded_probs = probabilities.astype(jnp.bfloat16)
        d_probs = jnp.einsum(
            "qhd,khd->hqk", block_grads, values, preferred_element_type=jnp.float32
        )
        row_dot = jnp.sum(probabilities * d_probs, axis=-1, keepdims=True)
        d_scores = (probabilities * (d_probs - row_dot)).astype(jnp.bfloat16)
        query_grads = (
            jnp.einsum("hqk,khd->qhd", d_scores, key_vectors, preferred_element_type=jnp.float32)
            * score_scale
        )
        key_grads = (
            key_grads
            + jnp.einsum(
                "hqk,qhd->khd", d_scores, block_queries, preferred_element_type=jnp.float32
            )
            * score_scale
        )
        value_grads = value_grads + jnp.einsum(
            "hqk,qhd->khd", rounded_probs, block_grads, preferred_element_type=jnp.float32
        )
        return ((key_grads, value_grads), query_grads)

    zero_sums = jnp.zeros((seq_len, head_count, head_size), jnp.float32)
    block_ids = jnp.arange(seq_len // block_rows, dtype=jnp.int32)
    (key_grads, value_grads), query_grads = lax.scan(
        one_block, (zero_sums, zero_sums), (block_ids, peaks, totals)
    )
    query_grads = query_grads.reshape(seq_len, head_count, head_size)
    flipped_sine = -full_sine
    combined = jnp.stack(
        [
            rotate(query_grads, full_cosine, flipped_sine),
            rotate(key_grads, full_cosine, flipped_sine),
            value_grads,
        ],
        axis=2,
    )
    return combined.astype(jnp.bfloat16).reshape(seq_len, head_count, triple)


def collect(ln_gain, ln_bias, w_qkv, w_attn, w_in, b_in, w_out, b_out):
    return (
        lax.all_gather(ln_gain, ("batch", "seq"), axis=0, tiled=True),
        lax.all_gather(ln_bias, ("batch", "seq"), axis=0, tiled=True),
        lax.all_gather(w_qkv, ("batch", "seq"), axis=0, tiled=True),
        lax.all_gather(w_attn, ("batch", "seq"), axis=0, tiled=True),
        lax.all_gather(w_in, ("batch", "seq"), axis=0, tiled=True),
        lax.all_gather(b_in, ("batch", "seq"), axis=0, tiled=True),
        lax.all_gather(w_out, ("batch", "seq"), axis=0, tiled=True),
        lax.all_gather(b_out, ("batch", "seq"), axis=0, tiled=True),
    )


def reduce_grads(gradients):
    return (
        lax.psum_scatter(gradients[0], ("batch", "seq"), scatter_dimension=0, tiled=True),
        lax.psum_scatter(gradients[1], ("batch", "seq"), scatter_dimension=0, tiled=True),
        lax.psum_scatter(gradients[2], ("batch", "seq"), scatter_dimension=0, tiled=True),
        lax.psum_scatter(gradients[3], ("batch", "seq"), scatter_dimension=0, tiled=True),
        lax.psum_scatter(gradients[4], ("batch", "seq"), scatter_dimension=0, tiled=True),
        lax.psum_scatter(gradients[5], ("batch", "seq"), scatter_dimension=0, tiled=True),
        lax.psum_scatter(gradients[6], ("batch", "seq"), scatter_dimension=0, tiled=True),
        lax.psum_scatter(gradients[7], ("batch", "seq"), scatter_dimension=0, tiled=True),
    )


def shards(inputs, ends, ln_gain, ln_bias, w_qkv, w_attn, w_in, b_in, w_out, b_out, cotangent):
    seq_devices = lax.axis_size("seq")
    windows, local_len, model_width = inputs.shape
    seq_len = local_len * seq_devices
    per_micro = windows // MICRO
    offset = lax.axis_index("seq") * local_len
    cosine, sine_table = rotary_tables(
        (offset + jnp.arange(local_len, dtype=jnp.int32)).astype(jnp.float32)
    )
    full_cosine, full_sine = rotary_tables(jnp.arange(seq_len, dtype=jnp.float32))
    outputs = []
    input_grads = []
    shard_sums = None
    for micro_index in range(MICRO):
        gathered = collect(ln_gain, ln_bias, w_qkv, w_attn, w_in, b_in, w_out, b_out)
        (
            gain_full,
            shift_full,
            qkv_full,
            attn_full,
            in_full,
            bias_in_full,
            out_full,
            bias_out_full,
        ) = gathered
        lower = micro_index * per_micro
        row_values = inputs[lower : lower + per_micro].astype(jnp.float32)
        grad_rows = cotangent[lower : lower + per_micro]
        window_ends = ends[lower : lower + per_micro]
        normed_f, norm_pull = jax.vjp(
            layer_norm, row_values, gain_full.astype(jnp.float32), shift_full.astype(jnp.float32)
        )
        normed = normed_f.astype(jnp.bfloat16)
        projected = jnp.einsum("pld,de->ple", normed, qkv_full, preferred_element_type=jnp.float32)
        arranged = projected.reshape(per_micro, local_len, HEADS, 3, HD)
        query_rot = rotate(arranged[:, :, :, 0], cosine, sine_table)
        key_rot = rotate(arranged[:, :, :, 1], cosine, sine_table)
        packed = jnp.stack([query_rot, key_rot, arranged[:, :, :, 2]], axis=3).astype(jnp.bfloat16)
        packed = packed.reshape(per_micro, local_len, HEADS, 3 * HD)
        head_view = lax.all_to_all(packed, "seq", split_axis=2, concat_axis=1, tiled=True)
        attended, peaks, totals = lax.map(
            lambda bundle: attend_forward(bundle[0], bundle[1]), (head_view, window_ends)
        )
        position_view = lax.all_to_all(
            attended, "seq", split_axis=1, concat_axis=2, tiled=True
        ).reshape(per_micro, local_len, model_width)
        branch_attn = jnp.einsum(
            "ple,ed->pld", position_view, attn_full, preferred_element_type=jnp.float32
        )
        hidden = jnp.einsum(
            "pld,di->pli", normed, in_full, preferred_element_type=jnp.float32
        ) + bias_in_full.astype(jnp.float32)
        activ_f, gelu_pull = jax.vjp(gelu_tanh, hidden)
        activated = activ_f.astype(jnp.bfloat16)
        branch_mlp = jnp.einsum(
            "pli,id->pld", activated, out_full, preferred_element_type=jnp.float32
        ) + bias_out_full.astype(jnp.float32)
        outputs.append((row_values + branch_attn + branch_mlp).astype(jnp.bfloat16))
        grad_b_out = jnp.sum(grad_rows.astype(jnp.float32), axis=(0, 1))
        grad_w_out = jnp.einsum(
            "pli,pld->id", activated, grad_rows, preferred_element_type=jnp.float32
        )
        d_activated = jnp.einsum(
            "pld,id->pli", grad_rows, out_full, preferred_element_type=jnp.float32
        )
        d_hidden = gelu_pull(d_activated)[0].astype(jnp.bfloat16)
        grad_b_in = jnp.sum(d_hidden.astype(jnp.float32), axis=(0, 1))
        grad_w_in = jnp.einsum("pld,pli->di", normed, d_hidden, preferred_element_type=jnp.float32)
        grad_w_attn = jnp.einsum(
            "ple,pld->ed", position_view, grad_rows, preferred_element_type=jnp.float32
        )
        d_attended = jnp.einsum(
            "pld,ed->ple", grad_rows, attn_full, preferred_element_type=jnp.float32
        ).astype(jnp.bfloat16)
        d_attended = d_attended.reshape(per_micro, local_len, HEADS, HD)
        d_head_view = lax.all_to_all(d_attended, "seq", split_axis=2, concat_axis=1, tiled=True)
        d_packed = lax.map(
            lambda bundle: attend_backward(
                bundle[0], bundle[1], bundle[2], bundle[3], bundle[4], full_cosine, full_sine
            ),
            (head_view, d_head_view, peaks, totals, window_ends),
        )
        d_projected = lax.all_to_all(
            d_packed, "seq", split_axis=1, concat_axis=2, tiled=True
        ).reshape(per_micro, local_len, 3 * model_width)
        grad_w_qkv = jnp.einsum(
            "pld,ple->de", normed, d_projected, preferred_element_type=jnp.float32
        )
        d_normed = jnp.einsum("pli,di->pld", d_hidden, in_full, preferred_element_type=jnp.float32)
        d_normed = d_normed + jnp.einsum(
            "ple,de->pld", d_projected, qkv_full, preferred_element_type=jnp.float32
        )
        d_rows, grad_gain, grad_shift = norm_pull(d_normed)
        input_grads.append(grad_rows.astype(jnp.float32) + d_rows)
        local_grads = (
            grad_gain,
            grad_shift,
            grad_w_qkv,
            grad_w_attn,
            grad_w_in,
            grad_b_in,
            grad_w_out,
            grad_b_out,
        )
        reduced = reduce_grads(local_grads)
        if shard_sums is None:
            shard_sums = reduced
        else:
            shard_sums = tuple((running + extra for running, extra in zip(shard_sums, reduced)))
    output = jnp.concatenate(outputs, axis=0)
    grad_inputs = jnp.concatenate(input_grads, axis=0)
    return (
        output,
        grad_inputs,
        shard_sums[0],
        shard_sums[1],
        shard_sums[2],
        shard_sums[3],
        shard_sums[4],
        shard_sums[5],
        shard_sums[6],
        shard_sums[7],
    )


HB, SB = 4, 4
NEG = -1e30
BF, F32 = jnp.bfloat16, jnp.float32
MESH = pl.DeviceIdType.MESH


def dot(a, b, ca, cb):
    return lax.dot_general(a, b, (((ca,), (cb,)), ((), ())), preferred_element_type=F32)


def rows(start, size):
    return pl.ds(pl.multiple_of(start, size), size)


def lanes(start, size=128):
    return pl.ds(pl.multiple_of(start, size), size)


def halves(low_source, high_source):
    def piece(source, upper):
        array, first = source
        tile = array[:, first // 128 * 128 : first // 128 * 128 + 128]
        return pltpu.roll(tile, 64, 1) if (first % 128 == 64) != upper else tile

    lane = lax.broadcasted_iota(jnp.int32, (1, 128), 1)
    return jnp.where(lane < 64, piece(low_source, False), piece(high_source, True))


def head_of(owner, j):
    return 4 * j + 2 * (owner % 2) + owner // 2


class Link:
    def __init__(self, send_sems, recv_sems):
        self.send_sems, self.recv_sems = send_sems, recv_sems
        self.first = {}
        self.used = 0

    def index(self, name, at, count):
        if name not in self.first:
            self.first[name] = self.used
            self.used += count
        return self.first[name] + at

    def copy(self, name, at, count, src, dst, device):
        i = self.index(name, at, count)
        return pltpu.make_async_remote_copy(
            src_ref=src,
            dst_ref=dst,
            send_sem=self.send_sems.at[i],
            recv_sem=self.recv_sems.at[i],
            device_id=device,
            device_id_type=MESH,
        )


def gelu_pair(v):
    square = v * v
    half = 0.5 + 0.5 * jnp.tanh(v * (gelu_factor + (gelu_factor * 0.044715) * square))
    value = v * half
    return value, half + (value - value * half) * (
        2.0 * gelu_factor + (6.0 * gelu_factor * 0.044715) * square
    )


def fused_layer(
    ends, gain, bias, bias_out, bias_in, wq, wa, wi, wo, turns, x_in, g_in,
    out_hbm, grad_in_hbm, grad_q_hbm, grad_a_hbm, grad_i_hbm, grad_o_hbm, grad_small_hbm,
    X, N, G, A, H, Wi, Wo, Wq, WaAll, Wa, PWI, PWQ, PRS, PRM, PR, QKV, att, dO,
    GO, XO, ZO, CO, GI, XI, ZN, ZF, ZD, CI, GQ, XQ, ZQ, CQ, GA, XA, ZA, CA, GT, XT, ZT,
    YR, SWI, RWI, SWQ, RWQ, SWT, RWT, TAIL,
    khat, ktT, vtT, doT, oT, dqT, dkA, dvA,
    grad_in, grad_q, grad_a, grad_small,
    send_sems, recv_sems, local_sems, out_sems,
):
    b = lax.axis_index("batch")
    s = lax.axis_index("seq")
    z, xx = b // 2, b % 2
    y, c = s // 2, s % 2
    oc, ox, oy = 1 - c, 1 - xx, 1 - y
    SL = 256
    S = 1024
    core = (b, 2 * y + oc)
    ypart = (b, 2 * oy + c)
    diag = (b, 2 * oy + oc)
    xpart = (2 * z + ox, s)

    def zdev(k):
        return (2 * ((z + k) % 4) + xx, s)

    def zfrom(k):
        return (z + 4 - k) % 4

    link = Link(send_sems, recv_sems)
    pending = []

    def start(make):
        make().start()
        pending.append(make)

    barrier = pltpu.get_barrier_semaphore()
    others = [xpart] + [zdev(k) for k in (1, 2, 3)]
    others += [(2 * ((z + k) % 4) + ox, s) for k in (1, 2, 3)]
    partners = [core, ypart, diag] + others
    for device in partners:
        pl.semaphore_signal(barrier, inc=1, device_id=device, device_id_type=MESH)

    own = rows(SL * s, SL)
    locals_ = []
    for w in range(2):
        locals_.append(pltpu.make_async_copy(x_in.at[w], X.at[w, own], local_sems.at[3 * w]))
        locals_.append(pltpu.make_async_copy(g_in.at[w], G.at[w, own], local_sems.at[3 * w + 1]))
    for cp in locals_:
        cp.start()

    for r in range(SB):
        for blk in range(8):
            PWI[r, :, 128 * blk : 128 * blk + 128] = wi[:, 512 * blk + 128 * r : 512 * blk + 128 * r + 128]
    TAIL[...] = jnp.zeros_like(TAIL)
    for i, values in enumerate((gain, bias, bias_out, bias_in)):
        TAIL[i : i + 1, 0 : values.shape[1]] = values[...].astype(F32)
    tile = TAIL[:, 0:128]
    row = lax.broadcasted_iota(jnp.int32, (16, 128), 0)
    tile = jnp.where(row < 3, pltpu.roll(tile, 32 * s, 1), tile)
    PRS[s] = tile.astype(BF)
    Wi[rows(128 * b + 32 * s, 32), :] = PWI[s]
    Wo[rows(128 * b, 128), :] = wo[...]
    WaAll[z, xx] = wa[...]

    wq_f = wq[...].astype(F32)
    for r in range(SB):
        for kind in range(3):
            for p in range(2):
                lo = 192 * head_of(r, 2 * p) + 64 * kind
                hi = 192 * head_of(r, 2 * p + 1) + 64 * kind
                at = 384 * p + 128 * kind
                PWQ[r, :, at : at + 128] = halves((wq_f, lo), (wq_f, hi)).astype(BF)
    Wq[rows(128 * b + 32 * s, 32), :] = PWQ[s]

    pl.semaphore_wait(barrier, len(partners))

    def seq_sends(name, src_of, dst):
        for i, (device, owner) in enumerate(
            ((core, 2 * y + oc), (ypart, 2 * oy + c), (diag, 2 * oy + oc))
        ):
            link.copy(name, i, 3, src_of(owner), dst(), device).start()

    def seq_left(name, src_of, dst):
        for i, (device, owner) in enumerate(
            ((core, 2 * y + oc), (ypart, 2 * oy + c), (diag, 2 * oy + oc))
        ):
            link.copy(name, i, 3, src_of(owner), dst(), device).wait_send()

    def seq_waits(name, src, dst_of):
        for i, owner in enumerate((2 * y + oc, 2 * oy + c, 2 * oy + oc)):
            link.copy(name, i, 3, src, dst_of(owner), core).wait_recv()

    def prm_block(owner):
        return PRS.at[owner]

    def wi_block(owner, u):
        return Wi.at[rows(128 * b + 32 * owner, 32), 256 * u : 256 * u + 256]

    def wq_block(owner):
        return Wq.at[rows(128 * b + 32 * owner, 32)]

    gathers = {
        "wi": (4, lambda bb, u: Wi.at[rows(128 * bb, 128), lanes(256 * u, 256)]),
        "wo": (2, lambda bb, u: Wo.at[rows(128 * bb + 64 * u, 64)]),
        "wq": (2, lambda bb, u: Wq.at[rows(128 * bb, 128), 384 * u : 384 * u + 384]),
        "wa": (1, lambda bb, u: WaAll.at[bb // 2, bb % 2]),
    }
    pair = z + 1 - 2 * (z % 2)

    def gather_copy(name, way, at, count, zz, side, u, device):
        held = gathers[name][1](2 * zz + side, u)
        return link.copy(name + way, count * u + at, count * gathers[name][0], held, held, device)

    by_line = ("wi", "wo")

    def up_copy(name, zz, u):
        return gather_copy(name, "l", zz, 5, zz, xx, u, (2 * (z + 1) + xx, s))

    def down_copy(name, zz, u):
        return gather_copy(name, "l", zz + 1, 5, zz, xx, u, (2 * (z - 1) + xx, s))

    def z_copy(name, zz, k, u):
        return gather_copy(name, "z", k - 1, 3, zz, xx, u, zdev(k))

    def x_copy(name, zz, side, u):
        return gather_copy(name, "x", zz, 4, zz, side, u, xpart)

    def gather_z(name, u):
        if name in by_line:

            @pl.when(z < 3)
            def _():
                up_copy(name, z, u).start()

            @pl.when(z > 0)
            def _():
                down_copy(name, z, u).start()

            return
        for far in (1, 2, 3):

            @pl.when(z + far <= 3)
            def _():
                z_copy(name, z, far, u).start()

            @pl.when(z >= far)
            def _():
                z_copy(name, z, 4 - far, u).start()

    def gather_x(name, u):
        x_copy(name, z, xx, u).start()

    def gather_pass(name, far, u):
        @pl.when(z >= far)
        def _():
            if name in by_line:
                up_copy(name, z - far, u).wait_recv()

                @pl.when(z < 3)
                def _():
                    up_copy(name, z - far, u).start()

            else:
                z_copy(name, z - far, far, u).wait_recv()
            x_copy(name, z - far, xx, u).start()

        @pl.when(z + far <= 3)
        def _():
            if name in by_line:
                down_copy(name, z + far, u).wait_recv()

                @pl.when(z > 0)
                def _():
                    down_copy(name, z + far, u).start()

            else:
                z_copy(name, z + far, 4 - far, u).wait_recv()
            x_copy(name, z + far, xx, u).start()

    def gather_block(name, zz, u):
        x_copy(name, zz, ox, u).wait_recv()

    def gather_end(name, u):
        for zz in range(4):
            gather_block(name, zz, u)

    def gather_left(name, u):
        if name not in by_line:
            for k in (1, 2, 3):
                z_copy(name, z, k, u).wait_send()
        for zz in range(4):
            if name in by_line:

                @pl.when((zz <= z) & (z < 3))
                def _():
                    up_copy(name, zz, u).wait_send()

                @pl.when((zz >= z) & (z > 0))
                def _():
                    down_copy(name, zz, u).wait_send()

            x_copy(name, zz, xx, u).wait_send()

    def rows_start(name, src, dst):
        for w in range(2):
            start(lambda w=w: link.copy(name + "c", w, 2, src.at[w], dst.at[w, own], core))
            start(lambda w=w: link.copy(name + "y", w, 2, src.at[w], dst.at[w, own], ypart))

    def rows_pass(name, dst, w):
        block = dst.at[w, rows(SL * (2 * oy + c), SL)]
        link.copy(name + "y", w, 2, block, block, core).wait_recv()
        link.copy(name + "f", w, 2, block, block, core).start()

    def rows_left(name, dst, w):
        block = dst.at[w, rows(SL * (2 * oy + c), SL)]
        link.copy(name + "f", w, 2, block, block, core).wait_send()

    def rows_end_core(name, dst, w):
        block = dst.at[w, rows(SL * (2 * y + oc), SL)]
        link.copy(name + "c", w, 2, block, block, core).wait_recv()

    def rows_end_far(name, dst, w):
        block = dst.at[w, rows(SL * (2 * oy + oc), SL)]
        link.copy(name + "f", w, 2, block, block, core).wait_recv()

    seq_sends("prms", lambda owner: prm_block(s), lambda: prm_block(s))
    for u in range(4):
        seq_sends(
            "wis%d" % u, lambda owner: PWI.at[owner, :, 256 * u : 256 * u + 256], lambda: wi_block(s, u)
        )
    gather_z("wa", 0)
    gather_x("wa", 0)
    gather_x("wo", 0)
    seq_sends("wqs", lambda owner: PWQ.at[owner], lambda: wq_block(s))
    rows_start("x", x_in, X)
    seq_waits("prms", prm_block(s), prm_block)
    total = PRS[0].astype(F32) + PRS[1].astype(F32) + PRS[2].astype(F32) + PRS[3].astype(F32)
    PRM[b] = jnp.where(row < 3, total, tile).astype(BF)
    for i, device in enumerate(others):
        start(lambda i=i, device=device: link.copy("prm", i, 7, PRM.at[b], PRM.at[b], device))
    for u in range(4):
        seq_waits("wis%d" % u, wi_block(s, u), lambda owner: wi_block(owner, u))
        gather_z("wi", u)
        gather_x("wi", u)
    rows_start("g", g_in, G)
    gather_pass("wi", 1, 0)
    gather_pass("wi", 1, 1)
    for far in (1, 2, 3):
        gather_pass("wa", far, 0)

    for i in range(7):
        k = (0, 1, 2, 3, 1, 2, 3)[i]
        bb = 2 * zfrom(k) + (ox if i in (0, 4, 5, 6) else xx)
        link.copy("prm", i, 7, PRM.at[bb], PRM.at[bb], core).wait_recv()
    for bb in range(8):
        PR[:, 128 * bb : 128 * bb + 128] = PRM[bb].astype(F32)[0:8]

    for cp in locals_:
        cp.wait()

    def norm_rows(w, owner):
        r = rows(SL * owner, SL)
        v = X[w, r, :].astype(F32)
        v = v - jnp.mean(v, axis=-1, keepdims=True)
        var = jnp.mean(v * v, axis=-1, keepdims=True)
        N[w, r, :] = (v * lax.rsqrt(var + norm_eps) * PR[0:1, :] + PR[1:2, :]).astype(BF)

    def norm_near(w, carry):
        norm_rows(w, s)
        norm_rows(w, 2 * y + oc)
        return carry

    def norm_far(w):
        rows_end_far("x", X, w)
        norm_rows(w, 2 * oy + c)
        norm_rows(w, 2 * oy + oc)

    for w in range(2):
        rows_end_core("x", X, w)
    lax.fori_loop(0, 2, norm_near, 0)
    gather_pass("wi", 2, 0)
    gather_pass("wi", 1, 2)
    gather_pass("wi", 1, 3)
    seq_waits("wqs", wq_block(s), wq_block)
    gather_z("wq", 0)
    gather_x("wq", 0)
    gather_pass("wi", 2, 1)
    gather_pass("wi", 3, 0)
    gather_pass("wi", 2, 2)
    gather_pass("wi", 3, 1)
    rows_pass("x", X, 0)
    gather_pass("wi", 2, 3)
    gather_z("wq", 1)
    gather_x("wq", 1)

    def hidden_step(i, carry):
        early = i < 12
        u = jnp.where(early, i // 3, i - 12)
        at = jnp.where(early, i % 3, 3)
        w = at % 2
        t = jnp.where(at < 2, y, oy)

        @pl.when(i == 0)
        def _():
            gather_end("wi", 0)

        @pl.when(i == 2)
        def _():
            norm_far(0)

        @pl.when(i == 3)
        def _():
            gather_pass("wi", 3, 2)
            gather_end("wi", 1)

        @pl.when(i == 5)
        def _():
            gather_pass("wi", 3, 3)
            gather_z("wo", 0)
            gather_z("wo", 1)
            gather_pass("wq", 1, 0)

        @pl.when(i == 6)
        def _():
            gather_end("wi", 2)

        @pl.when(i == 7)
        def _():
            rows_pass("x", X, 1)

        @pl.when(i == 9)
        def _():
            gather_pass("wq", 2, 0)
            gather_end("wi", 3)

        @pl.when(i == 11)
        def _():
            gather_pass("wq", 3, 0)

        @pl.when(i == 12)
        def _():
            norm_far(1)

        @pl.when(i == 14)
        def _():
            gather_pass("wq", 1, 1)
            gather_x("wo", 1)

        r, l = rows(512 * t, 512), lanes(256 * u, 256)
        v = dot(N[w, r, :], Wi[:, l], 1, 0) + PR[3:4, l]
        value, slope = gelu_pair(v)
        A[w, r, l] = value.astype(BF)
        H[w, r, l] = slope.astype(BF)
        return carry

    lax.fori_loop(0, 16, hidden_step, 0)
    for w in range(2):
        rows_left("x", X, w)
    gather_end("wa", 0)
    start(lambda: link.copy("wac", 0, 1, WaAll.at[:, oc], Wa.at[:, c], core))
    Wa[:, c] = WaAll[:, c]
    for far in (2, 3):
        gather_pass("wq", far, 1)
    for u in range(2):
        gather_pass("wo", 1, u)

    def add_into(dst, other):
        dst[...] = (dst[...].astype(F32) + other[...].astype(F32)).astype(BF)

    inner = (z == 1) | (z == 2)

    def far_chip(tt):
        return 2 * (1 - z // 2) + tt

    def zchip(zz):
        return (2 * zz + xx, s)

    def o_near(q):
        return link.copy("op", 0, 1, GO.at[q, xx], ZO.at[0], zchip(pair))

    def o_comb(q):
        return link.copy("oc", q % 2, 2, GO.at[q, xx], CO.at[q % 2], zchip(pair))

    def o_far(q):
        return link.copy("of", q % 2, 2, GO.at[q, xx], ZO.at[1], zchip(q))

    def of_pair(p):
        return lambda: ("q", GQ.at[p], XQ.at[p], ZQ.at[p], CQ.at[p], p, 2)

    def of_attn():
        return "a", GA, XA, ZA, CA, 0, 1

    def z_near(get):
        name, group, _, landed, _, at, count = get()
        return link.copy(name + "p", at, count, group.at[xx, pair], landed.at[0], zchip(pair))

    def z_comb(get, tt):
        name, group, _, _, comb, at, count = get()
        block = group.at[xx, far_chip(tt)]
        return link.copy(name + "c", 2 * at + tt, 2 * count, block, comb.at[tt], zchip(pair))

    def z_far(get, tt, side):
        name, group, _, landed, _, at, count = get()
        block = group.at[xx, far_chip(tt)]
        return link.copy(
            name + "f", 2 * at + side, 2 * count, block, landed.at[1], zchip(far_chip(tt))
        )

    def z_first(get):
        _, group, received, _, _, _, _ = get()
        add_into(group.at[xx, pair], received.at[pair])
        z_near(get).start()
        for tt in range(2):
            add_into(group.at[xx, far_chip(tt)], received.at[far_chip(tt)])

            @pl.when(~inner)
            def _():
                z_comb(get, tt).start()

    def z_second(get):
        @pl.when(inner)
        def _():
            _, group, _, _, comb, _, _ = get()
            for tt in range(2):
                z_comb(get, tt).wait_recv()
                add_into(group.at[xx, far_chip(tt)], comb.at[tt])
                z_far(get, tt, tt).start()

    def z_total(get):
        _, group, received, landed, _, _, _ = get()
        z_near(get).wait_recv()
        z_far(get, 0, z % 2).wait_recv()
        total = group[xx, z].astype(F32) + received[z].astype(F32)
        return total + landed[0].astype(F32) + landed[1].astype(F32)

    def z_gone(get):
        z_near(get).wait_send()
        for tt in range(2):

            @pl.when(inner)
            def _():
                z_far(get, tt, tt).wait_send()

            @pl.when(~inner)
            def _():
                z_comb(get, tt).wait_send()

    def first_o(q):
        o_x(q).wait_recv()

        @pl.when(z != q)
        def _():
            add_into(GO.at[q, xx], XO.at[q])

            @pl.when(q == pair)
            def _():
                o_near(q).start()

            @pl.when((q != pair) & ~inner)
            def _():
                o_comb(q).start()

    def half_chip(tt):
        return 2 * (z // 2) + tt

    def i_near(q):
        return link.copy("ip", q, 4, GI.at[q, xx, pair], ZN.at[q], zchip(pair))

    def i_comb(q, tt):
        block = GI.at[q, xx, far_chip(tt)]
        return link.copy("ic", 2 * (q % 2) + tt, 4, block, CI.at[q % 2, tt], zchip(pair))

    def i_far(q, tt, side):
        block = GI.at[q, xx, far_chip(tt)]
        return link.copy("if", 2 * (q % 2) + side, 4, block, ZF.at[q % 2], zchip(far_chip(tt)))

    def i_straight(q, tt, sender, side):
        block = GI.at[q, xx, far_chip(tt)]
        return link.copy(
            "id", 4 * (q % 2) + 2 * sender + side, 8, block, ZD.at[q % 2, sender], zchip(far_chip(tt))
        )

    def first_i(q, far):
        i_x(q).wait_recv()
        add_into(GI.at[q, xx, pair], XI.at[q, pair])
        i_near(q).start()
        for tt in range(2):
            add_into(GI.at[q, xx, far_chip(tt)], XI.at[q, far_chip(tt)])
            if far:

                @pl.when(~inner)
                def _():
                    i_comb(q, tt).start()

            else:
                i_straight(q, tt, z % 2, tt).start()

    def second_i(q):
        @pl.when(inner)
        def _():
            for tt in range(2):
                i_comb(q, tt).wait_recv()
                add_into(GI.at[q, xx, far_chip(tt)], CI.at[q % 2, tt])
                i_far(q, tt, tt).start()

    def total_i(q, far):
        i_near(q).wait_recv()
        total = GI[q, xx, z].astype(F32) + XI[q, z].astype(F32) + ZN[q].astype(F32)
        if far:
            for sender in range(2):
                i_straight(q, 0, sender, z % 2).wait_recv()
                total = total + ZD[q % 2, sender].astype(F32)
            return total
        i_far(q, 0, z % 2).wait_recv()
        return total + ZF[q % 2].astype(F32)

    def second_z(q):
        @pl.when(inner)
        def _():
            o_comb(q).wait_recv()
            add_into(GO.at[q, xx], CO.at[q % 2])
            o_far(q).start()

    def z_left():
        o_near(pair).wait_send()
        for tt in range(2):

            @pl.when(inner)
            def _():
                o_far(far_chip(tt)).wait_send()

            @pl.when(~inner)
            def _():
                o_comb(far_chip(tt)).wait_send()

        for q in range(4):
            i_near(q).wait_send()
        for a in range(2):
            for tt in range(2):
                i_straight(half_chip(a), tt, z % 2, tt).wait_send()

                @pl.when(inner)
                def _():
                    i_far(far_chip(a), tt, tt).wait_send()

                @pl.when(~inner)
                def _():
                    i_comb(far_chip(a), tt).wait_send()

        for p in range(2):
            z_gone(of_pair(p))
        z_gone(of_attn)

    def chunk(j):
        return jnp.where(j == 3, z, jnp.where(j == 2, pair, far_chip(0) + j))

    def o_x(q):
        return link.copy("ox", q, 4, GO.at[q, ox], XO.at[q], xpart)

    def i_x(q):
        return link.copy("ix", q, 4, GI.at[q, ox], XI.at[q], xpart)

    even = lax.broadcasted_iota(jnp.int32, (1, 128), 1) % 2 == 0

    def turn_rows(r):
        table = turns[r, :]
        other = pltpu.roll(table, 64, 1)
        low = lax.broadcasted_iota(jnp.int32, (1, 128), 1) < 64
        return jnp.where(low, table, other), jnp.where(low, other, table)

    def turn(v, cos_rows, sin_rows):
        swapped = jnp.where(even, pltpu.roll(v, 127, 1), pltpu.roll(v, 1, 1))
        return v * cos_rows + swapped * sin_rows

    def qkv_step(p):
        gather_end("wq", p)
        l = slice(384 * p, 384 * p + 384)

        def step(i, carry):
            w, r = i // 4, rows(256 * (i % 4), 256)
            v = dot(N[w, r, :], Wq[:, l], 1, 0)
            cos_rows, sin_rows = turn_rows(r)
            for kind in range(3):
                tile_v = v[:, 128 * kind : 128 * kind + 128]
                if kind < 2:
                    tile_v = turn(tile_v, cos_rows, sin_rows)
                if kind == 0:
                    tile_v = tile_v * 0.125
                QKV[w, r, 384 * p + 128 * kind : 384 * p + 128 * kind + 128] = tile_v.astype(BF)
            return carry

        lax.fori_loop(0, 8, step, 0)

    qkv_step(0)
    for w in range(2):
        rows_end_core("g", G, w)
    rows_pass("g", G, 0)
    for u in range(4):
        seq_left(
            "wis%d" % u, lambda owner: PWI.at[owner, :, 256 * u : 256 * u + 256], lambda: wi_block(s, u)
        )
    link.copy("wac", 0, 1, WaAll.at[:, oc], Wa.at[:, oc], core).wait_recv()
    TAIL[...] = jnp.zeros_like(TAIL)

    def do_step(w):
        def step(i, total):
            r = rows(512 * i, 512)
            g = G[w, r, :]
            dO[w, r, :] = dot(g, Wa[...].reshape(256, 1024), 1, 1).astype(BF)
            return total + jnp.sum(g.astype(F32), axis=0, keepdims=True)

        TAIL[2:3, :] += lax.fori_loop(0, 2, step, jnp.zeros((1, 1024), F32))

    rows_end_far("g", G, 0)
    do_step(0)
    gather_pass("wo", 2, 0)

    def units_back(j):
        q = chunk(j)
        l = lanes(256 * q, 256)

        def step(i, total):
            w, r = i // 2, rows(512 * (i % 2), 512)
            d = dot(G[w, r, :], Wo[rows(256 * q, 256), :], 1, 1) * H[w, r, l].astype(F32)
            d = d.astype(BF)
            H[w, r, l] = d
            return total + jnp.sum(d.astype(F32), axis=0, keepdims=True)

        TAIL[3:4, l] = lax.fori_loop(0, 4, step, jnp.zeros((1, 256), F32))

    def units_out(j):
        q = chunk(j)
        l = lanes(256 * q, 256)
        go = dot(A[0, :, l], G[0], 0, 0) + dot(A[1, :, l], G[1], 0, 0)
        GO[q, 0] = go[:128].astype(BF)
        GO[q, 1] = go[128:].astype(BF)

    def units_in(j):
        q = chunk(j)
        l = lanes(256 * q, 256)
        gi = dot(H[0, :, l], N[0], 0, 0) + dot(H[1, :, l], N[1], 0, 0)
        for bb in range(8):
            GI[q, bb % 2, bb // 2] = gi[:, 128 * bb : 128 * bb + 128].astype(BF)

    lane = lax.broadcasted_iota(jnp.int32, (1, 128), 1)
    place = lax.broadcasted_iota(jnp.int32, (S, 1), 0)
    BQ = 256
    key_i = lax.broadcasted_iota(jnp.int32, (BQ, BQ), 0)
    query_i = lax.broadcasted_iota(jnp.int32, (BQ, BQ), 1)
    inside = [(lane // 64) == hh for hh in range(2)]
    feature = [lane == (64 - 64 * hh) for hh in range(2)]

    def attend(w, p):
        ending = ends[w]

        def part(kind):
            return lanes(384 * p + 128 * kind)

        pl_ = lanes(128 * p)
        keys = QKV[w, :, part(1)]
        ktT[...] = keys.T
        vtT[...] = QKV[w, :, part(2)].T
        doT[...] = dO[w, :, pl_].T
        dkA[...] = jnp.zeros_like(dkA)
        dvA[...] = jnp.zeros_like(dvA)
        keys_f = keys.astype(F32)
        before = jnp.where(place < ending, NEG, 0.0)
        for hh in range(2):
            khat[hh] = jnp.where(inside[hh], keys_f, jnp.where(feature[hh], before, 0.0)).astype(BF)

        def begin(qb, hh):
            qr, nk = slice(qb * BQ, (qb + 1) * BQ), (qb + 1) * BQ
            q = QKV[w, qr, part(0)].astype(F32)
            after = jnp.where(place[qr] >= ending, 1.0, 0.0)
            q_in = jnp.where(inside[hh], q, 0.0).astype(BF)
            q_hat = jnp.where(inside[hh], q, jnp.where(feature[hh], after, 0.0)).astype(BF)
            d_in = jnp.where(inside[hh], dO[w, qr, pl_].astype(F32), 0.0).astype(BF)
            return dot(khat[hh, 0:nk, :], q_hat, 1, 1), dot(QKV[w, 0:nk, part(2)], d_in, 1, 1), q_in, d_in

        units = [(qb, hh) for qb in range(S // BQ) for hh in range(2)]
        upcoming, late = begin(*units[0]), None
        for i, (qb, hh) in enumerate(units):
            sc, dp, q_in, d_in = upcoming
            qr, nk = slice(qb * BQ, (qb + 1) * BQ), (qb + 1) * BQ
            hr = slice(64 * hh, 64 * hh + 64)
            if i + 1 < len(units):
                upcoming = begin(*units[i + 1])
            last = jnp.where(key_i <= query_i, sc[nk - BQ :], NEG)
            sc = last if qb == 0 else jnp.concatenate([sc[: nk - BQ], last], axis=0)
            e = jnp.exp(sc - jnp.max(sc, axis=0, keepdims=True))
            pn = e * (1.0 / jnp.sum(e, axis=0, keepdims=True))
            pb = pn.astype(BF)
            o = dot(vtT[hr, 0:nk], pb, 1, 0)
            if late is not None:
                late()
            oT[hr, qr] = o
            dd = jnp.sum(o * doT[hr, qr].astype(F32), axis=0, keepdims=True)
            ds = (pn * (dp - dd)).astype(BF)

            def late(hr=hr, qr=qr, nk=nk, ds=ds, pb=pb, q_in=q_in, d_in=d_in):
                dqT[hr, qr] = dot(ktT[hr, 0:nk], ds, 1, 0)
                dkA[0:nk, :] += dot(ds, q_in, 1, 0)
                dvA[0:nk, :] += dot(pb, d_in, 1, 0)

        late()
        cos_rows, sin_rows = turn_rows(slice(None))
        sin_rows = -sin_rows
        att[w, :, pl_] = oT[...].T.astype(BF)
        QKV[w, :, part(0)] = turn(dqT[...].T * 0.125, cos_rows, sin_rows).astype(BF)
        QKV[w, :, part(1)] = turn(dkA[...], cos_rows, sin_rows).astype(BF)
        QKV[w, :, part(2)] = dvA[...].astype(BF)

    shares = (A, H)

    def share_c(w, t, yy):
        src = shares[t].at[w, rows(SL * (2 * yy + oc), SL)]
        dst = X.at[w, rows(SL * (2 * t + yy), SL)]
        link.copy("sc", 4 * w + 2 * t + yy, 8, src, dst, core).start()

    def share_got(w, t, yy):
        slot = X.at[w, rows(SL * (2 * t + yy), SL)]
        link.copy("sc", 4 * w + 2 * t + yy, 8, slot, slot, core).wait_recv()
        return slot

    def share_y(w, t):
        src = shares[t].at[w, rows(SL * (2 * oy + c), SL)]
        add_into(src, share_got(w, t, oy))
        link.copy("sy", 2 * w + t, 4, src, YR.at[w, t], ypart).start()

    def share_out(w, r):
        value = dot(A[w, r, :], Wo[...], 1, 0) + dot(att[w, r, :], Wa[...].reshape(256, 1024), 1, 0)
        A[w, r, :] = value.astype(BF)

    def share_normed(w, r):
        d = dot(H[w, r, :], Wi[...], 1, 1) + dot(QKV[w, r, :], Wq[...], 1, 1)
        H[w, r, :] = d.astype(BF)
        n = (N[w, r, :].astype(F32) - PR[1:2, :]) / PR[0:1, :]
        TAIL[0:1, :] += jnp.sum(d, axis=0, keepdims=True)
        TAIL[1:2, :] += jnp.sum(d * n, axis=0, keepdims=True)

    def share_step(w, t):
        def step(i, carry):
            yy = jnp.where(i < 2, oy, y)
            cc = jnp.where(i % 2 == 0, oc, c)
            (share_out, share_normed)[t](w, rows(SL * (2 * yy + cc), SL))

            @pl.when(i == 0)
            def _():
                share_c(w, t, oy)

            @pl.when(i == 2)
            def _():
                share_y(w, t)
                share_c(w, t, y)

            return carry

        lax.fori_loop(0, 4, step, 0)

    def gq_step(p):
        l = slice(384 * p, 384 * p + 384)
        gq = dot(QKV[0, :, l], N[0], 0, 0) + dot(QKV[1, :, l], N[1], 0, 0)
        for bb in range(8):
            GQ[p, bb % 2, bb // 2] = gq[:, 128 * bb : 128 * bb + 128].astype(BF)
        link.copy("qx", p, 2, GQ.at[p, ox], XQ.at[p], xpart).start()

    def ga_c(p):
        two = slice(2 * p, 2 * p + 2)
        return link.copy("core_a", p, 2, PWI.at[two], GA.at[c, two], core)

    def ga_x(p):
        two = slice(2 * p, 2 * p + 2)
        return link.copy("x_a", p, 2, GA.at[ox, two], XA.at[two], xpart)

    def ga_step(p):
        l = slice(128 * p, 128 * p + 128)
        ga = dot(att[0, :, l], G[0], 0, 0) + dot(att[1, :, l], G[1], 0, 0)
        for j in range(2):
            for cc in range(2):
                piece = ga[64 * j + 32 * cc : 64 * j + 32 * cc + 32].astype(BF)

                @pl.when(cc == c)
                def _():
                    GA[c, 2 * p + j] = piece

                @pl.when(cc != c)
                def _():
                    PWI[2 * p + j] = piece

        ga_c(p).start()

    def ga_send(p):
        ga_c(p).wait_recv()
        ga_x(p).start()

    def first_q(p):
        link.copy("qx", p, 2, GQ.at[p, ox], XQ.at[p], xpart).wait_recv()
        z_first(of_pair(p))

    def first_a():
        for p in range(2):
            ga_x(p).wait_recv()
        z_first(of_attn)

    def attend_step(i, carry):
        w, p = i // 2, i % 2
        attend(w, p)

        @pl.when(i == 0)
        def _():
            gather_pass("wo", 2, 1)
            gather_pass("wo", 3, 0)
            rows_pass("g", G, 1)
            qkv_step(1)
            gather_pass("wo", 3, 1)
            rows_end_far("g", G, 1)
            for j in range(2):
                units_out(j)
                o_x(chunk(j)).start()

        @pl.when(i == 1)
        def _():
            do_step(1)

        @pl.when(i == 2)
        def _():
            gq_step(0)
            ga_step(0)
            for j in range(2, 4):
                units_out(j)
            for u in range(2):
                for zz in range(4):
                    gather_block("wo", zz, u)
            share_step(0, 0)
            first_o(chunk(0))
            first_o(chunk(1))
            ga_send(0)

        return carry

    lax.fori_loop(0, 4, attend_step, 0)
    gq_step(1)
    ga_step(1)

    def in_step(j, carry):
        units_back(j)
        units_in(j)
        i_x(chunk(j)).start()

        @pl.when(j == 0)
        def _():
            z_second(of_pair(0))

        @pl.when(j == 1)
        def _():
            first_q(1)

        @pl.when(j == 2)
        def _():
            first_a()

        return carry

    written = []

    def write(src, dst):
        cp = pltpu.make_async_copy(src, dst, out_sems.at[len(written)])
        cp.start()
        written.append(cp)
        return cp

    def to_seq(name, held, landed):
        landed[s] = held[s]
        seq_sends(name, lambda owner: held.at[owner], lambda: landed.at[s])

    def from_seq(name, landed):
        for i, owner in enumerate((2 * y + oc, 2 * oy + c, 2 * oy + oc)):
            link.copy(name, i, 3, landed.at[owner], landed.at[owner], core).wait_recv()

    second_z(chunk(0))
    first_q(0)
    ga_send(1)
    second_z(chunk(1))
    share_step(1, 0)
    lax.fori_loop(0, 4, in_step, 0)
    for j in range(2, 4):
        o_x(chunk(j)).start()
    z_second(of_pair(1))
    z_second(of_attn)
    first_i(chunk(0), True)
    share_step(0, 1)
    first_i(chunk(1), True)
    second_i(chunk(0))
    share_step(1, 1)
    for p in range(2):
        total_q = z_total(of_pair(p)).T.astype(BF)
        for owner in range(4):
            SWQ[owner, :, 384 * p : 384 * p + 384] = total_q[32 * owner : 32 * owner + 32]
    to_seq("swq", SWQ, RWQ)
    again = [
        pltpu.make_async_copy(x_in.at[w], N.at[w, 0:SL], local_sems.at[3 * w + 2]) for w in range(2)
    ]
    for cp in again:
        cp.start()
    tail = TAIL[...]
    for bb in range(8):
        GT[bb % 2, bb // 2] = tail[:, 128 * bb : 128 * bb + 128].astype(BF)
    for k in (1, 2, 3):
        start(lambda k=k: link.copy("tz", k - 1, 3, GT.at[:, (z + k) % 4], ZT.at[k - 1], zdev(k)))

    def tail_x():
        for k in (1, 2, 3):
            link.copy("tz", k - 1, 3, ZT.at[k - 1], ZT.at[k - 1], core).wait_recv()
        add_into(ZT.at[0], GT.at[:, z])
        add_into(ZT.at[1], ZT.at[2])
        add_into(ZT.at[0], ZT.at[1])
        start(lambda: link.copy("tx", 0, 1, ZT.at[0, ox], XT, xpart))

    def final_o():
        o_near(z).wait_recv()
        link.copy("of", z % 2, 2, ZO.at[1], ZO.at[1], core).wait_recv()
        dqT[...] = (
            GO[z, xx].astype(F32) + XO[z].astype(F32) + ZO[0].astype(F32) + ZO[1].astype(F32)
        )

    def final_i():
        for tt in range(2):
            for q, far in ((half_chip(tt), False), (far_chip(tt), True)):
                turned = total_i(q, far).T.astype(BF)
                for owner in range(4):
                    SWI[owner, :, lanes(256 * q, 256)] = turned[32 * owner : 32 * owner + 32]

    def final_rows(w):
        again[w].wait()
        v = N[w, 0:SL, :].astype(F32)
        mine = rows(SL * s, SL)
        for t in (1, 0):
            share_got(w, t, y)
            link.copy("sy", 2 * w + t, 4, YR.at[w, t], YR.at[w, t], core).wait_recv()
        value = (
            A[w, mine, :].astype(F32)
            + X[w, rows(SL * y, SL), :].astype(F32)
            + YR[w, 0].astype(F32)
        )
        A[w, mine, :] = (v + value + PR[2:3, :]).astype(BF)
        d = (
            H[w, mine, :].astype(F32)
            + X[w, rows(SL * (2 + y), SL), :].astype(F32)
            + YR[w, 1].astype(F32)
        )
        v = v - jnp.mean(v, axis=-1, keepdims=True)
        scale = lax.rsqrt(jnp.mean(v * v, axis=-1, keepdims=True) + norm_eps)
        v = v * scale
        d = d * PR[0:1, :]
        d = d - jnp.mean(d, axis=-1, keepdims=True) - v * jnp.mean(d * v, axis=-1, keepdims=True)
        grad_in[...] = G[w, mine, :].astype(F32) + scale * d
        write(A.at[w, own], out_hbm.at[w])
        return write(grad_in, grad_in_hbm.at[w])

    first_i(chunk(2), False)
    second_i(chunk(1))
    grad_a[...] = z_total(of_attn)
    write(grad_a, grad_a_hbm)
    first_i(chunk(3), False)
    first_o(chunk(2))
    first_rows = final_rows(0)
    tail_x()
    final_i()
    to_seq("swi", SWI, RWI)
    first_rows.wait()
    final_rows(1)
    from_seq("swq", RWQ)
    got = [RWQ[r].astype(F32) for r in range(4)]
    place_of = {}
    for r in range(4):
        for j in range(4):
            for kind in range(3):
                place_of[3 * head_of(r, j) + kind] = (got[r], 384 * (j // 2) + 128 * kind + 64 * (j % 2))
    for at in range(24):
        grad_q[:, 128 * at : 128 * at + 128] = halves(place_of[2 * at], place_of[2 * at + 1])
    write(grad_q, grad_q_hbm)
    link.copy("tx", 0, 1, XT, XT, core).wait_recv()
    total_t = ZT[0, xx].astype(F32) + XT[...].astype(F32)
    turned_t = jnp.concatenate([total_t, jnp.zeros((112, 128), F32)], axis=0).T.astype(BF)
    for owner in range(4):
        SWT[owner] = turned_t[32 * owner : 32 * owner + 32]
    to_seq("swt", SWT, RWT)
    first_o(chunk(3))
    final_o()
    write(dqT, grad_o_hbm)
    from_seq("swi", RWI)
    for r in range(4):
        for blk in range(8):
            at = 512 * blk + 128 * r
            oT[32 * (at // 1024) : 32 * (at // 1024) + 32, at % 1024 : at % 1024 + 128] = RWI[
                r, :, 128 * blk : 128 * blk + 128
            ].astype(F32)
    for q in range(4):
        write(oT.at[32 * q : 32 * q + 32], grad_i_hbm.at[:, 1024 * q : 1024 * q + 1024])

    from_seq("swt", RWT)
    mine = RWT[0].astype(F32)
    summed = mine + RWT[1].astype(F32) + RWT[2].astype(F32) + RWT[3].astype(F32)
    summed = jnp.where(lane == 2, mine, summed)
    summed = jnp.concatenate([summed, jnp.zeros((96, 128), F32)], axis=0).T
    grad_small[...] = jnp.where(lax.broadcasted_iota(jnp.int32, (8, 128), 0) < 3, summed[0:8], total_t[0:8])
    write(grad_small, grad_small_hbm)

    for make in pending:
        make().wait_send()
    seq_left("prms", lambda owner: prm_block(s), lambda: prm_block(s))
    seq_left("wqs", lambda owner: PWQ.at[owner], lambda: wq_block(s))
    seq_left("swi", lambda owner: SWI.at[owner], lambda: RWI.at[s])
    seq_left("swq", lambda owner: SWQ.at[owner], lambda: RWQ.at[s])
    seq_left("swt", lambda owner: SWT.at[owner], lambda: RWT.at[s])
    for name, (parts, _) in gathers.items():
        for u in range(parts):
            gather_left(name, u)
    for w in range(2):
        rows_left("g", G, w)
    for q in range(4):
        link.copy("ox", q, 4, GO.at[q, ox], XO.at[q], xpart).wait_send()
        link.copy("ix", q, 4, GI.at[q, ox], XI.at[q], xpart).wait_send()
    z_left()
    for w in range(2):
        for t in range(2):
            for yy in range(2):
                src = shares[t].at[w, rows(SL * (2 * yy + oc), SL)]
                dst = X.at[w, rows(SL * (2 * t + yy), SL)]
                link.copy("sc", 4 * w + 2 * t + yy, 8, src, dst, core).wait_send()
            src = shares[t].at[w, rows(SL * (2 * oy + c), SL)]
            link.copy("sy", 2 * w + t, 4, src, YR.at[w, t], ypart).wait_send()
    for p in range(2):
        link.copy("qx", p, 2, GQ.at[p, ox], XQ.at[p], xpart).wait_send()
        ga_c(p).wait_send()
        ga_x(p).wait_send()
    for cp in written:
        if cp is not first_rows:
            cp.wait()


def publish(*refs):
    sources, small, targets, row_targets = refs[:6], refs[6], refs[7:13], refs[13:17]
    held, (in_sems, out_sems) = refs[17:23], refs[23:]
    arrive = [
        pltpu.make_async_copy(sources[i], held[i], in_sems.at[i]) for i in range(6)
    ]
    leave = [
        pltpu.make_async_copy(held[i], targets[i], out_sems.at[i]) for i in range(6)
    ]
    largest_first = (1, 0, 4, 5, 2, 3)
    for i in largest_first:
        arrive[i].start()
    for i, target in enumerate(row_targets):
        target[...] = small[i : i + 1, 0 : target.shape[1]]
    for i in largest_first:
        arrive[i].wait()
        leave[i].start()
    for cp in leave:
        cp.wait()


def turn_tables(seq_len):
    inverse = 10000.0 ** (-2.0 * np.arange(ROTARY // 2) / ROTARY)
    angles = np.arange(seq_len)[:, None] * inverse[None, :]
    cosine = np.ones((seq_len, HD), np.float32)
    sine = np.zeros((seq_len, HD), np.float32)
    cosine[:, 0:ROTARY:2] = cosine[:, 1:ROTARY:2] = np.cos(angles)
    sine[:, 0:ROTARY:2] = -np.sin(angles)
    sine[:, 1:ROTARY:2] = np.sin(angles)
    return np.concatenate([cosine, sine], axis=1)


def fused_shards(inputs, ends, ln_gain, ln_bias, w_qkv, w_attn, w_in, b_in, w_out, b_out, cotangent):
    in_vmem = pl.BlockSpec(memory_space=pltpu.VMEM)
    in_any = pl.BlockSpec(memory_space=pl.ANY)
    rows_type = (2, 1024, 1024)
    shapes = (
        jax.ShapeDtypeStruct((2, 256, 1024), BF),
        jax.ShapeDtypeStruct((2, 256, 1024), F32),
        jax.ShapeDtypeStruct((32, 3072), F32),
        jax.ShapeDtypeStruct((32, 1024), F32),
        jax.ShapeDtypeStruct((32, 4096), F32),
        jax.ShapeDtypeStruct((128, 1024), F32),
    )
    results = pl.pallas_call(
        fused_layer,
        out_shape=shapes + (jax.ShapeDtypeStruct((8, 128), F32),),
        in_specs=[pl.BlockSpec(memory_space=pltpu.SMEM)] + [in_vmem] * 9 + [in_any] * 2,
        out_specs=(in_any,) * 7,
        scratch_shapes=[
            pltpu.VMEM(rows_type, BF),
            pltpu.VMEM(rows_type, BF),
            pltpu.VMEM(rows_type, BF),
            pltpu.VMEM(rows_type, BF),
            pltpu.VMEM(rows_type, BF),
            pltpu.VMEM((1024, 1024), BF),
            pltpu.VMEM((1024, 1024), BF),
            pltpu.VMEM((1024, 768), BF),
            pltpu.VMEM((4, 2, 32, 1024), BF),
            pltpu.VMEM((4, 2, 32, 1024), BF),
            pltpu.VMEM((4, 32, 1024), BF),
            pltpu.VMEM((4, 32, 768), BF),
            pltpu.VMEM((4, 16, 128), BF),
            pltpu.VMEM((8, 16, 128), BF),
            pltpu.VMEM((8, 1024), F32),
            pltpu.VMEM((2, 1024, 768), BF),
            pltpu.VMEM((2, 1024, 256), BF),
            pltpu.VMEM((2, 1024, 256), BF),
            pltpu.VMEM((4, 2, 128, 1024), BF),
            pltpu.VMEM((4, 128, 1024), BF),
            pltpu.VMEM((2, 128, 1024), BF),
            pltpu.VMEM((2, 128, 1024), BF),
            pltpu.VMEM((4, 2, 4, 256, 128), BF),
            pltpu.VMEM((4, 4, 256, 128), BF),
            pltpu.VMEM((4, 256, 128), BF),
            pltpu.VMEM((2, 256, 128), BF),
            pltpu.VMEM((2, 2, 256, 128), BF),
            pltpu.VMEM((2, 2, 256, 128), BF),
            pltpu.VMEM((2, 2, 4, 384, 128), BF),
            pltpu.VMEM((2, 4, 384, 128), BF),
            pltpu.VMEM((2, 2, 384, 128), BF),
            pltpu.VMEM((2, 2, 384, 128), BF),
            pltpu.VMEM((2, 4, 32, 1024), BF),
            pltpu.VMEM((4, 32, 1024), BF),
            pltpu.VMEM((2, 32, 1024), BF),
            pltpu.VMEM((2, 32, 1024), BF),
            pltpu.VMEM((2, 4, 16, 128), BF),
            pltpu.VMEM((16, 128), BF),
            pltpu.VMEM((3, 2, 16, 128), BF),
            pltpu.VMEM((2, 2, 256, 1024), BF),
            pltpu.VMEM((4, 32, 1024), BF),
            pltpu.VMEM((4, 32, 1024), BF),
            pltpu.VMEM((4, 32, 768), BF),
            pltpu.VMEM((4, 32, 768), BF),
            pltpu.VMEM((4, 32, 128), BF),
            pltpu.VMEM((4, 32, 128), BF),
            pltpu.VMEM((16, 1024), F32),
            pltpu.VMEM((2, 1024, 128), BF),
            pltpu.VMEM((128, 1024), BF),
            pltpu.VMEM((128, 1024), BF),
            pltpu.VMEM((128, 1024), BF),
            pltpu.VMEM((128, 1024), F32),
            pltpu.VMEM((128, 1024), F32),
            pltpu.VMEM((1024, 128), F32),
            pltpu.VMEM((1024, 128), F32),
            pltpu.VMEM((256, 1024), F32),
            pltpu.VMEM((32, 3072), F32),
            pltpu.VMEM((32, 1024), F32),
            pltpu.VMEM((8, 128), F32),
            pltpu.SemaphoreType.DMA((192,)),
            pltpu.SemaphoreType.DMA((192,)),
            pltpu.SemaphoreType.DMA((6,)),
            pltpu.SemaphoreType.DMA((14,)),
        ],
        compiler_params=pltpu.CompilerParams(
            collective_id=0, has_side_effects=True, vmem_limit_bytes=65400 * 2**10
        ),
        cost_estimate=pl.CostEstimate(flops=46 * 10**9, bytes_accessed=10**7, transcendentals=10**7),
    )(
        ends,
        ln_gain.reshape(1, 32),
        ln_bias.reshape(1, 32),
        b_out.reshape(1, 32),
        b_in.reshape(1, 128),
        w_qkv, w_attn, w_in, w_out, turn_tables(1024), inputs, cotangent)
    row = jax.ShapeDtypeStruct((1, 32), F32)
    final = pl.pallas_call(
        publish,
        out_shape=shapes + (row, row, row, jax.ShapeDtypeStruct((1, 128), F32)),
        in_specs=[in_any] * 6 + [in_vmem],
        out_specs=(in_any,) * 6 + (in_vmem,) * 4,
        scratch_shapes=[pltpu.VMEM(v.shape, v.dtype) for v in shapes]
        + [pltpu.SemaphoreType.DMA((6,)), pltpu.SemaphoreType.DMA((6,))],
        compiler_params=pltpu.CompilerParams(vmem_limit_bytes=60 * 2**20),
    )(*results)
    out, grad_in, grad_q, grad_a, grad_i, grad_o, bias, gain, bias_out, bias_in = final
    return (
        out,
        grad_in,
        gain.reshape(32),
        bias.reshape(32),
        grad_q,
        grad_a,
        grad_i,
        bias_in.reshape(128),
        grad_o,
        bias_out.reshape(32),
    )


def fits_fused(mesh):
    return mesh.shape["batch"] == 8 and mesh.shape["seq"] == 4


def solution(mesh):
    return jax.shard_map(
        fused_shards if fits_fused(mesh) else shards,
        mesh=mesh,
        in_specs=(
            P("batch", "seq", None),
            P("batch"),
            P(("batch", "seq")),
            P(("batch", "seq")),
            P(("batch", "seq"), None),
            P(("batch", "seq"), None),
            P(("batch", "seq"), None),
            P(("batch", "seq")),
            P(("batch", "seq"), None),
            P(("batch", "seq")),
            P("batch", "seq", None),
        ),
        out_specs=(
            P("batch", "seq", None),
            P("batch", "seq", None),
            P(("batch", "seq")),
            P(("batch", "seq")),
            P(("batch", "seq"), None),
            P(("batch", "seq"), None),
            P(("batch", "seq"), None),
            P(("batch", "seq")),
            P(("batch", "seq"), None),
            P(("batch", "seq")),
        ),
        check_vma=False,
    )
```

```python
import math

import jax
import jax.numpy as jnp
import numpy as np
from jax import lax
from jax.experimental import pallas as pl
from jax.experimental.pallas import tpu as pltpu
from jax.sharding import PartitionSpec as P

HEADS = 16
HD = 64
ROTARY = 32
MICRO = 2


norm_eps = 1e-05
gelu_factor = 0.7978845608028654
masked_score = -1e30


def gelu_tanh(values):
    return (
        0.5
        * values
        * (1.0 + jnp.tanh(gelu_factor * (values + 0.044715 * values * values * values)))
    )


def layer_norm(row_values, norm_gain, norm_shift):
    average = jnp.mean(row_values, axis=-1, keepdims=True)
    centered = row_values - average
    variance = jnp.mean(centered * centered, axis=-1, keepdims=True)
    return centered * lax.rsqrt(variance + norm_eps) * norm_gain + norm_shift


def rotary_tables(positions):
    pair_index = jnp.arange(ROTARY // 2, dtype=jnp.float32)
    inverse = 10000.0 ** (-2.0 * pair_index / ROTARY)
    angles = positions[:, None] * inverse[None, :]
    return (jnp.cos(angles), jnp.sin(angles))


def rotate(vectors, cosine, sine_table):
    rotated = vectors[..., :ROTARY]
    even_part = rotated[..., 0::2]
    odd_part = rotated[..., 1::2]
    cosine_wide = cosine[:, None, :]
    sine_wide = sine_table[:, None, :]
    new_even = even_part * cosine_wide - odd_part * sine_wide
    new_odd = odd_part * cosine_wide + even_part * sine_wide
    merged = jnp.stack([new_even, new_odd], axis=-1).reshape(rotated.shape)
    return jnp.concatenate([merged, vectors[..., ROTARY:]], axis=-1)


def visible(query_places, key_places, ending):
    query_after = query_places[:, None] >= ending
    key_after = key_places[None, :] >= ending
    return (key_places[None, :] <= query_places[:, None]) & (query_after == key_after)


def block_scores(block_queries, key_vectors, query_places, key_places, ending, score_scale):
    scores = (
        jnp.einsum("qhd,khd->hqk", block_queries, key_vectors, preferred_element_type=jnp.float32)
        * score_scale
    )
    return jnp.where(visible(query_places, key_places, ending)[None], scores, masked_score)


def attend_forward(packed, ending):
    seq_len, head_count, triple = packed.shape
    head_size = triple // 3
    block_rows = min(512, seq_len)
    score_scale = 1.0 / math.sqrt(head_size)
    queries = packed[:, :, :head_size]
    key_vectors = packed[:, :, head_size : 2 * head_size]
    values = packed[:, :, 2 * head_size :]
    key_places = jnp.arange(seq_len, dtype=jnp.int32)

    def one_block(block_index):
        first_row = block_index * block_rows
        block_queries = lax.dynamic_slice_in_dim(queries, first_row, block_rows, 0)
        query_places = first_row + jnp.arange(block_rows, dtype=jnp.int32)
        scores = block_scores(
            block_queries, key_vectors, query_places, key_places, ending, score_scale
        )
        row_peak = jnp.max(scores, axis=-1, keepdims=True)
        weights = jnp.exp(scores - row_peak)
        row_total = jnp.sum(weights, axis=-1, keepdims=True)
        probabilities = (weights / row_total).astype(jnp.bfloat16)
        result = jnp.einsum(
            "hqk,khd->qhd", probabilities, values, preferred_element_type=jnp.float32
        )
        return (result.astype(jnp.bfloat16), row_peak, row_total)

    results, peaks, totals = lax.map(one_block, jnp.arange(seq_len // block_rows, dtype=jnp.int32))
    return (results.reshape(seq_len, head_count, head_size), peaks, totals)


def attend_backward(packed, d_attended, peaks, totals, ending, full_cosine, full_sine):
    seq_len, head_count, triple = packed.shape
    head_size = triple // 3
    block_rows = min(512, seq_len)
    score_scale = 1.0 / math.sqrt(head_size)
    queries = packed[:, :, :head_size]
    key_vectors = packed[:, :, head_size : 2 * head_size]
    values = packed[:, :, 2 * head_size :]
    key_places = jnp.arange(seq_len, dtype=jnp.int32)

    def one_block(running, block_inputs):
        key_grads, value_grads = running
        block_index, row_peak, row_total = block_inputs
        first_row = block_index * block_rows
        block_queries = lax.dynamic_slice_in_dim(queries, first_row, block_rows, 0)
        block_grads = lax.dynamic_slice_in_dim(d_attended, first_row, block_rows, 0)
        query_places = first_row + jnp.arange(block_rows, dtype=jnp.int32)
        scores = block_scores(
            block_queries, key_vectors, query_places, key_places, ending, score_scale
        )
        probabilities = jnp.exp(scores - row_peak) / row_total
        rounded_probs = probabilities.astype(jnp.bfloat16)
        d_probs = jnp.einsum(
            "qhd,khd->hqk", block_grads, values, preferred_element_type=jnp.float32
        )
        row_dot = jnp.sum(probabilities * d_probs, axis=-1, keepdims=True)
        d_scores = (probabilities * (d_probs - row_dot)).astype(jnp.bfloat16)
        query_grads = (
            jnp.einsum("hqk,khd->qhd", d_scores, key_vectors, preferred_element_type=jnp.float32)
            * score_scale
        )
        key_grads = (
            key_grads
            + jnp.einsum(
                "hqk,qhd->khd", d_scores, block_queries, preferred_element_type=jnp.float32
            )
            * score_scale
        )
        value_grads = value_grads + jnp.einsum(
            "hqk,qhd->khd", rounded_probs, block_grads, preferred_element_type=jnp.float32
        )
        return ((key_grads, value_grads), query_grads)

    zero_sums = jnp.zeros((seq_len, head_count, head_size), jnp.float32)
    block_ids = jnp.arange(seq_len // block_rows, dtype=jnp.int32)
    (key_grads, value_grads), query_grads = lax.scan(
        one_block, (zero_sums, zero_sums), (block_ids, peaks, totals)
    )
    query_grads = query_grads.reshape(seq_len, head_count, head_size)
    flipped_sine = -full_sine
    combined = jnp.stack(
        [
            rotate(query_grads, full_cosine, flipped_sine),
            rotate(key_grads, full_cosine, flipped_sine),
            value_grads,
        ],
        axis=2,
    )
    return combined.astype(jnp.bfloat16).reshape(seq_len, head_count, triple)


def collect(ln_gain, ln_bias, w_qkv, w_attn, w_in, b_in, w_out, b_out):
    return (
        lax.all_gather(ln_gain, ("batch", "seq"), axis=0, tiled=True),
        lax.all_gather(ln_bias, ("batch", "seq"), axis=0, tiled=True),
        lax.all_gather(w_qkv, ("batch", "seq"), axis=0, tiled=True),
        lax.all_gather(w_attn, ("batch", "seq"), axis=0, tiled=True),
        lax.all_gather(w_in, ("batch", "seq"), axis=0, tiled=True),
        lax.all_gather(b_in, ("batch", "seq"), axis=0, tiled=True),
        lax.all_gather(w_out, ("batch", "seq"), axis=0, tiled=True),
        lax.all_gather(b_out, ("batch", "seq"), axis=0, tiled=True),
    )


def reduce_grads(gradients):
    return (
        lax.psum_scatter(gradients[0], ("batch", "seq"), scatter_dimension=0, tiled=True),
        lax.psum_scatter(gradients[1], ("batch", "seq"), scatter_dimension=0, tiled=True),
        lax.psum_scatter(gradients[2], ("batch", "seq"), scatter_dimension=0, tiled=True),
        lax.psum_scatter(gradients[3], ("batch", "seq"), scatter_dimension=0, tiled=True),
        lax.psum_scatter(gradients[4], ("batch", "seq"), scatter_dimension=0, tiled=True),
        lax.psum_scatter(gradients[5], ("batch", "seq"), scatter_dimension=0, tiled=True),
        lax.psum_scatter(gradients[6], ("batch", "seq"), scatter_dimension=0, tiled=True),
        lax.psum_scatter(gradients[7], ("batch", "seq"), scatter_dimension=0, tiled=True),
    )


def shards(inputs, ends, ln_gain, ln_bias, w_qkv, w_attn, w_in, b_in, w_out, b_out, cotangent):
    seq_devices = lax.axis_size("seq")
    windows, local_len, model_width = inputs.shape
    seq_len = local_len * seq_devices
    per_micro = windows // MICRO
    offset = lax.axis_index("seq") * local_len
    cosine, sine_table = rotary_tables(
        (offset + jnp.arange(local_len, dtype=jnp.int32)).astype(jnp.float32)
    )
    full_cosine, full_sine = rotary_tables(jnp.arange(seq_len, dtype=jnp.float32))
    outputs = []
    input_grads = []
    shard_sums = None
    for micro_index in range(MICRO):
        gathered = collect(ln_gain, ln_bias, w_qkv, w_attn, w_in, b_in, w_out, b_out)
        (
            gain_full,
            shift_full,
            qkv_full,
            attn_full,
            in_full,
            bias_in_full,
            out_full,
            bias_out_full,
        ) = gathered
        lower = micro_index * per_micro
        row_values = inputs[lower : lower + per_micro].astype(jnp.float32)
        grad_rows = cotangent[lower : lower + per_micro]
        window_ends = ends[lower : lower + per_micro]
        normed_f, norm_pull = jax.vjp(
            layer_norm, row_values, gain_full.astype(jnp.float32), shift_full.astype(jnp.float32)
        )
        normed = normed_f.astype(jnp.bfloat16)
        projected = jnp.einsum("pld,de->ple", normed, qkv_full, preferred_element_type=jnp.float32)
        arranged = projected.reshape(per_micro, local_len, HEADS, 3, HD)
        query_rot = rotate(arranged[:, :, :, 0], cosine, sine_table)
        key_rot = rotate(arranged[:, :, :, 1], cosine, sine_table)
        packed = jnp.stack([query_rot, key_rot, arranged[:, :, :, 2]], axis=3).astype(jnp.bfloat16)
        packed = packed.reshape(per_micro, local_len, HEADS, 3 * HD)
        head_view = lax.all_to_all(packed, "seq", split_axis=2, concat_axis=1, tiled=True)
        attended, peaks, totals = lax.map(
            lambda bundle: attend_forward(bundle[0], bundle[1]), (head_view, window_ends)
        )
        position_view = lax.all_to_all(
            attended, "seq", split_axis=1, concat_axis=2, tiled=True
        ).reshape(per_micro, local_len, model_width)
        branch_attn = jnp.einsum(
            "ple,ed->pld", position_view, attn_full, preferred_element_type=jnp.float32
        )
        hidden = jnp.einsum(
            "pld,di->pli", normed, in_full, preferred_element_type=jnp.float32
        ) + bias_in_full.astype(jnp.float32)
        activ_f, gelu_pull = jax.vjp(gelu_tanh, hidden)
        activated = activ_f.astype(jnp.bfloat16)
        branch_mlp = jnp.einsum(
            "pli,id->pld", activated, out_full, preferred_element_type=jnp.float32
        ) + bias_out_full.astype(jnp.float32)
        outputs.append((row_values + branch_attn + branch_mlp).astype(jnp.bfloat16))
        grad_b_out = jnp.sum(grad_rows.astype(jnp.float32), axis=(0, 1))
        grad_w_out = jnp.einsum(
            "pli,pld->id", activated, grad_rows, preferred_element_type=jnp.float32
        )
        d_activated = jnp.einsum(
            "pld,id->pli", grad_rows, out_full, preferred_element_type=jnp.float32
        )
        d_hidden = gelu_pull(d_activated)[0].astype(jnp.bfloat16)
        grad_b_in = jnp.sum(d_hidden.astype(jnp.float32), axis=(0, 1))
        grad_w_in = jnp.einsum("pld,pli->di", normed, d_hidden, preferred_element_type=jnp.float32)
        grad_w_attn = jnp.einsum(
            "ple,pld->ed", position_view, grad_rows, preferred_element_type=jnp.float32
        )
        d_attended = jnp.einsum(
            "pld,ed->ple", grad_rows, attn_full, preferred_element_type=jnp.float32
        ).astype(jnp.bfloat16)
        d_attended = d_attended.reshape(per_micro, local_len, HEADS, HD)
        d_head_view = lax.all_to_all(d_attended, "seq", split_axis=2, concat_axis=1, tiled=True)
        d_packed = lax.map(
            lambda bundle: attend_backward(
                bundle[0], bundle[1], bundle[2], bundle[3], bundle[4], full_cosine, full_sine
            ),
            (head_view, d_head_view, peaks, totals, window_ends),
        )
        d_projected = lax.all_to_all(
            d_packed, "seq", split_axis=1, concat_axis=2, tiled=True
        ).reshape(per_micro, local_len, 3 * model_width)
        grad_w_qkv = jnp.einsum(
            "pld,ple->de", normed, d_projected, preferred_element_type=jnp.float32
        )
        d_normed = jnp.einsum("pli,di->pld", d_hidden, in_full, preferred_element_type=jnp.float32)
        d_normed = d_normed + jnp.einsum(
            "ple,de->pld", d_projected, qkv_full, preferred_element_type=jnp.float32
        )
        d_rows, grad_gain, grad_shift = norm_pull(d_normed)
        input_grads.append(grad_rows.astype(jnp.float32) + d_rows)
        local_grads = (
            grad_gain,
            grad_shift,
            grad_w_qkv,
            grad_w_attn,
            grad_w_in,
            grad_b_in,
            grad_w_out,
            grad_b_out,
        )
        reduced = reduce_grads(local_grads)
        if shard_sums is None:
            shard_sums = reduced
        else:
            shard_sums = tuple((running + extra for running, extra in zip(shard_sums, reduced)))
    output = jnp.concatenate(outputs, axis=0)
    grad_inputs = jnp.concatenate(input_grads, axis=0)
    return (
        output,
        grad_inputs,
        shard_sums[0],
        shard_sums[1],
        shard_sums[2],
        shard_sums[3],
        shard_sums[4],
        shard_sums[5],
        shard_sums[6],
        shard_sums[7],
    )


HB, SB = 4, 4
NEG = -1e30
BF, F32 = jnp.bfloat16, jnp.float32
MESH = pl.DeviceIdType.MESH


def dot(a, b, ca, cb):
    return lax.dot_general(a, b, (((ca,), (cb,)), ((), ())), preferred_element_type=F32)


def rows(start, size):
    return pl.ds(pl.multiple_of(start, size), size)


def lanes(start, size=128):
    return pl.ds(pl.multiple_of(start, size), size)


def halves(low_source, high_source):
    def piece(source, upper):
        array, first = source
        tile = array[:, first // 128 * 128 : first // 128 * 128 + 128]
        return pltpu.roll(tile, 64, 1) if (first % 128 == 64) != upper else tile

    lane = lax.broadcasted_iota(jnp.int32, (1, 128), 1)
    return jnp.where(lane < 64, piece(low_source, False), piece(high_source, True))


def head_of(owner, j):
    return 4 * j + 2 * (owner % 2) + owner // 2


class Link:
    def __init__(self, send_sems, recv_sems):
        self.send_sems, self.recv_sems = send_sems, recv_sems
        self.first = {}
        self.used = 0

    def index(self, name, at, count):
        if name not in self.first:
            self.first[name] = self.used
            self.used += count
        return self.first[name] + at

    def copy(self, name, at, count, src, dst, device):
        i = self.index(name, at, count)
        return pltpu.make_async_remote_copy(
            src_ref=src,
            dst_ref=dst,
            send_sem=self.send_sems.at[i],
            recv_sem=self.recv_sems.at[i],
            device_id=device,
            device_id_type=MESH,
        )


def gelu_pair(v):
    square = v * v
    half = 0.5 + 0.5 * jnp.tanh(v * (gelu_factor + (gelu_factor * 0.044715) * square))
    value = v * half
    return value, half + (value - value * half) * (
        2.0 * gelu_factor + (6.0 * gelu_factor * 0.044715) * square
    )


def fused_layer(
    ends, gain, bias, bias_out, bias_in, wq, wa, wi, wo, turns, x_in, g_in,
    out_hbm, grad_in_hbm, grad_q_hbm, grad_a_hbm, grad_i_hbm, grad_o_hbm, grad_small_hbm,
    X, N, G, A, H, Wi, Wo, Wq, WaAll, Wa, PWI, PWQ, PRS, PRM, PR, QKV, att, dO,
    GO, XO, ZO, CO, GI, XI, ZN, ZF, ZD, CI, GQ, XQ, ZQ, CQ, GA, XA, ZA, CA, GT, XT, ZT,
    YR, SWI, RWI, SWQ, RWQ, SWT, RWT, TAIL,
    khat, ktT, vtT, doT, oT, dqT, dkA, dvA,
    grad_in, grad_q, grad_a, grad_small,
    send_sems, recv_sems, local_sems, out_sems,
):
    b = lax.axis_index("batch")
    s = lax.axis_index("seq")
    z, xx = b // 2, b % 2
    y, c = s // 2, s % 2
    oc, ox, oy = 1 - c, 1 - xx, 1 - y
    SL = 256
    S = 1024
    core = (b, 2 * y + oc)
    ypart = (b, 2 * oy + c)
    diag = (b, 2 * oy + oc)
    xpart = (2 * z + ox, s)

    def zdev(k):
        return (2 * ((z + k) % 4) + xx, s)

    def zfrom(k):
        return (z + 4 - k) % 4

    link = Link(send_sems, recv_sems)
    pending = []

    def start(make):
        make().start()
        pending.append(make)

    barrier = pltpu.get_barrier_semaphore()
    others = [xpart] + [zdev(k) for k in (1, 2, 3)]
    others += [(2 * ((z + k) % 4) + ox, s) for k in (1, 2, 3)]
    partners = [core, ypart, diag] + others
    for device in partners:
        pl.semaphore_signal(barrier, inc=1, device_id=device, device_id_type=MESH)

    own = rows(SL * s, SL)
    locals_ = []
    for w in range(2):
        locals_.append(pltpu.make_async_copy(x_in.at[w], X.at[w, own], local_sems.at[3 * w]))
        locals_.append(pltpu.make_async_copy(g_in.at[w], G.at[w, own], local_sems.at[3 * w + 1]))
    for cp in locals_:
        cp.start()

    for r in range(SB):
        for blk in range(8):
            PWI[r, :, 128 * blk : 128 * blk + 128] = wi[:, 512 * blk + 128 * r : 512 * blk + 128 * r + 128]
    TAIL[...] = jnp.zeros_like(TAIL)
    for i, values in enumerate((gain, bias, bias_out, bias_in)):
        TAIL[i : i + 1, 0 : values.shape[1]] = values[...].astype(F32)
    tile = TAIL[:, 0:128]
    row = lax.broadcasted_iota(jnp.int32, (16, 128), 0)
    tile = jnp.where(row < 3, pltpu.roll(tile, 32 * s, 1), tile)
    PRS[s] = tile.astype(BF)
    Wi[rows(128 * b + 32 * s, 32), :] = PWI[s]
    Wo[rows(128 * b, 128), :] = wo[...]
    WaAll[z, xx] = wa[...]

    wq_f = wq[...].astype(F32)
    for r in range(SB):
        for kind in range(3):
            for p in range(2):
                lo = 192 * head_of(r, 2 * p) + 64 * kind
                hi = 192 * head_of(r, 2 * p + 1) + 64 * kind
                at = 384 * p + 128 * kind
                PWQ[r, :, at : at + 128] = halves((wq_f, lo), (wq_f, hi)).astype(BF)
    Wq[rows(128 * b + 32 * s, 32), :] = PWQ[s]

    pl.semaphore_wait(barrier, len(partners))

    def seq_sends(name, src_of, dst):
        for i, (device, owner) in enumerate(
            ((core, 2 * y + oc), (ypart, 2 * oy + c), (diag, 2 * oy + oc))
        ):
            link.copy(name, i, 3, src_of(owner), dst(), device).start()

    def seq_left(name, src_of, dst):
        for i, (device, owner) in enumerate(
            ((core, 2 * y + oc), (ypart, 2 * oy + c), (diag, 2 * oy + oc))
        ):
            link.copy(name, i, 3, src_of(owner), dst(), device).wait_send()

    def seq_waits(name, src, dst_of):
        for i, owner in enumerate((2 * y + oc, 2 * oy + c, 2 * oy + oc)):
            link.copy(name, i, 3, src, dst_of(owner), core).wait_recv()

    def prm_block(owner):
        return PRS.at[owner]

    def wi_block(owner, u):
        return Wi.at[rows(128 * b + 32 * owner, 32), 256 * u : 256 * u + 256]

    def wq_block(owner):
        return Wq.at[rows(128 * b + 32 * owner, 32)]

    gathers = {
        "wi": (4, lambda bb, u: Wi.at[rows(128 * bb, 128), lanes(256 * u, 256)]),
        "wo": (2, lambda bb, u: Wo.at[rows(128 * bb + 64 * u, 64)]),
        "wq": (2, lambda bb, u: Wq.at[rows(128 * bb, 128), 384 * u : 384 * u + 384]),
        "wa": (1, lambda bb, u: WaAll.at[bb // 2, bb % 2]),
    }
    pair = z + 1 - 2 * (z % 2)

    def gather_copy(name, way, at, count, zz, side, u, device):
        held = gathers[name][1](2 * zz + side, u)
        return link.copy(name + way, count * u + at, count * gathers[name][0], held, held, device)

    by_line = ("wi", "wo")

    def up_copy(name, zz, u):
        return gather_copy(name, "l", zz, 5, zz, xx, u, (2 * (z + 1) + xx, s))

    def down_copy(name, zz, u):
        return gather_copy(name, "l", zz + 1, 5, zz, xx, u, (2 * (z - 1) + xx, s))

    def z_copy(name, zz, k, u):
        return gather_copy(name, "z", k - 1, 3, zz, xx, u, zdev(k))

    def x_copy(name, zz, side, u):
        return gather_copy(name, "x", zz, 4, zz, side, u, xpart)

    def gather_z(name, u):
        if name in by_line:

            @pl.when(z < 3)
            def _():
                up_copy(name, z, u).start()

            @pl.when(z > 0)
            def _():
                down_copy(name, z, u).start()

            return
        for far in (1, 2, 3):

            @pl.when(z + far <= 3)
            def _():
                z_copy(name, z, far, u).start()

            @pl.when(z >= far)
            def _():
                z_copy(name, z, 4 - far, u).start()

    def gather_x(name, u):
        x_copy(name, z, xx, u).start()

    def gather_pass(name, far, u):
        @pl.when(z >= far)
        def _():
            if name in by_line:
                up_copy(name, z - far, u).wait_recv()

                @pl.when(z < 3)
                def _():
                    up_copy(name, z - far, u).start()

            else:
                z_copy(name, z - far, far, u).wait_recv()
            x_copy(name, z - far, xx, u).start()

        @pl.when(z + far <= 3)
        def _():
            if name in by_line:
                down_copy(name, z + far, u).wait_recv()

                @pl.when(z > 0)
                def _():
                    down_copy(name, z + far, u).start()

            else:
                z_copy(name, z + far, 4 - far, u).wait_recv()
            x_copy(name, z + far, xx, u).start()

    def gather_block(name, zz, u):
        x_copy(name, zz, ox, u).wait_recv()

    def gather_end(name, u):
        for zz in range(4):
            gather_block(name, zz, u)

    def gather_left(name, u):
        if name not in by_line:
            for k in (1, 2, 3):
                z_copy(name, z, k, u).wait_send()
        for zz in range(4):
            if name in by_line:

                @pl.when((zz <= z) & (z < 3))
                def _():
                    up_copy(name, zz, u).wait_send()

                @pl.when((zz >= z) & (z > 0))
                def _():
                    down_copy(name, zz, u).wait_send()

            x_copy(name, zz, xx, u).wait_send()

    def rows_start(name, src, dst):
        for w in range(2):
            start(lambda w=w: link.copy(name + "c", w, 2, src.at[w], dst.at[w, own], core))
            start(lambda w=w: link.copy(name + "y", w, 2, src.at[w], dst.at[w, own], ypart))

    def rows_pass(name, dst, w):
        block = dst.at[w, rows(SL * (2 * oy + c), SL)]
        link.copy(name + "y", w, 2, block, block, core).wait_recv()
        link.copy(name + "f", w, 2, block, block, core).start()

    def rows_left(name, dst, w):
        block = dst.at[w, rows(SL * (2 * oy + c), SL)]
        link.copy(name + "f", w, 2, block, block, core).wait_send()

    def rows_end_core(name, dst, w):
        block = dst.at[w, rows(SL * (2 * y + oc), SL)]
        link.copy(name + "c", w, 2, block, block, core).wait_recv()

    def rows_end_far(name, dst, w):
        block = dst.at[w, rows(SL * (2 * oy + oc), SL)]
        link.copy(name + "f", w, 2, block, block, core).wait_recv()

    seq_sends("prms", lambda owner: prm_block(s), lambda: prm_block(s))
    for u in range(4):
        seq_sends(
            "wis%d" % u, lambda owner: PWI.at[owner, :, 256 * u : 256 * u + 256], lambda: wi_block(s, u)
        )
    gather_z("wa", 0)
    gather_x("wa", 0)
    gather_x("wo", 0)
    seq_sends("wqs", lambda owner: PWQ.at[owner], lambda: wq_block(s))
    rows_start("x", x_in, X)
    seq_waits("prms", prm_block(s), prm_block)
    total = PRS[0].astype(F32) + PRS[1].astype(F32) + PRS[2].astype(F32) + PRS[3].astype(F32)
    PRM[b] = jnp.where(row < 3, total, tile).astype(BF)
    for i, device in enumerate(others):
        start(lambda i=i, device=device: link.copy("prm", i, 7, PRM.at[b], PRM.at[b], device))
    for u in range(4):
        seq_waits("wis%d" % u, wi_block(s, u), lambda owner: wi_block(owner, u))
        gather_z("wi", u)
        gather_x("wi", u)
    rows_start("g", g_in, G)
    gather_pass("wi", 1, 0)
    gather_pass("wi", 1, 1)
    for far in (1, 2, 3):
        gather_pass("wa", far, 0)

    for i in range(7):
        k = (0, 1, 2, 3, 1, 2, 3)[i]
        bb = 2 * zfrom(k) + (ox if i in (0, 4, 5, 6) else xx)
        link.copy("prm", i, 7, PRM.at[bb], PRM.at[bb], core).wait_recv()
    for bb in range(8):
        PR[:, 128 * bb : 128 * bb + 128] = PRM[bb].astype(F32)[0:8]

    for cp in locals_:
        cp.wait()

    def norm_rows(w, owner):
        r = rows(SL * owner, SL)
        v = X[w, r, :].astype(F32)
        v = v - jnp.mean(v, axis=-1, keepdims=True)
        var = jnp.mean(v * v, axis=-1, keepdims=True)
        N[w, r, :] = (v * lax.rsqrt(var + norm_eps) * PR[0:1, :] + PR[1:2, :]).astype(BF)

    def norm_near(w, carry):
        norm_rows(w, s)
        norm_rows(w, 2 * y + oc)
        return carry

    def norm_far(w):
        rows_end_far("x", X, w)
        norm_rows(w, 2 * oy + c)
        norm_rows(w, 2 * oy + oc)

    for w in range(2):
        rows_end_core("x", X, w)
    lax.fori_loop(0, 2, norm_near, 0)
    gather_pass("wi", 2, 0)
    gather_pass("wi", 1, 2)
    gather_pass("wi", 1, 3)
    seq_waits("wqs", wq_block(s), wq_block)
    gather_z("wq", 0)
    gather_x("wq", 0)
    gather_pass("wi", 2, 1)
    gather_pass("wi", 3, 0)
    gather_pass("wi", 2, 2)
    gather_pass("wi", 3, 1)
    rows_pass("x", X, 0)
    gather_pass("wi", 2, 3)
    gather_z("wq", 1)
    gather_x("wq", 1)

    def hidden_step(i, carry):
        early = i < 12
        u = jnp.where(early, i // 3, i - 12)
        at = jnp.where(early, i % 3, 3)
        w = at % 2
        t = jnp.where(at < 2, y, oy)

        @pl.when(i == 0)
        def _():
            gather_end("wi", 0)

        @pl.when(i == 2)
        def _():
            norm_far(0)

        @pl.when(i == 3)
        def _():
            gather_pass("wi", 3, 2)
            gather_end("wi", 1)

        @pl.when(i == 5)
        def _():
            gather_pass("wi", 3, 3)
            gather_z("wo", 0)
            gather_z("wo", 1)
            gather_pass("wq", 1, 0)

        @pl.when(i == 6)
        def _():
            gather_end("wi", 2)

        @pl.when(i == 7)
        def _():
            rows_pass("x", X, 1)

        @pl.when(i == 9)
        def _():
            gather_pass("wq", 2, 0)
            gather_end("wi", 3)

        @pl.when(i == 11)
        def _():
            gather_pass("wq", 3, 0)

        @pl.when(i == 12)
        def _():
            norm_far(1)

        @pl.when(i == 14)
        def _():
            gather_pass("wq", 1, 1)
            gather_x("wo", 1)

        r, l = rows(512 * t, 512), lanes(256 * u, 256)
        v = dot(N[w, r, :], Wi[:, l], 1, 0) + PR[3:4, l]
        value, slope = gelu_pair(v)
        A[w, r, l] = value.astype(BF)
        H[w, r, l] = slope.astype(BF)
        return carry

    lax.fori_loop(0, 16, hidden_step, 0)
    for w in range(2):
        rows_left("x", X, w)
    gather_end("wa", 0)
    start(lambda: link.copy("wac", 0, 1, WaAll.at[:, oc], Wa.at[:, c], core))
    Wa[:, c] = WaAll[:, c]
    for far in (2, 3):
        gather_pass("wq", far, 1)
    for u in range(2):
        gather_pass("wo", 1, u)

    def add_into(dst, other):
        dst[...] = (dst[...].astype(F32) + other[...].astype(F32)).astype(BF)

    inner = (z == 1) | (z == 2)

    def far_chip(tt):
        return 2 * (1 - z // 2) + tt

    def zchip(zz):
        return (2 * zz + xx, s)

    def o_near(q):
        return link.copy("op", 0, 1, GO.at[q, xx], ZO.at[0], zchip(pair))

    def o_comb(q):
        return link.copy("oc", q % 2, 2, GO.at[q, xx], CO.at[q % 2], zchip(pair))

    def o_far(q):
        return link.copy("of", q % 2, 2, GO.at[q, xx], ZO.at[1], zchip(q))

    def of_pair(p):
        return lambda: ("q", GQ.at[p], XQ.at[p], ZQ.at[p], CQ.at[p], p, 2)

    def of_attn():
        return "a", GA, XA, ZA, CA, 0, 1

    def z_near(get):
        name, group, _, landed, _, at, count = get()
        return link.copy(name + "p", at, count, group.at[xx, pair], landed.at[0], zchip(pair))

    def z_comb(get, tt):
        name, group, _, _, comb, at, count = get()
        block = group.at[xx, far_chip(tt)]
        return link.copy(name + "c", 2 * at + tt, 2 * count, block, comb.at[tt], zchip(pair))

    def z_far(get, tt, side):
        name, group, _, landed, _, at, count = get()
        block = group.at[xx, far_chip(tt)]
        return link.copy(
            name + "f", 2 * at + side, 2 * count, block, landed.at[1], zchip(far_chip(tt))
        )

    def z_first(get):
        _, group, received, _, _, _, _ = get()
        add_into(group.at[xx, pair], received.at[pair])
        z_near(get).start()
        for tt in range(2):
            add_into(group.at[xx, far_chip(tt)], received.at[far_chip(tt)])

            @pl.when(~inner)
            def _():
                z_comb(get, tt).start()

    def z_second(get):
        @pl.when(inner)
        def _():
            _, group, _, _, comb, _, _ = get()
            for tt in range(2):
                z_comb(get, tt).wait_recv()
                add_into(group.at[xx, far_chip(tt)], comb.at[tt])
                z_far(get, tt, tt).start()

    def z_total(get):
        _, group, received, landed, _, _, _ = get()
        z_near(get).wait_recv()
        z_far(get, 0, z % 2).wait_recv()
        total = group[xx, z].astype(F32) + received[z].astype(F32)
        return total + landed[0].astype(F32) + landed[1].astype(F32)

    def z_gone(get):
        z_near(get).wait_send()
        for tt in range(2):

            @pl.when(inner)
            def _():
                z_far(get, tt, tt).wait_send()

            @pl.when(~inner)
            def _():
                z_comb(get, tt).wait_send()

    def first_o(q):
        o_x(q).wait_recv()

        @pl.when(z != q)
        def _():
            add_into(GO.at[q, xx], XO.at[q])

            @pl.when(q == pair)
            def _():
                o_near(q).start()

            @pl.when((q != pair) & ~inner)
            def _():
                o_comb(q).start()

    def half_chip(tt):
        return 2 * (z // 2) + tt

    def i_near(q):
        return link.copy("ip", q, 4, GI.at[q, xx, pair], ZN.at[q], zchip(pair))

    def i_comb(q, tt):
        block = GI.at[q, xx, far_chip(tt)]
        return link.copy("ic", 2 * (q % 2) + tt, 4, block, CI.at[q % 2, tt], zchip(pair))

    def i_far(q, tt, side):
        block = GI.at[q, xx, far_chip(tt)]
        return link.copy("if", 2 * (q % 2) + side, 4, block, ZF.at[q % 2], zchip(far_chip(tt)))

    def i_straight(q, tt, sender, side):
        block = GI.at[q, xx, far_chip(tt)]
        return link.copy(
            "id", 4 * (q % 2) + 2 * sender + side, 8, block, ZD.at[q % 2, sender], zchip(far_chip(tt))
        )

    def first_i(q, far):
        i_x(q).wait_recv()
        add_into(GI.at[q, xx, pair], XI.at[q, pair])
        i_near(q).start()
        for tt in range(2):
            add_into(GI.at[q, xx, far_chip(tt)], XI.at[q, far_chip(tt)])
            if far:

                @pl.when(~inner)
                def _():
                    i_comb(q, tt).start()

            else:
                i_straight(q, tt, z % 2, tt).start()

    def second_i(q):
        @pl.when(inner)
        def _():
            for tt in range(2):
                i_comb(q, tt).wait_recv()
                add_into(GI.at[q, xx, far_chip(tt)], CI.at[q % 2, tt])
                i_far(q, tt, tt).start()

    def total_i(q, far):
        i_near(q).wait_recv()
        total = GI[q, xx, z].astype(F32) + XI[q, z].astype(F32) + ZN[q].astype(F32)
        if far:
            for sender in range(2):
                i_straight(q, 0, sender, z % 2).wait_recv()
                total = total + ZD[q % 2, sender].astype(F32)
            return total
        i_far(q, 0, z % 2).wait_recv()
        return total + ZF[q % 2].astype(F32)

    def second_z(q):
        @pl.when(inner)
        def _():
            o_comb(q).wait_recv()
            add_into(GO.at[q, xx], CO.at[q % 2])
            o_far(q).start()

    def z_left():
        o_near(pair).wait_send()
        for tt in range(2):

            @pl.when(inner)
            def _():
                o_far(far_chip(tt)).wait_send()

            @pl.when(~inner)
            def _():
                o_comb(far_chip(tt)).wait_send()

        for q in range(4):
            i_near(q).wait_send()
        for a in range(2):
            for tt in range(2):
                i_straight(half_chip(a), tt, z % 2, tt).wait_send()

                @pl.when(inner)
                def _():
                    i_far(far_chip(a), tt, tt).wait_send()

                @pl.when(~inner)
                def _():
                    i_comb(far_chip(a), tt).wait_send()

        for p in range(2):
            z_gone(of_pair(p))
        z_gone(of_attn)

    def chunk(j):
        return jnp.where(j == 3, z, jnp.where(j == 2, pair, far_chip(0) + j))

    def o_x(q):
        return link.copy("ox", q, 4, GO.at[q, ox], XO.at[q], xpart)

    def i_x(q):
        return link.copy("ix", q, 4, GI.at[q, ox], XI.at[q], xpart)

    even = lax.broadcasted_iota(jnp.int32, (1, 128), 1) % 2 == 0

    def turn_rows(r):
        table = turns[r, :]
        other = pltpu.roll(table, 64, 1)
        low = lax.broadcasted_iota(jnp.int32, (1, 128), 1) < 64
        return jnp.where(low, table, other), jnp.where(low, other, table)

    def turn(v, cos_rows, sin_rows):
        swapped = jnp.where(even, pltpu.roll(v, 127, 1), pltpu.roll(v, 1, 1))
        return v * cos_rows + swapped * sin_rows

    def qkv_step(p):
        gather_end("wq", p)
        l = slice(384 * p, 384 * p + 384)

        def step(i, carry):
            w, r = i // 4, rows(256 * (i % 4), 256)
            v = dot(N[w, r, :], Wq[:, l], 1, 0)
            cos_rows, sin_rows = turn_rows(r)
            for kind in range(3):
                tile_v = v[:, 128 * kind : 128 * kind + 128]
                if kind < 2:
                    tile_v = turn(tile_v, cos_rows, sin_rows)
                if kind == 0:
                    tile_v = tile_v * 0.125
                QKV[w, r, 384 * p + 128 * kind : 384 * p + 128 * kind + 128] = tile_v.astype(BF)
            return carry

        lax.fori_loop(0, 8, step, 0)

    qkv_step(0)
    for w in range(2):
        rows_end_core("g", G, w)
    rows_pass("g", G, 0)
    for u in range(4):
        seq_left(
            "wis%d" % u, lambda owner: PWI.at[owner, :, 256 * u : 256 * u + 256], lambda: wi_block(s, u)
        )
    link.copy("wac", 0, 1, WaAll.at[:, oc], Wa.at[:, oc], core).wait_recv()
    TAIL[...] = jnp.zeros_like(TAIL)

    def do_step(w):
        def step(i, total):
            r = rows(512 * i, 512)
            g = G[w, r, :]
            dO[w, r, :] = dot(g, Wa[...].reshape(256, 1024), 1, 1).astype(BF)
            return total + jnp.sum(g.astype(F32), axis=0, keepdims=True)

        TAIL[2:3, :] += lax.fori_loop(0, 2, step, jnp.zeros((1, 1024), F32))

    rows_end_far("g", G, 0)
    do_step(0)
    gather_pass("wo", 2, 0)

    def units_back(j):
        q = chunk(j)
        l = lanes(256 * q, 256)

        def step(w, total):
            d = dot(G[w], Wo[rows(256 * q, 256), :], 1, 1) * H[w, :, l].astype(F32)
            d = d.astype(BF)
            H[w, :, l] = d
            return total + jnp.sum(d.astype(F32), axis=0, keepdims=True)

        TAIL[3:4, l] = lax.fori_loop(0, 2, step, jnp.zeros((1, 256), F32))

    def units_out(j):
        q = chunk(j)
        l = lanes(256 * q, 256)
        go = dot(A[0, :, l], G[0], 0, 0) + dot(A[1, :, l], G[1], 0, 0)
        GO[q, 0] = go[:128].astype(BF)
        GO[q, 1] = go[128:].astype(BF)

    def units_in(j):
        q = chunk(j)
        l = lanes(256 * q, 256)
        gi = dot(H[0, :, l], N[0], 0, 0) + dot(H[1, :, l], N[1], 0, 0)
        for bb in range(8):
            GI[q, bb % 2, bb // 2] = gi[:, 128 * bb : 128 * bb + 128].astype(BF)

    lane = lax.broadcasted_iota(jnp.int32, (1, 128), 1)
    place = lax.broadcasted_iota(jnp.int32, (S, 1), 0)
    BQ = 256
    key_i = lax.broadcasted_iota(jnp.int32, (BQ, BQ), 0)
    query_i = lax.broadcasted_iota(jnp.int32, (BQ, BQ), 1)
    inside = [(lane // 64) == hh for hh in range(2)]
    feature = [lane == (64 - 64 * hh) for hh in range(2)]

    def attend(w, p):
        ending = ends[w]

        def part(kind):
            return lanes(384 * p + 128 * kind)

        pl_ = lanes(128 * p)
        keys = QKV[w, :, part(1)]
        ktT[...] = keys.T
        vtT[...] = QKV[w, :, part(2)].T
        doT[...] = dO[w, :, pl_].T
        dkA[...] = jnp.zeros_like(dkA)
        dvA[...] = jnp.zeros_like(dvA)
        keys_f = keys.astype(F32)
        before = jnp.where(place < ending, NEG, 0.0)
        for hh in range(2):
            khat[hh] = jnp.where(inside[hh], keys_f, jnp.where(feature[hh], before, 0.0)).astype(BF)

        def begin(qb, hh):
            qr, nk = slice(qb * BQ, (qb + 1) * BQ), (qb + 1) * BQ
            q = QKV[w, qr, part(0)].astype(F32)
            after = jnp.where(place[qr] >= ending, 1.0, 0.0)
            q_in = jnp.where(inside[hh], q, 0.0).astype(BF)
            q_hat = jnp.where(inside[hh], q, jnp.where(feature[hh], after, 0.0)).astype(BF)
            d_in = jnp.where(inside[hh], dO[w, qr, pl_].astype(F32), 0.0).astype(BF)
            return dot(khat[hh, 0:nk, :], q_hat, 1, 1), dot(QKV[w, 0:nk, part(2)], d_in, 1, 1), q_in, d_in

        units = [(qb, hh) for qb in range(S // BQ) for hh in range(2)]
        upcoming, late = begin(*units[0]), None
        for i, (qb, hh) in enumerate(units):
            sc, dp, q_in, d_in = upcoming
            qr, nk = slice(qb * BQ, (qb + 1) * BQ), (qb + 1) * BQ
            hr = slice(64 * hh, 64 * hh + 64)
            if i + 1 < len(units):
                upcoming = begin(*units[i + 1])
            last = jnp.where(key_i <= query_i, sc[nk - BQ :], NEG)
            sc = last if qb == 0 else jnp.concatenate([sc[: nk - BQ], last], axis=0)
            e = jnp.exp(sc - jnp.max(sc, axis=0, keepdims=True))
            pn = e * (1.0 / jnp.sum(e, axis=0, keepdims=True))
            pb = pn.astype(BF)
            o = dot(vtT[hr, 0:nk], pb, 1, 0)
            if late is not None:
                late()
            oT[hr, qr] = o
            dd = jnp.sum(o * doT[hr, qr].astype(F32), axis=0, keepdims=True)
            ds = (pn * (dp - dd)).astype(BF)

            def late(hr=hr, qr=qr, nk=nk, ds=ds, pb=pb, q_in=q_in, d_in=d_in):
                dqT[hr, qr] = dot(ktT[hr, 0:nk], ds, 1, 0)
                dkA[0:nk, :] += dot(ds, q_in, 1, 0)
                dvA[0:nk, :] += dot(pb, d_in, 1, 0)

        late()
        cos_rows, sin_rows = turn_rows(slice(None))
        sin_rows = -sin_rows
        att[w, :, pl_] = oT[...].T.astype(BF)
        QKV[w, :, part(0)] = turn(dqT[...].T * 0.125, cos_rows, sin_rows).astype(BF)
        QKV[w, :, part(1)] = turn(dkA[...], cos_rows, sin_rows).astype(BF)
        QKV[w, :, part(2)] = dvA[...].astype(BF)

    shares = (A, H)

    def share_c(w, t, yy):
        src = shares[t].at[w, rows(SL * (2 * yy + oc), SL)]
        dst = X.at[w, rows(SL * (2 * t + yy), SL)]
        link.copy("sc", 4 * w + 2 * t + yy, 8, src, dst, core).start()

    def share_got(w, t, yy):
        slot = X.at[w, rows(SL * (2 * t + yy), SL)]
        link.copy("sc", 4 * w + 2 * t + yy, 8, slot, slot, core).wait_recv()
        return slot

    def share_y(w, t):
        src = shares[t].at[w, rows(SL * (2 * oy + c), SL)]
        add_into(src, share_got(w, t, oy))
        link.copy("sy", 2 * w + t, 4, src, YR.at[w, t], ypart).start()

    def share_out(w, r):
        value = dot(A[w, r, :], Wo[...], 1, 0) + dot(att[w, r, :], Wa[...].reshape(256, 1024), 1, 0)
        A[w, r, :] = value.astype(BF)

    def share_normed(w, r):
        d = dot(H[w, r, :], Wi[...], 1, 1) + dot(QKV[w, r, :], Wq[...], 1, 1)
        H[w, r, :] = d.astype(BF)
        n = (N[w, r, :].astype(F32) - PR[1:2, :]) / PR[0:1, :]
        TAIL[0:1, :] += jnp.sum(d, axis=0, keepdims=True)
        TAIL[1:2, :] += jnp.sum(d * n, axis=0, keepdims=True)

    def share_step(w, t, between=None):
        def step(i, carry):
            yy = jnp.where(i < 2, oy, y)
            cc = jnp.where(i % 2 == 0, oc, c)
            (share_out, share_normed)[t](w, rows(SL * (2 * yy + cc), SL))

            @pl.when(i == 0)
            def _():
                share_c(w, t, oy)

            if between is not None:
                pl.when(i == 1)(between)

            @pl.when(i == 2)
            def _():
                share_y(w, t)
                share_c(w, t, y)

            return carry

        lax.fori_loop(0, 4, step, 0)

    def gq_step(p):
        l = slice(384 * p, 384 * p + 384)
        gq = dot(QKV[0, :, l], N[0], 0, 0) + dot(QKV[1, :, l], N[1], 0, 0)
        for bb in range(8):
            GQ[p, bb % 2, bb // 2] = gq[:, 128 * bb : 128 * bb + 128].astype(BF)
        link.copy("qx", p, 2, GQ.at[p, ox], XQ.at[p], xpart).start()

    def ga_c(p):
        two = slice(2 * p, 2 * p + 2)
        return link.copy("core_a", p, 2, PWI.at[two], GA.at[c, two], core)

    def ga_x(p):
        two = slice(2 * p, 2 * p + 2)
        return link.copy("x_a", p, 2, GA.at[ox, two], XA.at[two], xpart)

    def ga_step(p):
        l = slice(128 * p, 128 * p + 128)
        ga = dot(att[0, :, l], G[0], 0, 0) + dot(att[1, :, l], G[1], 0, 0)
        for j in range(2):
            for cc in range(2):
                piece = ga[64 * j + 32 * cc : 64 * j + 32 * cc + 32].astype(BF)

                @pl.when(cc == c)
                def _():
                    GA[c, 2 * p + j] = piece

                @pl.when(cc != c)
                def _():
                    PWI[2 * p + j] = piece

        ga_c(p).start()

    def ga_send(p):
        ga_c(p).wait_recv()
        ga_x(p).start()

    def first_q(p):
        link.copy("qx", p, 2, GQ.at[p, ox], XQ.at[p], xpart).wait_recv()
        z_first(of_pair(p))

    def first_a():
        for p in range(2):
            ga_x(p).wait_recv()
        z_first(of_attn)

    def attend_step(i, carry):
        w, p = i // 2, i % 2
        attend(w, p)

        @pl.when(i == 0)
        def _():
            gather_pass("wo", 2, 1)
            gather_pass("wo", 3, 0)
            rows_pass("g", G, 1)
            qkv_step(1)
            gather_pass("wo", 3, 1)
            rows_end_far("g", G, 1)
            for j in range(2):
                units_out(j)
                o_x(chunk(j)).start()

        @pl.when(i == 1)
        def _():
            do_step(1)

        @pl.when(i == 2)
        def _():
            gq_step(0)
            ga_step(0)
            for j in range(2, 4):
                units_out(j)
            for u in range(2):
                for zz in range(4):
                    gather_block("wo", zz, u)
            share_step(0, 0)
            first_o(chunk(0))
            first_o(chunk(1))
            ga_send(0)

        return carry

    lax.fori_loop(0, 4, attend_step, 0)
    gq_step(1)
    ga_step(1)

    def in_step(j, carry):
        units_back(j)
        units_in(j)
        i_x(chunk(j)).start()

        @pl.when(j == 0)
        def _():
            z_second(of_pair(0))

        @pl.when(j == 1)
        def _():
            first_q(1)

        @pl.when(j == 2)
        def _():
            first_a()

        return carry

    written = []

    def write(src, dst):
        cp = pltpu.make_async_copy(src, dst, out_sems.at[len(written)])
        cp.start()
        written.append(cp)
        return cp

    def to_seq(name, held, landed):
        landed[s] = held[s]
        seq_sends(name, lambda owner: held.at[owner], lambda: landed.at[s])

    def from_seq(name, landed):
        for i, owner in enumerate((2 * y + oc, 2 * oy + c, 2 * oy + oc)):
            link.copy(name, i, 3, landed.at[owner], landed.at[owner], core).wait_recv()

    second_z(chunk(0))
    first_q(0)
    ga_send(1)
    second_z(chunk(1))
    share_step(1, 0)
    lax.fori_loop(0, 4, in_step, 0)
    for j in range(2, 4):
        o_x(chunk(j)).start()

    def between_first():
        first_i(chunk(0), True)
        z_second(of_pair(1))
        z_second(of_attn)

    def between_second():
        first_i(chunk(1), True)
        second_i(chunk(0))

    share_step(0, 1, between_first)
    share_step(1, 1, between_second)
    for p in range(2):
        total_q = z_total(of_pair(p)).T.astype(BF)
        for owner in range(4):
            SWQ[owner, :, 384 * p : 384 * p + 384] = total_q[32 * owner : 32 * owner + 32]
    to_seq("swq", SWQ, RWQ)
    again = [
        pltpu.make_async_copy(x_in.at[w], N.at[w, 0:SL], local_sems.at[3 * w + 2]) for w in range(2)
    ]
    for cp in again:
        cp.start()
    tail = TAIL[...]
    for bb in range(8):
        GT[bb % 2, bb // 2] = tail[:, 128 * bb : 128 * bb + 128].astype(BF)
    for k in (1, 2, 3):
        start(lambda k=k: link.copy("tz", k - 1, 3, GT.at[:, (z + k) % 4], ZT.at[k - 1], zdev(k)))

    def tail_x():
        for k in (1, 2, 3):
            link.copy("tz", k - 1, 3, ZT.at[k - 1], ZT.at[k - 1], core).wait_recv()
        add_into(ZT.at[0], GT.at[:, z])
        add_into(ZT.at[1], ZT.at[2])
        add_into(ZT.at[0], ZT.at[1])
        start(lambda: link.copy("tx", 0, 1, ZT.at[0, ox], XT, xpart))

    def final_o():
        o_near(z).wait_recv()
        link.copy("of", z % 2, 2, ZO.at[1], ZO.at[1], core).wait_recv()
        dqT[...] = (
            GO[z, xx].astype(F32) + XO[z].astype(F32) + ZO[0].astype(F32) + ZO[1].astype(F32)
        )

    def final_i():
        for tt in range(2):
            for q, far in ((half_chip(tt), False), (far_chip(tt), True)):
                turned = total_i(q, far).T.astype(BF)
                for owner in range(4):
                    SWI[owner, :, lanes(256 * q, 256)] = turned[32 * owner : 32 * owner + 32]

    def final_rows(w):
        again[w].wait()
        v = N[w, 0:SL, :].astype(F32)
        mine = rows(SL * s, SL)
        for t in (1, 0):
            share_got(w, t, y)
            link.copy("sy", 2 * w + t, 4, YR.at[w, t], YR.at[w, t], core).wait_recv()
        value = (
            A[w, mine, :].astype(F32)
            + X[w, rows(SL * y, SL), :].astype(F32)
            + YR[w, 0].astype(F32)
        )
        A[w, mine, :] = (v + value + PR[2:3, :]).astype(BF)
        d = (
            H[w, mine, :].astype(F32)
            + X[w, rows(SL * (2 + y), SL), :].astype(F32)
            + YR[w, 1].astype(F32)
        )
        v = v - jnp.mean(v, axis=-1, keepdims=True)
        scale = lax.rsqrt(jnp.mean(v * v, axis=-1, keepdims=True) + norm_eps)
        v = v * scale
        d = d * PR[0:1, :]
        d = d - jnp.mean(d, axis=-1, keepdims=True) - v * jnp.mean(d * v, axis=-1, keepdims=True)
        grad_in[...] = G[w, mine, :].astype(F32) + scale * d
        write(A.at[w, own], out_hbm.at[w])
        return write(grad_in, grad_in_hbm.at[w])

    first_i(chunk(2), False)
    second_i(chunk(1))
    grad_a[...] = z_total(of_attn)
    write(grad_a, grad_a_hbm)
    first_i(chunk(3), False)
    first_o(chunk(2))
    first_rows = final_rows(0)
    tail_x()
    final_i()
    to_seq("swi", SWI, RWI)
    first_rows.wait()
    final_rows(1)
    from_seq("swq", RWQ)
    got = [RWQ[r].astype(F32) for r in range(4)]
    place_of = {}
    for r in range(4):
        for j in range(4):
            for kind in range(3):
                place_of[3 * head_of(r, j) + kind] = (got[r], 384 * (j // 2) + 128 * kind + 64 * (j % 2))
    for at in range(24):
        grad_q[:, 128 * at : 128 * at + 128] = halves(place_of[2 * at], place_of[2 * at + 1])
    write(grad_q, grad_q_hbm)
    link.copy("tx", 0, 1, XT, XT, core).wait_recv()
    total_t = ZT[0, xx].astype(F32) + XT[...].astype(F32)
    turned_t = jnp.concatenate([total_t, jnp.zeros((112, 128), F32)], axis=0).T.astype(BF)
    for owner in range(4):
        SWT[owner] = turned_t[32 * owner : 32 * owner + 32]
    to_seq("swt", SWT, RWT)
    first_o(chunk(3))
    final_o()
    write(dqT, grad_o_hbm)
    from_seq("swi", RWI)
    for r in range(4):
        for blk in range(8):
            at = 512 * blk + 128 * r
            oT[32 * (at // 1024) : 32 * (at // 1024) + 32, at % 1024 : at % 1024 + 128] = RWI[
                r, :, 128 * blk : 128 * blk + 128
            ].astype(F32)
    for q in range(4):
        write(oT.at[32 * q : 32 * q + 32], grad_i_hbm.at[:, 1024 * q : 1024 * q + 1024])

    from_seq("swt", RWT)
    mine = RWT[0].astype(F32)
    summed = mine + RWT[1].astype(F32) + RWT[2].astype(F32) + RWT[3].astype(F32)
    summed = jnp.where(lane == 2, mine, summed)
    summed = jnp.concatenate([summed, jnp.zeros((96, 128), F32)], axis=0).T
    grad_small[...] = jnp.where(lax.broadcasted_iota(jnp.int32, (8, 128), 0) < 3, summed[0:8], total_t[0:8])
    write(grad_small, grad_small_hbm)

    for make in pending:
        make().wait_send()
    seq_left("prms", lambda owner: prm_block(s), lambda: prm_block(s))
    seq_left("wqs", lambda owner: PWQ.at[owner], lambda: wq_block(s))
    seq_left("swi", lambda owner: SWI.at[owner], lambda: RWI.at[s])
    seq_left("swq", lambda owner: SWQ.at[owner], lambda: RWQ.at[s])
    seq_left("swt", lambda owner: SWT.at[owner], lambda: RWT.at[s])
    for name, (parts, _) in gathers.items():
        for u in range(parts):
            gather_left(name, u)
    for w in range(2):
        rows_left("g", G, w)
    for q in range(4):
        link.copy("ox", q, 4, GO.at[q, ox], XO.at[q], xpart).wait_send()
        link.copy("ix", q, 4, GI.at[q, ox], XI.at[q], xpart).wait_send()
    z_left()
    for w in range(2):
        for t in range(2):
            for yy in range(2):
                src = shares[t].at[w, rows(SL * (2 * yy + oc), SL)]
                dst = X.at[w, rows(SL * (2 * t + yy), SL)]
                link.copy("sc", 4 * w + 2 * t + yy, 8, src, dst, core).wait_send()
            src = shares[t].at[w, rows(SL * (2 * oy + c), SL)]
            link.copy("sy", 2 * w + t, 4, src, YR.at[w, t], ypart).wait_send()
    for p in range(2):
        link.copy("qx", p, 2, GQ.at[p, ox], XQ.at[p], xpart).wait_send()
        ga_c(p).wait_send()
        ga_x(p).wait_send()
    for cp in written:
        if cp is not first_rows:
            cp.wait()


def publish(*refs):
    sources, targets, (in_sems, out_sems) = refs[:7], refs[7:17], refs[28:]
    held, row_held = refs[17:24], refs[24:28]
    arrive = [pltpu.make_async_copy(sources[i], held[i], in_sems.at[i]) for i in range(7)]
    leave = [pltpu.make_async_copy(held[i], targets[i], out_sems.at[i]) for i in range(6)]
    leave += [
        pltpu.make_async_copy(row_held[i], targets[6 + i], out_sems.at[6 + i]) for i in range(4)
    ]
    largest_first = (1, 0, 4, 5, 2, 3)
    for i in (6,) + largest_first:
        arrive[i].start()
    arrive[6].wait()
    for i in range(4):
        row_held[i][...] = held[6][i : i + 1, 0 : row_held[i].shape[1]]
        leave[6 + i].start()
    for i in largest_first:
        arrive[i].wait()
        leave[i].start()
    for cp in leave:
        cp.wait()


def turn_tables(seq_len):
    inverse = 10000.0 ** (-2.0 * np.arange(ROTARY // 2) / ROTARY)
    angles = np.arange(seq_len)[:, None] * inverse[None, :]
    cosine = np.ones((seq_len, HD), np.float32)
    sine = np.zeros((seq_len, HD), np.float32)
    cosine[:, 0:ROTARY:2] = cosine[:, 1:ROTARY:2] = np.cos(angles)
    sine[:, 0:ROTARY:2] = -np.sin(angles)
    sine[:, 1:ROTARY:2] = np.sin(angles)
    return np.concatenate([cosine, sine], axis=1)


def fused_shards(inputs, ends, ln_gain, ln_bias, w_qkv, w_attn, w_in, b_in, w_out, b_out, cotangent):
    in_vmem = pl.BlockSpec(memory_space=pltpu.VMEM)
    in_any = pl.BlockSpec(memory_space=pl.ANY)
    rows_type = (2, 1024, 1024)
    shapes = (
        jax.ShapeDtypeStruct((2, 256, 1024), BF),
        jax.ShapeDtypeStruct((2, 256, 1024), F32),
        jax.ShapeDtypeStruct((32, 3072), F32),
        jax.ShapeDtypeStruct((32, 1024), F32),
        jax.ShapeDtypeStruct((32, 4096), F32),
        jax.ShapeDtypeStruct((128, 1024), F32),
    )
    results = pl.pallas_call(
        fused_layer,
        out_shape=shapes + (jax.ShapeDtypeStruct((8, 128), F32),),
        in_specs=[pl.BlockSpec(memory_space=pltpu.SMEM)] + [in_vmem] * 9 + [in_any] * 2,
        out_specs=(in_any,) * 7,
        scratch_shapes=[
            pltpu.VMEM(rows_type, BF),
            pltpu.VMEM(rows_type, BF),
            pltpu.VMEM(rows_type, BF),
            pltpu.VMEM(rows_type, BF),
            pltpu.VMEM(rows_type, BF),
            pltpu.VMEM((1024, 1024), BF),
            pltpu.VMEM((1024, 1024), BF),
            pltpu.VMEM((1024, 768), BF),
            pltpu.VMEM((4, 2, 32, 1024), BF),
            pltpu.VMEM((4, 2, 32, 1024), BF),
            pltpu.VMEM((4, 32, 1024), BF),
            pltpu.VMEM((4, 32, 768), BF),
            pltpu.VMEM((4, 16, 128), BF),
            pltpu.VMEM((8, 16, 128), BF),
            pltpu.VMEM((8, 1024), F32),
            pltpu.VMEM((2, 1024, 768), BF),
            pltpu.VMEM((2, 1024, 256), BF),
            pltpu.VMEM((2, 1024, 256), BF),
            pltpu.VMEM((4, 2, 128, 1024), BF),
            pltpu.VMEM((4, 128, 1024), BF),
            pltpu.VMEM((2, 128, 1024), BF),
            pltpu.VMEM((2, 128, 1024), BF),
            pltpu.VMEM((4, 2, 4, 256, 128), BF),
            pltpu.VMEM((4, 4, 256, 128), BF),
            pltpu.VMEM((4, 256, 128), BF),
            pltpu.VMEM((2, 256, 128), BF),
            pltpu.VMEM((2, 2, 256, 128), BF),
            pltpu.VMEM((2, 2, 256, 128), BF),
            pltpu.VMEM((2, 2, 4, 384, 128), BF),
            pltpu.VMEM((2, 4, 384, 128), BF),
            pltpu.VMEM((2, 2, 384, 128), BF),
            pltpu.VMEM((2, 2, 384, 128), BF),
            pltpu.VMEM((2, 4, 32, 1024), BF),
            pltpu.VMEM((4, 32, 1024), BF),
            pltpu.VMEM((2, 32, 1024), BF),
            pltpu.VMEM((2, 32, 1024), BF),
            pltpu.VMEM((2, 4, 16, 128), BF),
            pltpu.VMEM((16, 128), BF),
            pltpu.VMEM((3, 2, 16, 128), BF),
            pltpu.VMEM((2, 2, 256, 1024), BF),
            pltpu.VMEM((4, 32, 1024), BF),
            pltpu.VMEM((4, 32, 1024), BF),
            pltpu.VMEM((4, 32, 768), BF),
            pltpu.VMEM((4, 32, 768), BF),
            pltpu.VMEM((4, 32, 128), BF),
            pltpu.VMEM((4, 32, 128), BF),
            pltpu.VMEM((16, 1024), F32),
            pltpu.VMEM((2, 1024, 128), BF),
            pltpu.VMEM((128, 1024), BF),
            pltpu.VMEM((128, 1024), BF),
            pltpu.VMEM((128, 1024), BF),
            pltpu.VMEM((128, 1024), F32),
            pltpu.VMEM((128, 1024), F32),
            pltpu.VMEM((1024, 128), F32),
            pltpu.VMEM((1024, 128), F32),
            pltpu.VMEM((256, 1024), F32),
            pltpu.VMEM((32, 3072), F32),
            pltpu.VMEM((32, 1024), F32),
            pltpu.VMEM((8, 128), F32),
            pltpu.SemaphoreType.DMA((192,)),
            pltpu.SemaphoreType.DMA((192,)),
            pltpu.SemaphoreType.DMA((6,)),
            pltpu.SemaphoreType.DMA((14,)),
        ],
        compiler_params=pltpu.CompilerParams(
            collective_id=0, has_side_effects=True, vmem_limit_bytes=65400 * 2**10
        ),
        cost_estimate=pl.CostEstimate(flops=46 * 10**9, bytes_accessed=10**7, transcendentals=10**7),
    )(
        ends,
        ln_gain.reshape(1, 32),
        ln_bias.reshape(1, 32),
        b_out.reshape(1, 32),
        b_in.reshape(1, 128),
        w_qkv, w_attn, w_in, w_out, turn_tables(1024), inputs, cotangent)
    row = jax.ShapeDtypeStruct((1, 32), F32)
    rows_out = (row, row, row, jax.ShapeDtypeStruct((1, 128), F32))
    held = shapes + (jax.ShapeDtypeStruct((8, 128), F32),) + rows_out
    final = pl.pallas_call(
        publish,
        out_shape=shapes + rows_out,
        in_specs=[in_any] * 7,
        out_specs=(in_any,) * 10,
        scratch_shapes=[pltpu.VMEM(v.shape, v.dtype) for v in held]
        + [pltpu.SemaphoreType.DMA((7,)), pltpu.SemaphoreType.DMA((10,))],
        compiler_params=pltpu.CompilerParams(vmem_limit_bytes=60 * 2**20),
    )(*results)
    out, grad_in, grad_q, grad_a, grad_i, grad_o, bias, gain, bias_out, bias_in = final
    return (
        out,
        grad_in,
        gain.reshape(32),
        bias.reshape(32),
        grad_q,
        grad_a,
        grad_i,
        bias_in.reshape(128),
        grad_o,
        bias_out.reshape(32),
    )


def fits_fused(mesh):
    return mesh.shape["batch"] == 8 and mesh.shape["seq"] == 4


def solution(mesh):
    return jax.shard_map(
        fused_shards if fits_fused(mesh) else shards,
        mesh=mesh,
        in_specs=(
            P("batch", "seq", None),
            P("batch"),
            P(("batch", "seq")),
            P(("batch", "seq")),
            P(("batch", "seq"), None),
            P(("batch", "seq"), None),
            P(("batch", "seq"), None),
            P(("batch", "seq")),
            P(("batch", "seq"), None),
            P(("batch", "seq")),
            P("batch", "seq", None),
        ),
        out_specs=(
            P("batch", "seq", None),
            P("batch", "seq", None),
            P(("batch", "seq")),
            P(("batch", "seq")),
            P(("batch", "seq"), None),
            P(("batch", "seq"), None),
            P(("batch", "seq"), None),
            P(("batch", "seq")),
            P(("batch", "seq"), None),
            P(("batch", "seq")),
        ),
        check_vma=False,
    )
```

```python
import math

import jax
import jax.numpy as jnp
import numpy as np
from jax import lax
from jax.experimental import pallas as pl
from jax.experimental.pallas import tpu as pltpu
from jax.sharding import PartitionSpec as P

HEADS = 16
HD = 64
ROTARY = 32
MICRO = 2


norm_eps = 1e-05
gelu_factor = 0.7978845608028654
masked_score = -1e30


def gelu_tanh(values):
    return (
        0.5
        * values
        * (1.0 + jnp.tanh(gelu_factor * (values + 0.044715 * values * values * values)))
    )


def layer_norm(row_values, norm_gain, norm_shift):
    average = jnp.mean(row_values, axis=-1, keepdims=True)
    centered = row_values - average
    variance = jnp.mean(centered * centered, axis=-1, keepdims=True)
    return centered * lax.rsqrt(variance + norm_eps) * norm_gain + norm_shift


def rotary_tables(positions):
    pair_index = jnp.arange(ROTARY // 2, dtype=jnp.float32)
    inverse = 10000.0 ** (-2.0 * pair_index / ROTARY)
    angles = positions[:, None] * inverse[None, :]
    return (jnp.cos(angles), jnp.sin(angles))


def rotate(vectors, cosine, sine_table):
    rotated = vectors[..., :ROTARY]
    even_part = rotated[..., 0::2]
    odd_part = rotated[..., 1::2]
    cosine_wide = cosine[:, None, :]
    sine_wide = sine_table[:, None, :]
    new_even = even_part * cosine_wide - odd_part * sine_wide
    new_odd = odd_part * cosine_wide + even_part * sine_wide
    merged = jnp.stack([new_even, new_odd], axis=-1).reshape(rotated.shape)
    return jnp.concatenate([merged, vectors[..., ROTARY:]], axis=-1)


def visible(query_places, key_places, ending):
    query_after = query_places[:, None] >= ending
    key_after = key_places[None, :] >= ending
    return (key_places[None, :] <= query_places[:, None]) & (query_after == key_after)


def block_scores(block_queries, key_vectors, query_places, key_places, ending, score_scale):
    scores = (
        jnp.einsum("qhd,khd->hqk", block_queries, key_vectors, preferred_element_type=jnp.float32)
        * score_scale
    )
    return jnp.where(visible(query_places, key_places, ending)[None], scores, masked_score)


def attend_forward(packed, ending):
    seq_len, head_count, triple = packed.shape
    head_size = triple // 3
    block_rows = min(512, seq_len)
    score_scale = 1.0 / math.sqrt(head_size)
    queries = packed[:, :, :head_size]
    key_vectors = packed[:, :, head_size : 2 * head_size]
    values = packed[:, :, 2 * head_size :]
    key_places = jnp.arange(seq_len, dtype=jnp.int32)

    def one_block(block_index):
        first_row = block_index * block_rows
        block_queries = lax.dynamic_slice_in_dim(queries, first_row, block_rows, 0)
        query_places = first_row + jnp.arange(block_rows, dtype=jnp.int32)
        scores = block_scores(
            block_queries, key_vectors, query_places, key_places, ending, score_scale
        )
        row_peak = jnp.max(scores, axis=-1, keepdims=True)
        weights = jnp.exp(scores - row_peak)
        row_total = jnp.sum(weights, axis=-1, keepdims=True)
        probabilities = (weights / row_total).astype(jnp.bfloat16)
        result = jnp.einsum(
            "hqk,khd->qhd", probabilities, values, preferred_element_type=jnp.float32
        )
        return (result.astype(jnp.bfloat16), row_peak, row_total)

    results, peaks, totals = lax.map(one_block, jnp.arange(seq_len // block_rows, dtype=jnp.int32))
    return (results.reshape(seq_len, head_count, head_size), peaks, totals)


def attend_backward(packed, d_attended, peaks, totals, ending, full_cosine, full_sine):
    seq_len, head_count, triple = packed.shape
    head_size = triple // 3
    block_rows = min(512, seq_len)
    score_scale = 1.0 / math.sqrt(head_size)
    queries = packed[:, :, :head_size]
    key_vectors = packed[:, :, head_size : 2 * head_size]
    values = packed[:, :, 2 * head_size :]
    key_places = jnp.arange(seq_len, dtype=jnp.int32)

    def one_block(running, block_inputs):
        key_grads, value_grads = running
        block_index, row_peak, row_total = block_inputs
        first_row = block_index * block_rows
        block_queries = lax.dynamic_slice_in_dim(queries, first_row, block_rows, 0)
        block_grads = lax.dynamic_slice_in_dim(d_attended, first_row, block_rows, 0)
        query_places = first_row + jnp.arange(block_rows, dtype=jnp.int32)
        scores = block_scores(
            block_queries, key_vectors, query_places, key_places, ending, score_scale
        )
        probabilities = jnp.exp(scores - row_peak) / row_total
        rounded_probs = probabilities.astype(jnp.bfloat16)
        d_probs = jnp.einsum(
            "qhd,khd->hqk", block_grads, values, preferred_element_type=jnp.float32
        )
        row_dot = jnp.sum(probabilities * d_probs, axis=-1, keepdims=True)
        d_scores = (probabilities * (d_probs - row_dot)).astype(jnp.bfloat16)
        query_grads = (
            jnp.einsum("hqk,khd->qhd", d_scores, key_vectors, preferred_element_type=jnp.float32)
            * score_scale
        )
        key_grads = (
            key_grads
            + jnp.einsum(
                "hqk,qhd->khd", d_scores, block_queries, preferred_element_type=jnp.float32
            )
            * score_scale
        )
        value_grads = value_grads + jnp.einsum(
            "hqk,qhd->khd", rounded_probs, block_grads, preferred_element_type=jnp.float32
        )
        return ((key_grads, value_grads), query_grads)

    zero_sums = jnp.zeros((seq_len, head_count, head_size), jnp.float32)
    block_ids = jnp.arange(seq_len // block_rows, dtype=jnp.int32)
    (key_grads, value_grads), query_grads = lax.scan(
        one_block, (zero_sums, zero_sums), (block_ids, peaks, totals)
    )
    query_grads = query_grads.reshape(seq_len, head_count, head_size)
    flipped_sine = -full_sine
    combined = jnp.stack(
        [
            rotate(query_grads, full_cosine, flipped_sine),
            rotate(key_grads, full_cosine, flipped_sine),
            value_grads,
        ],
        axis=2,
    )
    return combined.astype(jnp.bfloat16).reshape(seq_len, head_count, triple)


def collect(ln_gain, ln_bias, w_qkv, w_attn, w_in, b_in, w_out, b_out):
    return (
        lax.all_gather(ln_gain, ("batch", "seq"), axis=0, tiled=True),
        lax.all_gather(ln_bias, ("batch", "seq"), axis=0, tiled=True),
        lax.all_gather(w_qkv, ("batch", "seq"), axis=0, tiled=True),
        lax.all_gather(w_attn, ("batch", "seq"), axis=0, tiled=True),
        lax.all_gather(w_in, ("batch", "seq"), axis=0, tiled=True),
        lax.all_gather(b_in, ("batch", "seq"), axis=0, tiled=True),
        lax.all_gather(w_out, ("batch", "seq"), axis=0, tiled=True),
        lax.all_gather(b_out, ("batch", "seq"), axis=0, tiled=True),
    )


def reduce_grads(gradients):
    return (
        lax.psum_scatter(gradients[0], ("batch", "seq"), scatter_dimension=0, tiled=True),
        lax.psum_scatter(gradients[1], ("batch", "seq"), scatter_dimension=0, tiled=True),
        lax.psum_scatter(gradients[2], ("batch", "seq"), scatter_dimension=0, tiled=True),
        lax.psum_scatter(gradients[3], ("batch", "seq"), scatter_dimension=0, tiled=True),
        lax.psum_scatter(gradients[4], ("batch", "seq"), scatter_dimension=0, tiled=True),
        lax.psum_scatter(gradients[5], ("batch", "seq"), scatter_dimension=0, tiled=True),
        lax.psum_scatter(gradients[6], ("batch", "seq"), scatter_dimension=0, tiled=True),
        lax.psum_scatter(gradients[7], ("batch", "seq"), scatter_dimension=0, tiled=True),
    )


def shards(inputs, ends, ln_gain, ln_bias, w_qkv, w_attn, w_in, b_in, w_out, b_out, cotangent):
    seq_devices = lax.axis_size("seq")
    windows, local_len, model_width = inputs.shape
    seq_len = local_len * seq_devices
    per_micro = windows // MICRO
    offset = lax.axis_index("seq") * local_len
    cosine, sine_table = rotary_tables(
        (offset + jnp.arange(local_len, dtype=jnp.int32)).astype(jnp.float32)
    )
    full_cosine, full_sine = rotary_tables(jnp.arange(seq_len, dtype=jnp.float32))
    outputs = []
    input_grads = []
    shard_sums = None
    for micro_index in range(MICRO):
        gathered = collect(ln_gain, ln_bias, w_qkv, w_attn, w_in, b_in, w_out, b_out)
        (
            gain_full,
            shift_full,
            qkv_full,
            attn_full,
            in_full,
            bias_in_full,
            out_full,
            bias_out_full,
        ) = gathered
        lower = micro_index * per_micro
        row_values = inputs[lower : lower + per_micro].astype(jnp.float32)
        grad_rows = cotangent[lower : lower + per_micro]
        window_ends = ends[lower : lower + per_micro]
        normed_f, norm_pull = jax.vjp(
            layer_norm, row_values, gain_full.astype(jnp.float32), shift_full.astype(jnp.float32)
        )
        normed = normed_f.astype(jnp.bfloat16)
        projected = jnp.einsum("pld,de->ple", normed, qkv_full, preferred_element_type=jnp.float32)
        arranged = projected.reshape(per_micro, local_len, HEADS, 3, HD)
        query_rot = rotate(arranged[:, :, :, 0], cosine, sine_table)
        key_rot = rotate(arranged[:, :, :, 1], cosine, sine_table)
        packed = jnp.stack([query_rot, key_rot, arranged[:, :, :, 2]], axis=3).astype(jnp.bfloat16)
        packed = packed.reshape(per_micro, local_len, HEADS, 3 * HD)
        head_view = lax.all_to_all(packed, "seq", split_axis=2, concat_axis=1, tiled=True)
        attended, peaks, totals = lax.map(
            lambda bundle: attend_forward(bundle[0], bundle[1]), (head_view, window_ends)
        )
        position_view = lax.all_to_all(
            attended, "seq", split_axis=1, concat_axis=2, tiled=True
        ).reshape(per_micro, local_len, model_width)
        branch_attn = jnp.einsum(
            "ple,ed->pld", position_view, attn_full, preferred_element_type=jnp.float32
        )
        hidden = jnp.einsum(
            "pld,di->pli", normed, in_full, preferred_element_type=jnp.float32
        ) + bias_in_full.astype(jnp.float32)
        activ_f, gelu_pull = jax.vjp(gelu_tanh, hidden)
        activated = activ_f.astype(jnp.bfloat16)
        branch_mlp = jnp.einsum(
            "pli,id->pld", activated, out_full, preferred_element_type=jnp.float32
        ) + bias_out_full.astype(jnp.float32)
        outputs.append((row_values + branch_attn + branch_mlp).astype(jnp.bfloat16))
        grad_b_out = jnp.sum(grad_rows.astype(jnp.float32), axis=(0, 1))
        grad_w_out = jnp.einsum(
            "pli,pld->id", activated, grad_rows, preferred_element_type=jnp.float32
        )
        d_activated = jnp.einsum(
            "pld,id->pli", grad_rows, out_full, preferred_element_type=jnp.float32
        )
        d_hidden = gelu_pull(d_activated)[0].astype(jnp.bfloat16)
        grad_b_in = jnp.sum(d_hidden.astype(jnp.float32), axis=(0, 1))
        grad_w_in = jnp.einsum("pld,pli->di", normed, d_hidden, preferred_element_type=jnp.float32)
        grad_w_attn = jnp.einsum(
            "ple,pld->ed", position_view, grad_rows, preferred_element_type=jnp.float32
        )
        d_attended = jnp.einsum(
            "pld,ed->ple", grad_rows, attn_full, preferred_element_type=jnp.float32
        ).astype(jnp.bfloat16)
        d_attended = d_attended.reshape(per_micro, local_len, HEADS, HD)
        d_head_view = lax.all_to_all(d_attended, "seq", split_axis=2, concat_axis=1, tiled=True)
        d_packed = lax.map(
            lambda bundle: attend_backward(
                bundle[0], bundle[1], bundle[2], bundle[3], bundle[4], full_cosine, full_sine
            ),
            (head_view, d_head_view, peaks, totals, window_ends),
        )
        d_projected = lax.all_to_all(
            d_packed, "seq", split_axis=1, concat_axis=2, tiled=True
        ).reshape(per_micro, local_len, 3 * model_width)
        grad_w_qkv = jnp.einsum(
            "pld,ple->de", normed, d_projected, preferred_element_type=jnp.float32
        )
        d_normed = jnp.einsum("pli,di->pld", d_hidden, in_full, preferred_element_type=jnp.float32)
        d_normed = d_normed + jnp.einsum(
            "ple,de->pld", d_projected, qkv_full, preferred_element_type=jnp.float32
        )
        d_rows, grad_gain, grad_shift = norm_pull(d_normed)
        input_grads.append(grad_rows.astype(jnp.float32) + d_rows)
        local_grads = (
            grad_gain,
            grad_shift,
            grad_w_qkv,
            grad_w_attn,
            grad_w_in,
            grad_b_in,
            grad_w_out,
            grad_b_out,
        )
        reduced = reduce_grads(local_grads)
        if shard_sums is None:
            shard_sums = reduced
        else:
            shard_sums = tuple((running + extra for running, extra in zip(shard_sums, reduced)))
    output = jnp.concatenate(outputs, axis=0)
    grad_inputs = jnp.concatenate(input_grads, axis=0)
    return (
        output,
        grad_inputs,
        shard_sums[0],
        shard_sums[1],
        shard_sums[2],
        shard_sums[3],
        shard_sums[4],
        shard_sums[5],
        shard_sums[6],
        shard_sums[7],
    )


SB = 4
SEND_SEMS = 93
NEG = -1e30
BF, F32 = jnp.bfloat16, jnp.float32
MESH = pl.DeviceIdType.MESH


def dot(a, b, ca, cb):
    return lax.dot_general(a, b, (((ca,), (cb,)), ((), ())), preferred_element_type=F32)


def rows(start, size):
    return pl.ds(pl.multiple_of(start, size), size)


def lanes(start, size=128):
    return pl.ds(pl.multiple_of(start, size), size)


def halves(low_source, high_source):
    def piece(source, upper):
        array, first = source
        tile = array[:, first // 128 * 128 : first // 128 * 128 + 128]
        return pltpu.roll(tile, 64, 1) if (first % 128 == 64) != upper else tile

    lane = lax.broadcasted_iota(jnp.int32, (1, 128), 1)
    return jnp.where(lane < 64, piece(low_source, False), piece(high_source, True))


def head_of(owner, j):
    return 4 * j + 2 * (owner % 2) + owner // 2


class Link:
    slow = ("wox", "wol", "gf")

    def __init__(self, send_sems, recv_sems):
        self.send_sems, self.recv_sems = send_sems, recv_sems
        self.receives, self.sends, self.slow_sends = {}, {}, {}

    @staticmethod
    def index(table, name, at, count):
        if name not in table:
            table[name] = (sum(size for _, size in table.values()), count)
        return table[name][0] + at

    def reuse(self):
        self.sends = {}

    def copy(self, name, at, count, src, dst, device):
        if name in self.slow:
            send = SEND_SEMS + self.index(self.slow_sends, name, at, count)
        else:
            send = self.index(self.sends, name, at, count)
        receive = self.index(self.receives, name, at, count)
        return pltpu.make_async_remote_copy(
            src_ref=src,
            dst_ref=dst,
            send_sem=self.send_sems.at[send],
            recv_sem=self.recv_sems.at[receive],
            device_id=device,
            device_id_type=MESH,
        )


def gelu_pair(v):
    square = v * v
    half = 0.5 + 0.5 * jnp.tanh(v * (gelu_factor + (gelu_factor * 0.044715) * square))
    value = v * half
    return value, half + (value - value * half) * (
        2.0 * gelu_factor + (6.0 * gelu_factor * 0.044715) * square
    )


def fused_layer(
    ends, gain, bias, bias_out, bias_in, wq, wa, wi, wo, turns, x_in, g_in,
    out_hbm, grad_in_hbm, grad_q_hbm, grad_a_hbm, grad_i_hbm, grad_o_hbm, grad_small_hbm,
    X, N, G, A, H, Wi, Wo, Wq, WaAll, Wa, PWI, PWQ, PRS, PRM, PR, QKV, att, dO,
    GO, XO, ZO, CO, GI, XI, ZN, ZF, ZD, CI, GQ, XQ, ZQ, CQ, GA, XA, ZA, CA, GT, XT, ZT,
    YR, SWI, RWI, SWQ, RWQ, SWT, RWT, TAIL,
    khat, ktT, vtT, doT, oT, dqT, dkA, dvA,
    grad_in, grad_q, grad_a, grad_small,
    send_sems, recv_sems, local_sems, out_sems,
):
    b = lax.axis_index("batch")
    s = lax.axis_index("seq")
    z, xx = b // 2, b % 2
    y, c = s // 2, s % 2
    oc, ox, oy = 1 - c, 1 - xx, 1 - y
    SL = 256
    S = 1024
    core = (b, 2 * y + oc)
    ypart = (b, 2 * oy + c)
    diag = (b, 2 * oy + oc)
    xpart = (2 * z + ox, s)

    def zdev(k):
        return (2 * ((z + k) % 4) + xx, s)

    def zfrom(k):
        return (z + 4 - k) % 4

    link = Link(send_sems, recv_sems)
    pending = []

    def start(make):
        make().start()
        pending.append(make)

    barrier = pltpu.get_barrier_semaphore()
    others = [xpart] + [zdev(k) for k in (1, 2, 3)]
    others += [(2 * ((z + k) % 4) + ox, s) for k in (1, 2, 3)]
    partners = [core, ypart, diag] + others
    for device in partners:
        pl.semaphore_signal(barrier, inc=1, device_id=device, device_id_type=MESH)

    own = rows(SL * s, SL)
    locals_ = []
    for w in range(2):
        locals_.append(pltpu.make_async_copy(x_in.at[w], X.at[w, own], local_sems.at[3 * w]))
        locals_.append(pltpu.make_async_copy(g_in.at[w], G.at[w, own], local_sems.at[3 * w + 1]))
    for cp in locals_:
        cp.start()

    for r in range(SB):
        for blk in range(8):
            PWI[r, :, 128 * blk : 128 * blk + 128] = wi[:, 512 * blk + 128 * r : 512 * blk + 128 * r + 128]
    TAIL[...] = jnp.zeros_like(TAIL)
    for i, values in enumerate((gain, bias, bias_out, bias_in)):
        TAIL[i : i + 1, 0 : values.shape[1]] = values[...].astype(F32)
    tile = TAIL[:, 0:128]
    row = lax.broadcasted_iota(jnp.int32, (16, 128), 0)
    tile = jnp.where(row < 3, pltpu.roll(tile, 32 * s, 1), tile)
    PRS[s] = tile.astype(BF)
    Wi[rows(128 * b + 32 * s, 32), :] = PWI[s]
    Wo[rows(128 * b, 128), :] = wo[...]
    WaAll[z, xx] = wa[...]

    wq_f = wq[...].astype(F32)
    for r in range(SB):
        for kind in range(3):
            for p in range(2):
                lo = 192 * head_of(r, 2 * p) + 64 * kind
                hi = 192 * head_of(r, 2 * p + 1) + 64 * kind
                at = 384 * p + 128 * kind
                PWQ[r, :, at : at + 128] = halves((wq_f, lo), (wq_f, hi)).astype(BF)
    Wq[rows(128 * b + 32 * s, 32), :] = PWQ[s]

    pl.semaphore_wait(barrier, len(partners))

    def seq_sends(name, src_of, dst):
        for i, (device, owner) in enumerate(
            ((core, 2 * y + oc), (ypart, 2 * oy + c), (diag, 2 * oy + oc))
        ):
            link.copy(name, i, 3, src_of(owner), dst(), device).start()

    def seq_left(name, src_of, dst):
        for i, (device, owner) in enumerate(
            ((core, 2 * y + oc), (ypart, 2 * oy + c), (diag, 2 * oy + oc))
        ):
            link.copy(name, i, 3, src_of(owner), dst(), device).wait_send()

    def seq_waits(name, src, dst_of):
        for i, owner in enumerate((2 * y + oc, 2 * oy + c, 2 * oy + oc)):
            link.copy(name, i, 3, src, dst_of(owner), core).wait_recv()

    def prm_block(owner):
        return PRS.at[owner]

    def wi_block(owner, u):
        return Wi.at[rows(128 * b + 32 * owner, 32), 256 * u : 256 * u + 256]

    def wq_block(owner):
        return Wq.at[rows(128 * b + 32 * owner, 32)]

    gathers = {
        "wi": (4, lambda bb, u: Wi.at[rows(128 * bb, 128), lanes(256 * u, 256)]),
        "wo": (2, lambda bb, u: Wo.at[rows(128 * bb + 64 * u, 64)]),
        "wq": (2, lambda bb, u: Wq.at[rows(128 * bb, 128), 384 * u : 384 * u + 384]),
        "wa": (1, lambda bb, u: WaAll.at[bb // 2, bb % 2]),
    }
    pair = z + 1 - 2 * (z % 2)

    def gather_copy(name, way, at, count, zz, side, u, device):
        held = gathers[name][1](2 * zz + side, u)
        return link.copy(name + way, count * u + at, count * gathers[name][0], held, held, device)

    by_line = ("wi", "wo")

    def up_copy(name, zz, u):
        return gather_copy(name, "l", zz, 5, zz, xx, u, (2 * (z + 1) + xx, s))

    def down_copy(name, zz, u):
        return gather_copy(name, "l", zz + 1, 5, zz, xx, u, (2 * (z - 1) + xx, s))

    def z_copy(name, zz, k, u):
        return gather_copy(name, "z", k - 1, 3, zz, xx, u, zdev(k))

    def x_copy(name, zz, side, u):
        return gather_copy(name, "x", zz, 4, zz, side, u, xpart)

    def gather_z(name, u):
        if name in by_line:

            @pl.when(z < 3)
            def _():
                up_copy(name, z, u).start()

            @pl.when(z > 0)
            def _():
                down_copy(name, z, u).start()

            return
        for far in (1, 2, 3):

            @pl.when(z + far <= 3)
            def _():
                z_copy(name, z, far, u).start()

            @pl.when(z >= far)
            def _():
                z_copy(name, z, 4 - far, u).start()

    def gather_x(name, u):
        x_copy(name, z, xx, u).start()

    def gather_pass(name, far, u):
        @pl.when(z >= far)
        def _():
            if name in by_line:
                up_copy(name, z - far, u).wait_recv()

                @pl.when(z < 3)
                def _():
                    up_copy(name, z - far, u).start()

            else:
                z_copy(name, z - far, far, u).wait_recv()
            x_copy(name, z - far, xx, u).start()

        @pl.when(z + far <= 3)
        def _():
            if name in by_line:
                down_copy(name, z + far, u).wait_recv()

                @pl.when(z > 0)
                def _():
                    down_copy(name, z + far, u).start()

            else:
                z_copy(name, z + far, 4 - far, u).wait_recv()
            x_copy(name, z + far, xx, u).start()

    def gather_block(name, zz, u):
        x_copy(name, zz, ox, u).wait_recv()

    def gather_end(name, u):
        for zz in range(4):
            gather_block(name, zz, u)

    def gather_left(name, u):
        if name not in by_line:
            for k in (1, 2, 3):
                z_copy(name, z, k, u).wait_send()
        for zz in range(4):
            if name in by_line:

                @pl.when((zz <= z) & (z < 3))
                def _():
                    up_copy(name, zz, u).wait_send()

                @pl.when((zz >= z) & (z > 0))
                def _():
                    down_copy(name, zz, u).wait_send()

            x_copy(name, zz, xx, u).wait_send()

    def rows_start(name, src, dst):
        for w in range(2):
            start(lambda w=w: link.copy(name + "c", w, 2, src.at[w], dst.at[w, own], core))
            start(lambda w=w: link.copy(name + "y", w, 2, src.at[w], dst.at[w, own], ypart))

    def rows_pass(name, dst, w):
        block = dst.at[w, rows(SL * (2 * oy + c), SL)]
        link.copy(name + "y", w, 2, block, block, core).wait_recv()
        link.copy(name + "f", w, 2, block, block, core).start()

    def rows_left(name, dst, w):
        block = dst.at[w, rows(SL * (2 * oy + c), SL)]
        link.copy(name + "f", w, 2, block, block, core).wait_send()

    def rows_end_core(name, dst, w):
        block = dst.at[w, rows(SL * (2 * y + oc), SL)]
        link.copy(name + "c", w, 2, block, block, core).wait_recv()

    def rows_end_far(name, dst, w):
        block = dst.at[w, rows(SL * (2 * oy + oc), SL)]
        link.copy(name + "f", w, 2, block, block, core).wait_recv()

    seq_sends("prms", lambda owner: prm_block(s), lambda: prm_block(s))
    for u in range(4):
        seq_sends(
            "wis%d" % u, lambda owner: PWI.at[owner, :, 256 * u : 256 * u + 256], lambda: wi_block(s, u)
        )
    gather_z("wa", 0)
    gather_x("wa", 0)
    gather_x("wo", 0)
    seq_sends("wqs", lambda owner: PWQ.at[owner], lambda: wq_block(s))
    rows_start("x", x_in, X)
    seq_waits("prms", prm_block(s), prm_block)
    total = PRS[0].astype(F32) + PRS[1].astype(F32) + PRS[2].astype(F32) + PRS[3].astype(F32)
    PRM[b] = jnp.where(row < 3, total, tile).astype(BF)
    for i, device in enumerate(others):
        start(lambda i=i, device=device: link.copy("prm", i, 7, PRM.at[b], PRM.at[b], device))
    for u in range(4):
        seq_waits("wis%d" % u, wi_block(s, u), lambda owner: wi_block(owner, u))
        gather_z("wi", u)
        gather_x("wi", u)
    rows_start("g", g_in, G)
    gather_pass("wi", 1, 0)
    gather_pass("wi", 1, 1)
    for far in (1, 2, 3):
        gather_pass("wa", far, 0)

    for i in range(7):
        k = (0, 1, 2, 3, 1, 2, 3)[i]
        bb = 2 * zfrom(k) + (ox if i in (0, 4, 5, 6) else xx)
        link.copy("prm", i, 7, PRM.at[bb], PRM.at[bb], core).wait_recv()
    for bb in range(8):
        PR[:, 128 * bb : 128 * bb + 128] = PRM[bb].astype(F32)[0:8]

    for cp in locals_:
        cp.wait()

    def norm_rows(w, owner):
        r = rows(SL * owner, SL)
        v = X[w, r, :].astype(F32)
        v = v - jnp.mean(v, axis=-1, keepdims=True)
        var = jnp.mean(v * v, axis=-1, keepdims=True)
        N[w, r, :] = (v * lax.rsqrt(var + norm_eps) * PR[0:1, :] + PR[1:2, :]).astype(BF)

    def norm_near(w, carry):
        norm_rows(w, s)
        norm_rows(w, 2 * y + oc)
        return carry

    def norm_far(w):
        rows_end_far("x", X, w)
        norm_rows(w, 2 * oy + c)
        norm_rows(w, 2 * oy + oc)

    for w in range(2):
        rows_end_core("x", X, w)
    lax.fori_loop(0, 2, norm_near, 0)
    gather_pass("wi", 2, 0)
    gather_pass("wi", 1, 2)
    gather_pass("wi", 1, 3)
    seq_waits("wqs", wq_block(s), wq_block)
    gather_z("wq", 0)
    gather_x("wq", 0)
    gather_pass("wi", 2, 1)
    gather_pass("wi", 3, 0)
    gather_pass("wi", 2, 2)
    gather_pass("wi", 3, 1)
    rows_pass("x", X, 0)
    gather_pass("wi", 2, 3)
    gather_z("wq", 1)
    gather_x("wq", 1)

    def hidden_step(i, carry):
        early = i < 12
        u = jnp.where(early, i // 3, i - 12)
        at = jnp.where(early, i % 3, 3)
        w = at % 2
        t = jnp.where(at < 2, y, oy)

        @pl.when(i == 0)
        def _():
            gather_end("wi", 0)

        @pl.when(i == 2)
        def _():
            norm_far(0)

        @pl.when(i == 3)
        def _():
            gather_pass("wi", 3, 2)
            gather_end("wi", 1)

        @pl.when(i == 5)
        def _():
            gather_pass("wi", 3, 3)
            gather_z("wo", 0)
            gather_z("wo", 1)
            gather_pass("wq", 1, 0)

        @pl.when(i == 6)
        def _():
            gather_end("wi", 2)

        @pl.when(i == 7)
        def _():
            rows_pass("x", X, 1)

        @pl.when(i == 9)
        def _():
            gather_pass("wq", 2, 0)
            gather_end("wi", 3)

        @pl.when(i == 11)
        def _():
            gather_pass("wq", 3, 0)

        @pl.when(i == 12)
        def _():
            norm_far(1)

        @pl.when(i == 14)
        def _():
            gather_pass("wq", 1, 1)
            gather_x("wo", 1)

        r, l = rows(512 * t, 512), lanes(256 * u, 256)
        v = dot(N[w, r, :], Wi[:, l], 1, 0) + PR[3:4, l]
        value, slope = gelu_pair(v)
        A[w, r, l] = value.astype(BF)
        H[w, r, l] = slope.astype(BF)
        return carry

    lax.fori_loop(0, 16, hidden_step, 0)
    for w in range(2):
        rows_left("x", X, w)
    gather_end("wa", 0)
    start(lambda: link.copy("wac", 0, 1, WaAll.at[:, oc], Wa.at[:, c], core))
    Wa[:, c] = WaAll[:, c]
    for far in (2, 3):
        gather_pass("wq", far, 1)
    for u in range(2):
        gather_pass("wo", 1, u)

    def add_into(dst, other):
        dst[...] = (dst[...].astype(F32) + other[...].astype(F32)).astype(BF)

    inner = (z == 1) | (z == 2)

    def far_chip(tt):
        return 2 * (1 - z // 2) + tt

    def zchip(zz):
        return (2 * zz + xx, s)

    def o_near(q):
        return link.copy("op", 0, 1, GO.at[q, xx], ZO.at[0], zchip(pair))

    def o_comb(q):
        return link.copy("oc", q % 2, 2, GO.at[q, xx], CO.at[q % 2], zchip(pair))

    def o_far(q):
        return link.copy("of", q % 2, 2, GO.at[q, xx], ZO.at[1], zchip(q))

    def of_pair(p):
        return lambda: ("q", GQ.at[p], XQ.at[p], ZQ.at[p], CQ.at[p], p, 2)

    def of_attn():
        return "a", GA, XA, ZA, CA, 0, 1

    def z_near(get):
        name, group, _, landed, _, at, count = get()
        return link.copy(name + "p", at, count, group.at[xx, pair], landed.at[0], zchip(pair))

    def z_comb(get, tt):
        name, group, _, _, comb, at, count = get()
        block = group.at[xx, far_chip(tt)]
        return link.copy(name + "c", 2 * at + tt, 2 * count, block, comb.at[tt], zchip(pair))

    def z_far(get, tt, side):
        name, group, _, landed, _, at, count = get()
        block = group.at[xx, far_chip(tt)]
        return link.copy(
            name + "f", 2 * at + side, 2 * count, block, landed.at[1], zchip(far_chip(tt))
        )

    def z_first(get):
        _, group, received, _, _, _, _ = get()
        add_into(group.at[xx, pair], received.at[pair])
        z_near(get).start()
        for tt in range(2):
            add_into(group.at[xx, far_chip(tt)], received.at[far_chip(tt)])

            @pl.when(~inner)
            def _():
                z_comb(get, tt).start()

    def z_second(get):
        @pl.when(inner)
        def _():
            _, group, _, _, comb, _, _ = get()
            for tt in range(2):
                z_comb(get, tt).wait_recv()
                add_into(group.at[xx, far_chip(tt)], comb.at[tt])
                z_far(get, tt, tt).start()

    def z_total(get):
        _, group, received, landed, _, _, _ = get()
        z_near(get).wait_recv()
        z_far(get, 0, z % 2).wait_recv()
        total = group[xx, z].astype(F32) + received[z].astype(F32)
        return total + landed[0].astype(F32) + landed[1].astype(F32)

    def z_gone(get):
        z_near(get).wait_send()
        for tt in range(2):

            @pl.when(inner)
            def _():
                z_far(get, tt, tt).wait_send()

            @pl.when(~inner)
            def _():
                z_comb(get, tt).wait_send()

    def first_o(q):
        o_x(q).wait_recv()

        @pl.when(z != q)
        def _():
            add_into(GO.at[q, xx], XO.at[q])

            @pl.when(q == pair)
            def _():
                o_near(q).start()

            @pl.when((q != pair) & ~inner)
            def _():
                o_comb(q).start()

    def half_chip(tt):
        return 2 * (z // 2) + tt

    def i_near(q):
        return link.copy("ip", q, 4, GI.at[q, xx, pair], ZN.at[q], zchip(pair))

    def i_comb(q, tt):
        block = GI.at[q, xx, far_chip(tt)]
        return link.copy("ic", 2 * (q % 2) + tt, 4, block, CI.at[q % 2, tt], zchip(pair))

    def i_far(q, tt, side):
        block = GI.at[q, xx, far_chip(tt)]
        return link.copy("if", 2 * (q % 2) + side, 4, block, ZF.at[q % 2], zchip(far_chip(tt)))

    def i_straight(q, tt, sender, side):
        block = GI.at[q, xx, far_chip(tt)]
        return link.copy(
            "id", 4 * (q % 2) + 2 * sender + side, 8, block, ZD.at[q % 2, sender], zchip(far_chip(tt))
        )

    def first_i(q, far):
        i_x(q).wait_recv()
        add_into(GI.at[q, xx, pair], XI.at[q, pair])
        i_near(q).start()
        for tt in range(2):
            add_into(GI.at[q, xx, far_chip(tt)], XI.at[q, far_chip(tt)])
            if far:

                @pl.when(~inner)
                def _():
                    i_comb(q, tt).start()

            else:
                i_straight(q, tt, z % 2, tt).start()

    def second_i(q):
        @pl.when(inner)
        def _():
            for tt in range(2):
                i_comb(q, tt).wait_recv()
                add_into(GI.at[q, xx, far_chip(tt)], CI.at[q % 2, tt])
                i_far(q, tt, tt).start()

    def total_i(q, far):
        i_near(q).wait_recv()
        total = GI[q, xx, z].astype(F32) + XI[q, z].astype(F32) + ZN[q].astype(F32)
        if far:
            for sender in range(2):
                i_straight(q, 0, sender, z % 2).wait_recv()
                total = total + ZD[q % 2, sender].astype(F32)
            return total
        i_far(q, 0, z % 2).wait_recv()
        return total + ZF[q % 2].astype(F32)

    def second_z(q):
        @pl.when(inner)
        def _():
            o_comb(q).wait_recv()
            add_into(GO.at[q, xx], CO.at[q % 2])
            o_far(q).start()

    def z_left():
        o_near(pair).wait_send()
        for tt in range(2):

            @pl.when(inner)
            def _():
                o_far(far_chip(tt)).wait_send()

            @pl.when(~inner)
            def _():
                o_comb(far_chip(tt)).wait_send()

        for q in range(4):
            i_near(q).wait_send()
        for a in range(2):
            for tt in range(2):
                i_straight(half_chip(a), tt, z % 2, tt).wait_send()

                @pl.when(inner)
                def _():
                    i_far(far_chip(a), tt, tt).wait_send()

                @pl.when(~inner)
                def _():
                    i_comb(far_chip(a), tt).wait_send()

        for p in range(2):
            z_gone(of_pair(p))
        z_gone(of_attn)

    def chunk(j):
        return jnp.where(j == 3, z, jnp.where(j == 2, pair, far_chip(0) + j))

    def o_x(q):
        return link.copy("ox", q, 4, GO.at[q, ox], XO.at[q], xpart)

    def i_x(q):
        return link.copy("ix", q, 4, GI.at[q, ox], XI.at[q], xpart)

    even = lax.broadcasted_iota(jnp.int32, (1, 128), 1) % 2 == 0

    def turn_rows(r):
        table = turns[r, :]
        other = pltpu.roll(table, 64, 1)
        low = lax.broadcasted_iota(jnp.int32, (1, 128), 1) < 64
        return jnp.where(low, table, other), jnp.where(low, other, table)

    def turn(v, cos_rows, sin_rows):
        swapped = jnp.where(even, pltpu.roll(v, 127, 1), pltpu.roll(v, 1, 1))
        return v * cos_rows + swapped * sin_rows

    def qkv_step(p):
        gather_end("wq", p)
        l = slice(384 * p, 384 * p + 384)

        def step(i, carry):
            w, r = i // 4, rows(256 * (i % 4), 256)
            v = dot(N[w, r, :], Wq[:, l], 1, 0)
            cos_rows, sin_rows = turn_rows(r)
            for kind in range(3):
                tile_v = v[:, 128 * kind : 128 * kind + 128]
                if kind < 2:
                    tile_v = turn(tile_v, cos_rows, sin_rows)
                if kind == 0:
                    tile_v = tile_v * 0.125
                QKV[w, r, 384 * p + 128 * kind : 384 * p + 128 * kind + 128] = tile_v.astype(BF)
            return carry

        lax.fori_loop(0, 8, step, 0)

    qkv_step(0)
    for w in range(2):
        rows_end_core("g", G, w)
    rows_pass("g", G, 0)
    for u in range(4):
        seq_left(
            "wis%d" % u, lambda owner: PWI.at[owner, :, 256 * u : 256 * u + 256], lambda: wi_block(s, u)
        )
    link.copy("wac", 0, 1, WaAll.at[:, oc], Wa.at[:, oc], core).wait_recv()
    TAIL[...] = jnp.zeros_like(TAIL)

    def do_step(w):
        def step(i, total):
            r = rows(512 * i, 512)
            g = G[w, r, :]
            dO[w, r, :] = dot(g, Wa[...].reshape(256, 1024), 1, 1).astype(BF)
            return total + jnp.sum(g.astype(F32), axis=0, keepdims=True)

        TAIL[2:3, :] += lax.fori_loop(0, 2, step, jnp.zeros((1, 1024), F32))

    rows_end_far("g", G, 0)
    do_step(0)
    gather_pass("wo", 2, 0)

    def units_back(j):
        q = chunk(j)
        l = lanes(256 * q, 256)

        def step(w, total):
            d = dot(G[w], Wo[rows(256 * q, 256), :], 1, 1) * H[w, :, l].astype(F32)
            d = d.astype(BF)
            H[w, :, l] = d
            return total + jnp.sum(d.astype(F32), axis=0, keepdims=True)

        TAIL[3:4, l] = lax.fori_loop(0, 2, step, jnp.zeros((1, 256), F32))

    def units_out(j):
        q = chunk(j)
        l = lanes(256 * q, 256)
        go = dot(A[0, :, l], G[0], 0, 0) + dot(A[1, :, l], G[1], 0, 0)
        GO[q, 0] = go[:128].astype(BF)
        GO[q, 1] = go[128:].astype(BF)

    def units_in(j):
        q = chunk(j)
        l = lanes(256 * q, 256)
        gi = dot(H[0, :, l], N[0], 0, 0) + dot(H[1, :, l], N[1], 0, 0)
        for bb in range(8):
            GI[q, bb % 2, bb // 2] = gi[:, 128 * bb : 128 * bb + 128].astype(BF)

    lane = lax.broadcasted_iota(jnp.int32, (1, 128), 1)
    place = lax.broadcasted_iota(jnp.int32, (S, 1), 0)
    BQ = 256
    key_i = lax.broadcasted_iota(jnp.int32, (BQ, BQ), 0)
    query_i = lax.broadcasted_iota(jnp.int32, (BQ, BQ), 1)
    inside = [(lane // 64) == hh for hh in range(2)]
    feature = [lane == (64 - 64 * hh) for hh in range(2)]

    def attend(w, p):
        ending = ends[w]

        def part(kind):
            return lanes(384 * p + 128 * kind)

        pl_ = lanes(128 * p)
        keys = QKV[w, :, part(1)]
        ktT[...] = keys.T
        vtT[...] = QKV[w, :, part(2)].T
        doT[...] = dO[w, :, pl_].T
        dkA[...] = jnp.zeros_like(dkA)
        dvA[...] = jnp.zeros_like(dvA)
        keys_f = keys.astype(F32)
        before = jnp.where(place < ending, NEG, 0.0)
        for hh in range(2):
            khat[hh] = jnp.where(inside[hh], keys_f, jnp.where(feature[hh], before, 0.0)).astype(BF)

        def begin(qb, hh):
            qr, nk = slice(qb * BQ, (qb + 1) * BQ), (qb + 1) * BQ
            q = QKV[w, qr, part(0)].astype(F32)
            after = jnp.where(place[qr] >= ending, 1.0, 0.0)
            q_in = jnp.where(inside[hh], q, 0.0).astype(BF)
            q_hat = jnp.where(inside[hh], q, jnp.where(feature[hh], after, 0.0)).astype(BF)
            d_in = jnp.where(inside[hh], dO[w, qr, pl_].astype(F32), 0.0).astype(BF)
            return dot(khat[hh, 0:nk, :], q_hat, 1, 1), dot(QKV[w, 0:nk, part(2)], d_in, 1, 1), q_in, d_in

        units = [(qb, hh) for qb in range(S // BQ) for hh in range(2)]
        upcoming, late = begin(*units[0]), None
        for i, (qb, hh) in enumerate(units):
            sc, dp, q_in, d_in = upcoming
            qr, nk = slice(qb * BQ, (qb + 1) * BQ), (qb + 1) * BQ
            hr = slice(64 * hh, 64 * hh + 64)
            if i + 1 < len(units):
                upcoming = begin(*units[i + 1])
            last = jnp.where(key_i <= query_i, sc[nk - BQ :], NEG)
            sc = last if qb == 0 else jnp.concatenate([sc[: nk - BQ], last], axis=0)
            e = jnp.exp(sc - jnp.max(sc, axis=0, keepdims=True))
            pn = e * (1.0 / jnp.sum(e, axis=0, keepdims=True))
            pb = pn.astype(BF)
            o = dot(vtT[hr, 0:nk], pb, 1, 0)
            if late is not None:
                late()
            oT[hr, qr] = o
            dd = jnp.sum(o * doT[hr, qr].astype(F32), axis=0, keepdims=True)
            ds = (pn * (dp - dd)).astype(BF)

            def late(hr=hr, qr=qr, nk=nk, ds=ds, pb=pb, q_in=q_in, d_in=d_in):
                dqT[hr, qr] = dot(ktT[hr, 0:nk], ds, 1, 0)
                dkA[0:nk, :] += dot(ds, q_in, 1, 0)
                dvA[0:nk, :] += dot(pb, d_in, 1, 0)

        late()
        cos_rows, sin_rows = turn_rows(slice(None))
        sin_rows = -sin_rows
        att[w, :, pl_] = oT[...].T.astype(BF)
        QKV[w, :, part(0)] = turn(dqT[...].T * 0.125, cos_rows, sin_rows).astype(BF)
        QKV[w, :, part(1)] = turn(dkA[...], cos_rows, sin_rows).astype(BF)
        QKV[w, :, part(2)] = dvA[...].astype(BF)

    shares = (A, H)

    def share_c(w, t, yy):
        src = shares[t].at[w, rows(SL * (2 * yy + oc), SL)]
        dst = X.at[w, rows(SL * (2 * t + yy), SL)]
        link.copy("sc", 4 * w + 2 * t + yy, 8, src, dst, core).start()

    def share_got(w, t, yy):
        slot = X.at[w, rows(SL * (2 * t + yy), SL)]
        link.copy("sc", 4 * w + 2 * t + yy, 8, slot, slot, core).wait_recv()
        return slot

    def share_y(w, t):
        src = shares[t].at[w, rows(SL * (2 * oy + c), SL)]
        add_into(src, share_got(w, t, oy))
        link.copy("sy", 2 * w + t, 4, src, YR.at[w, t], ypart).start()

    def share_out(w, r):
        value = dot(A[w, r, :], Wo[...], 1, 0) + dot(att[w, r, :], Wa[...].reshape(256, 1024), 1, 0)
        A[w, r, :] = value.astype(BF)

    def share_normed(w, r):
        d = dot(H[w, r, :], Wi[...], 1, 1) + dot(QKV[w, r, :], Wq[...], 1, 1)
        H[w, r, :] = d.astype(BF)
        n = (N[w, r, :].astype(F32) - PR[1:2, :]) / PR[0:1, :]
        TAIL[0:1, :] += jnp.sum(d, axis=0, keepdims=True)
        TAIL[1:2, :] += jnp.sum(d * n, axis=0, keepdims=True)

    def share_step(w, t, between=None):
        def step(i, carry):
            yy = jnp.where(i < 2, oy, y)
            cc = jnp.where(i % 2 == 0, oc, c)
            (share_out, share_normed)[t](w, rows(SL * (2 * yy + cc), SL))

            @pl.when(i == 0)
            def _():
                share_c(w, t, oy)

            if between is not None:
                pl.when(i == 1)(between)

            @pl.when(i == 2)
            def _():
                share_y(w, t)
                share_c(w, t, y)

            return carry

        lax.fori_loop(0, 4, step, 0)

    def gq_step(p):
        l = slice(384 * p, 384 * p + 384)
        gq = dot(QKV[0, :, l], N[0], 0, 0) + dot(QKV[1, :, l], N[1], 0, 0)
        for bb in range(8):
            GQ[p, bb % 2, bb // 2] = gq[:, 128 * bb : 128 * bb + 128].astype(BF)
        link.copy("qx", p, 2, GQ.at[p, ox], XQ.at[p], xpart).start()

    def ga_c(p):
        two = slice(2 * p, 2 * p + 2)
        return link.copy("core_a", p, 2, PWI.at[two], GA.at[c, two], core)

    def ga_x(p):
        two = slice(2 * p, 2 * p + 2)
        return link.copy("x_a", p, 2, GA.at[ox, two], XA.at[two], xpart)

    def ga_step(p):
        l = slice(128 * p, 128 * p + 128)
        ga = dot(att[0, :, l], G[0], 0, 0) + dot(att[1, :, l], G[1], 0, 0)
        for j in range(2):
            for cc in range(2):
                piece = ga[64 * j + 32 * cc : 64 * j + 32 * cc + 32].astype(BF)

                @pl.when(cc == c)
                def _():
                    GA[c, 2 * p + j] = piece

                @pl.when(cc != c)
                def _():
                    PWI[2 * p + j] = piece

        ga_c(p).start()

    def ga_send(p):
        ga_c(p).wait_recv()
        ga_x(p).start()

    def first_q(p):
        link.copy("qx", p, 2, GQ.at[p, ox], XQ.at[p], xpart).wait_recv()
        z_first(of_pair(p))

    def first_a():
        for p in range(2):
            ga_x(p).wait_recv()
        z_first(of_attn)

    def sends_left():
        for make in pending:
            make().wait_send()
        pending.clear()
        seq_left("prms", lambda owner: prm_block(s), lambda: prm_block(s))
        seq_left("wqs", lambda owner: PWQ.at[owner], lambda: wq_block(s))
        for name in ("wi", "wq", "wa"):
            for u in range(gathers[name][0]):
                gather_left(name, u)
        link.reuse()

    def attend_step(i, carry):
        w, p = i // 2, i % 2
        attend(w, p)

        @pl.when(i == 0)
        def _():
            gather_pass("wo", 2, 1)
            gather_pass("wo", 3, 0)
            rows_pass("g", G, 1)
            qkv_step(1)
            sends_left()
            gather_pass("wo", 3, 1)
            rows_end_far("g", G, 1)
            for j in range(2):
                units_out(j)
                o_x(chunk(j)).start()

        @pl.when(i == 1)
        def _():
            do_step(1)

        @pl.when(i == 2)
        def _():
            gq_step(0)
            ga_step(0)
            for j in range(2, 4):
                units_out(j)
            for u in range(2):
                for zz in range(4):
                    gather_block("wo", zz, u)
            share_step(0, 0)
            first_o(chunk(0))
            first_o(chunk(1))
            ga_send(0)

        return carry

    lax.fori_loop(0, 4, attend_step, 0)
    gq_step(1)
    ga_step(1)

    def in_step(j, carry):
        turn_j = (j + 2) % 4
        units_back(turn_j)
        units_in(turn_j)
        i_x(chunk(turn_j)).start()

        @pl.when(j == 0)
        def _():
            z_second(of_pair(0))

        @pl.when(j == 1)
        def _():
            first_q(1)

        @pl.when(j == 2)
        def _():
            first_a()

        return carry

    written = []

    def write(src, dst):
        cp = pltpu.make_async_copy(src, dst, out_sems.at[len(written)])
        cp.start()
        written.append(cp)
        return cp

    def to_seq(name, held, landed):
        landed[s] = held[s]
        seq_sends(name, lambda owner: held.at[owner], lambda: landed.at[s])

    def from_seq(name, landed):
        for i, owner in enumerate((2 * y + oc, 2 * oy + c, 2 * oy + oc)):
            link.copy(name, i, 3, landed.at[owner], landed.at[owner], core).wait_recv()

    second_z(chunk(0))
    first_q(0)
    ga_send(1)
    second_z(chunk(1))
    share_step(1, 0)
    lax.fori_loop(0, 4, in_step, 0)
    for j in range(2, 4):
        o_x(chunk(j)).start()

    def between_first():
        first_i(chunk(2), False)
        z_second(of_pair(1))
        z_second(of_attn)

    def between_second():
        first_i(chunk(3), False)

    share_step(0, 1, between_first)
    share_step(1, 1, between_second)
    again = [
        pltpu.make_async_copy(x_in.at[w], N.at[w, 0:SL], local_sems.at[3 * w + 2]) for w in range(2)
    ]
    for cp in again:
        cp.start()
    tail = TAIL[...]
    for bb in range(8):
        GT[bb % 2, bb // 2] = tail[:, 128 * bb : 128 * bb + 128].astype(BF)
    for k in (1, 2, 3):
        start(lambda k=k: link.copy("tz", k - 1, 3, GT.at[:, (z + k) % 4], ZT.at[k - 1], zdev(k)))

    def tail_x():
        for k in (1, 2, 3):
            link.copy("tz", k - 1, 3, ZT.at[k - 1], ZT.at[k - 1], core).wait_recv()
        add_into(ZT.at[0], GT.at[:, z])
        add_into(ZT.at[1], ZT.at[2])
        add_into(ZT.at[0], ZT.at[1])
        start(lambda: link.copy("tx", 0, 1, ZT.at[0, ox], XT, xpart))

    def final_o():
        o_near(z).wait_recv()
        link.copy("of", z % 2, 2, ZO.at[1], ZO.at[1], core).wait_recv()
        dqT[...] = (
            GO[z, xx].astype(F32) + XO[z].astype(F32) + ZO[0].astype(F32) + ZO[1].astype(F32)
        )

    def final_i():
        for tt in range(2):
            for q, far in ((half_chip(tt), False), (far_chip(tt), True)):
                turned = total_i(q, far).T.astype(BF)
                for owner in range(4):
                    SWI[owner, :, lanes(256 * q, 256)] = turned[32 * owner : 32 * owner + 32]

    def final_rows(w):
        again[w].wait()
        v = N[w, 0:SL, :].astype(F32)
        mine = rows(SL * s, SL)
        for t in (1, 0):
            share_got(w, t, y)
            link.copy("sy", 2 * w + t, 4, YR.at[w, t], YR.at[w, t], core).wait_recv()
        value = (
            A[w, mine, :].astype(F32)
            + X[w, rows(SL * y, SL), :].astype(F32)
            + YR[w, 0].astype(F32)
        )
        A[w, mine, :] = (v + value + PR[2:3, :]).astype(BF)
        d = (
            H[w, mine, :].astype(F32)
            + X[w, rows(SL * (2 + y), SL), :].astype(F32)
            + YR[w, 1].astype(F32)
        )
        v = v - jnp.mean(v, axis=-1, keepdims=True)
        scale = lax.rsqrt(jnp.mean(v * v, axis=-1, keepdims=True) + norm_eps)
        v = v * scale
        d = d * PR[0:1, :]
        d = d - jnp.mean(d, axis=-1, keepdims=True) - v * jnp.mean(d * v, axis=-1, keepdims=True)
        grad_in[...] = G[w, mine, :].astype(F32) + scale * d
        write(A.at[w, own], out_hbm.at[w])
        return write(grad_in, grad_in_hbm.at[w])

    first_i(chunk(0), True)
    first_i(chunk(1), True)
    second_i(chunk(0))
    for p in range(2):
        total_q = z_total(of_pair(p)).T.astype(BF)
        for owner in range(4):
            SWQ[owner, :, 384 * p : 384 * p + 384] = total_q[32 * owner : 32 * owner + 32]
    to_seq("swq", SWQ, RWQ)
    second_i(chunk(1))
    first_o(chunk(2))
    grad_a[...] = z_total(of_attn)
    write(grad_a, grad_a_hbm)
    first_rows = final_rows(0)
    tail_x()
    final_i()
    to_seq("swi", SWI, RWI)
    first_rows.wait()
    final_rows(1)
    from_seq("swq", RWQ)
    got = [RWQ[r].astype(F32) for r in range(4)]
    place_of = {}
    for r in range(4):
        for j in range(4):
            for kind in range(3):
                place_of[3 * head_of(r, j) + kind] = (got[r], 384 * (j // 2) + 128 * kind + 64 * (j % 2))
    for at in range(24):
        grad_q[:, 128 * at : 128 * at + 128] = halves(place_of[2 * at], place_of[2 * at + 1])
    write(grad_q, grad_q_hbm)
    link.copy("tx", 0, 1, XT, XT, core).wait_recv()
    total_t = ZT[0, xx].astype(F32) + XT[...].astype(F32)
    turned_t = jnp.concatenate([total_t, jnp.zeros((112, 128), F32)], axis=0).T.astype(BF)
    for owner in range(4):
        SWT[owner] = turned_t[32 * owner : 32 * owner + 32]
    to_seq("swt", SWT, RWT)
    first_o(chunk(3))
    final_o()
    write(dqT, grad_o_hbm)
    from_seq("swi", RWI)
    for r in range(4):
        for blk in range(8):
            at = 512 * blk + 128 * r
            oT[32 * (at // 1024) : 32 * (at // 1024) + 32, at % 1024 : at % 1024 + 128] = RWI[
                r, :, 128 * blk : 128 * blk + 128
            ].astype(F32)
    for q in range(4):
        write(oT.at[32 * q : 32 * q + 32], grad_i_hbm.at[:, 1024 * q : 1024 * q + 1024])

    from_seq("swt", RWT)
    mine = RWT[0].astype(F32)
    summed = mine + RWT[1].astype(F32) + RWT[2].astype(F32) + RWT[3].astype(F32)
    summed = jnp.where(lane == 2, mine, summed)
    summed = jnp.concatenate([summed, jnp.zeros((96, 128), F32)], axis=0).T
    grad_small[...] = jnp.where(lax.broadcasted_iota(jnp.int32, (8, 128), 0) < 3, summed[0:8], total_t[0:8])
    write(grad_small, grad_small_hbm)

    for make in pending:
        make().wait_send()
    seq_left("swi", lambda owner: SWI.at[owner], lambda: RWI.at[s])
    seq_left("swq", lambda owner: SWQ.at[owner], lambda: RWQ.at[s])
    seq_left("swt", lambda owner: SWT.at[owner], lambda: RWT.at[s])
    for u in range(2):
        gather_left("wo", u)
    for w in range(2):
        rows_left("g", G, w)
    for q in range(4):
        link.copy("ox", q, 4, GO.at[q, ox], XO.at[q], xpart).wait_send()
        link.copy("ix", q, 4, GI.at[q, ox], XI.at[q], xpart).wait_send()
    z_left()
    for w in range(2):
        for t in range(2):
            for yy in range(2):
                src = shares[t].at[w, rows(SL * (2 * yy + oc), SL)]
                dst = X.at[w, rows(SL * (2 * t + yy), SL)]
                link.copy("sc", 4 * w + 2 * t + yy, 8, src, dst, core).wait_send()
            src = shares[t].at[w, rows(SL * (2 * oy + c), SL)]
            link.copy("sy", 2 * w + t, 4, src, YR.at[w, t], ypart).wait_send()
    for p in range(2):
        link.copy("qx", p, 2, GQ.at[p, ox], XQ.at[p], xpart).wait_send()
        ga_c(p).wait_send()
        ga_x(p).wait_send()
    for cp in written:
        if cp is not first_rows:
            cp.wait()


def publish(*refs):
    sources, targets, (in_sems, out_sems) = refs[:7], refs[7:17], refs[28:]
    held, row_held = refs[17:24], refs[24:28]
    arrive = [pltpu.make_async_copy(sources[i], held[i], in_sems.at[i]) for i in range(7)]
    leave = [pltpu.make_async_copy(held[i], targets[i], out_sems.at[i]) for i in range(6)]
    leave += [
        pltpu.make_async_copy(row_held[i], targets[6 + i], out_sems.at[6 + i]) for i in range(4)
    ]
    largest_first = (1, 0, 4, 5, 2, 3)
    for i in (6,) + largest_first:
        arrive[i].start()
    arrive[6].wait()
    for i in range(4):
        row_held[i][...] = held[6][i : i + 1, 0 : row_held[i].shape[1]]
        leave[6 + i].start()
    for i in largest_first:
        arrive[i].wait()
        leave[i].start()
    for cp in leave:
        cp.wait()


def turn_tables(seq_len):
    inverse = 10000.0 ** (-2.0 * np.arange(ROTARY // 2) / ROTARY)
    angles = np.arange(seq_len)[:, None] * inverse[None, :]
    cosine = np.ones((seq_len, HD), np.float32)
    sine = np.zeros((seq_len, HD), np.float32)
    cosine[:, 0:ROTARY:2] = cosine[:, 1:ROTARY:2] = np.cos(angles)
    sine[:, 0:ROTARY:2] = -np.sin(angles)
    sine[:, 1:ROTARY:2] = np.sin(angles)
    return np.concatenate([cosine, sine], axis=1)


def fused_shards(inputs, ends, ln_gain, ln_bias, w_qkv, w_attn, w_in, b_in, w_out, b_out, cotangent):
    in_vmem = pl.BlockSpec(memory_space=pltpu.VMEM)
    in_any = pl.BlockSpec(memory_space=pl.ANY)
    rows_type = (2, 1024, 1024)
    shapes = (
        jax.ShapeDtypeStruct((2, 256, 1024), BF),
        jax.ShapeDtypeStruct((2, 256, 1024), F32),
        jax.ShapeDtypeStruct((32, 3072), F32),
        jax.ShapeDtypeStruct((32, 1024), F32),
        jax.ShapeDtypeStruct((32, 4096), F32),
        jax.ShapeDtypeStruct((128, 1024), F32),
    )
    results = pl.pallas_call(
        fused_layer,
        out_shape=shapes + (jax.ShapeDtypeStruct((8, 128), F32),),
        in_specs=[pl.BlockSpec(memory_space=pltpu.SMEM)] + [in_vmem] * 9 + [in_any] * 2,
        out_specs=(in_any,) * 7,
        scratch_shapes=[
            pltpu.VMEM(rows_type, BF),
            pltpu.VMEM(rows_type, BF),
            pltpu.VMEM(rows_type, BF),
            pltpu.VMEM(rows_type, BF),
            pltpu.VMEM(rows_type, BF),
            pltpu.VMEM((1024, 1024), BF),
            pltpu.VMEM((1024, 1024), BF),
            pltpu.VMEM((1024, 768), BF),
            pltpu.VMEM((4, 2, 32, 1024), BF),
            pltpu.VMEM((4, 2, 32, 1024), BF),
            pltpu.VMEM((4, 32, 1024), BF),
            pltpu.VMEM((4, 32, 768), BF),
            pltpu.VMEM((4, 16, 128), BF),
            pltpu.VMEM((8, 16, 128), BF),
            pltpu.VMEM((8, 1024), F32),
            pltpu.VMEM((2, 1024, 768), BF),
            pltpu.VMEM((2, 1024, 256), BF),
            pltpu.VMEM((2, 1024, 256), BF),
            pltpu.VMEM((4, 2, 128, 1024), BF),
            pltpu.VMEM((4, 128, 1024), BF),
            pltpu.VMEM((2, 128, 1024), BF),
            pltpu.VMEM((2, 128, 1024), BF),
            pltpu.VMEM((4, 2, 4, 256, 128), BF),
            pltpu.VMEM((4, 4, 256, 128), BF),
            pltpu.VMEM((4, 256, 128), BF),
            pltpu.VMEM((2, 256, 128), BF),
            pltpu.VMEM((2, 2, 256, 128), BF),
            pltpu.VMEM((2, 2, 256, 128), BF),
            pltpu.VMEM((2, 2, 4, 384, 128), BF),
            pltpu.VMEM((2, 4, 384, 128), BF),
            pltpu.VMEM((2, 2, 384, 128), BF),
            pltpu.VMEM((2, 2, 384, 128), BF),
            pltpu.VMEM((2, 4, 32, 1024), BF),
            pltpu.VMEM((4, 32, 1024), BF),
            pltpu.VMEM((2, 32, 1024), BF),
            pltpu.VMEM((2, 32, 1024), BF),
            pltpu.VMEM((2, 4, 16, 128), BF),
            pltpu.VMEM((16, 128), BF),
            pltpu.VMEM((3, 2, 16, 128), BF),
            pltpu.VMEM((2, 2, 256, 1024), BF),
            pltpu.VMEM((4, 32, 1024), BF),
            pltpu.VMEM((4, 32, 1024), BF),
            pltpu.VMEM((4, 32, 768), BF),
            pltpu.VMEM((4, 32, 768), BF),
            pltpu.VMEM((4, 32, 128), BF),
            pltpu.VMEM((4, 32, 128), BF),
            pltpu.VMEM((16, 1024), F32),
            pltpu.VMEM((2, 1024, 128), BF),
            pltpu.VMEM((128, 1024), BF),
            pltpu.VMEM((128, 1024), BF),
            pltpu.VMEM((128, 1024), BF),
            pltpu.VMEM((128, 1024), F32),
            pltpu.VMEM((128, 1024), F32),
            pltpu.VMEM((1024, 128), F32),
            pltpu.VMEM((1024, 128), F32),
            pltpu.VMEM((256, 1024), F32),
            pltpu.VMEM((32, 3072), F32),
            pltpu.VMEM((32, 1024), F32),
            pltpu.VMEM((8, 128), F32),
            pltpu.SemaphoreType.DMA((113,)),
            pltpu.SemaphoreType.DMA((192,)),
            pltpu.SemaphoreType.DMA((6,)),
            pltpu.SemaphoreType.DMA((14,)),
        ],
        compiler_params=pltpu.CompilerParams(
            collective_id=0, has_side_effects=True, vmem_limit_bytes=65400 * 2**10
        ),
        cost_estimate=pl.CostEstimate(flops=46 * 10**9, bytes_accessed=10**7, transcendentals=10**7),
    )(
        ends,
        ln_gain.reshape(1, 32),
        ln_bias.reshape(1, 32),
        b_out.reshape(1, 32),
        b_in.reshape(1, 128),
        w_qkv, w_attn, w_in, w_out, turn_tables(1024), inputs, cotangent)
    row = jax.ShapeDtypeStruct((1, 32), F32)
    rows_out = (row, row, row, jax.ShapeDtypeStruct((1, 128), F32))
    held = shapes + (jax.ShapeDtypeStruct((8, 128), F32),) + rows_out
    final = pl.pallas_call(
        publish,
        out_shape=shapes + rows_out,
        in_specs=[in_any] * 7,
        out_specs=(in_any,) * 10,
        scratch_shapes=[pltpu.VMEM(v.shape, v.dtype) for v in held]
        + [pltpu.SemaphoreType.DMA((7,)), pltpu.SemaphoreType.DMA((10,))],
        compiler_params=pltpu.CompilerParams(vmem_limit_bytes=60 * 2**20),
    )(*results)
    out, grad_in, grad_q, grad_a, grad_i, grad_o, bias, gain, bias_out, bias_in = final
    return (
        out,
        grad_in,
        gain.reshape(32),
        bias.reshape(32),
        grad_q,
        grad_a,
        grad_i,
        bias_in.reshape(128),
        grad_o,
        bias_out.reshape(32),
    )


def fits_fused(mesh):
    return mesh.shape["batch"] == 8 and mesh.shape["seq"] == 4


def solution(mesh):
    return jax.shard_map(
        fused_shards if fits_fused(mesh) else shards,
        mesh=mesh,
        in_specs=(
            P("batch", "seq", None),
            P("batch"),
            P(("batch", "seq")),
            P(("batch", "seq")),
            P(("batch", "seq"), None),
            P(("batch", "seq"), None),
            P(("batch", "seq"), None),
            P(("batch", "seq")),
            P(("batch", "seq"), None),
            P(("batch", "seq")),
            P("batch", "seq", None),
        ),
        out_specs=(
            P("batch", "seq", None),
            P("batch", "seq", None),
            P(("batch", "seq")),
            P(("batch", "seq")),
            P(("batch", "seq"), None),
            P(("batch", "seq"), None),
            P(("batch", "seq"), None),
            P(("batch", "seq")),
            P(("batch", "seq"), None),
            P(("batch", "seq")),
        ),
        check_vma=False,
    )
```
